128 devices in a mesh: dp: 16 (over y, z_hi, core), tensor: 8 (over z_lo, x).
Axes of the slice: x: 4, y: 4, z: 4 (z_hi: 2, z_lo: 2; z = z_hi * 2 + z_lo), core: 2. Of those that a mesh axis runs over, the one named last changes fastest.
Arguments:
- tokens: bfloat16 [16384, 2048], P(('dp', 'tensor')), may hold values from -6 to 6
- expert_index: int32 [16384, 6], P(('dp', 'tensor')), may hold values from 0 to 7, all different within a row; in each aligned block of 128 rows (0 to 127, 128 to 255, ...) at most 128 rows name the same one
- cotangent: bfloat16 [16384, 2048], P(('dp', 'tensor')), may hold values from -6 to 6
- input_gain: float32 [2048], replicated, may hold values from 0.5 to 1.5
- query_weight: bfloat16 [2048, 3072], P(None, 'tensor'), may hold values from -0.125 to 0.125
- latent_down: bfloat16 [2048, 576], replicated, may hold values from -0.125 to 0.125
- latent_gain: float32 [512], replicated, may hold values from 0.5 to 1.5
- latent_up: bfloat16 [512, 4096], P(None, 'tensor'), may hold values from -0.25 to 0.25
- output_weight: bfloat16 [2048, 2048], P(None, 'tensor'), may hold values from -1.5 to 1.5
- mixer_gain: float32 [2048], replicated, may hold values from 0.5 to 1.5
- router_weight: bfloat16 [2048, 8], replicated, may hold values from -0.0625 to 0.0625
- shared_gate: bfloat16 [2048, 2816], P(None, 'tensor'), may hold values from -0.125 to 0.125
- shared_up: bfloat16 [2048, 2816], P(None, 'tensor'), may hold values from -0.125 to 0.125
- shared_down: bfloat16 [2048, 2816], P(None, 'tensor'), may hold values from -0.21875 to 0.21875
- expert_gate: bfloat16 [2048, 8, 1408], P(None, 'tensor'), may hold values from -0.125 to 0.125
- expert_up: bfloat16 [2048, 8, 1408], P(None, 'tensor'), may hold values from -0.125 to 0.125
- expert_down: bfloat16 [2048, 8, 1408], P(None, 'tensor'), may hold values from -0.625 to 0.625
Outputs:
- layer_out: bfloat16 [16384, 2048], P(('dp', 'tensor'))
- grad_tokens: float32 [16384, 2048], P(('dp', 'tensor'))
- grad_input_gain: float32 [2048], P(('dp', 'tensor'))
- grad_query_weight: float32 [2048, 3072], P('dp', 'tensor')
- grad_latent_down: float32 [2048, 576], P(('dp', 'tensor'))
- grad_latent_gain: float32 [512], P(('dp', 'tensor'))
- grad_latent_up: float32 [512, 4096], P('dp', 'tensor')
- grad_output_weight: float32 [2048, 2048], P('dp', 'tensor')
- grad_mixer_gain: float32 [2048], P(('dp', 'tensor'))
- grad_router_weight: float32 [2048, 8], P(('dp', 'tensor'))
- grad_shared_gate: float32 [2048, 2816], P('dp', 'tensor')
- grad_shared_up: float32 [2048, 2816], P('dp', 'tensor')
- grad_shared_down: float32 [2048, 2816], P('dp', 'tensor')
- grad_expert_gate: float32 [2048, 8, 1408], P('dp', 'tensor')
- grad_expert_up: float32 [2048, 8, 1408], P('dp', 'tensor')
- grad_expert_down: float32 [2048, 8, 1408], P('dp', 'tensor')
The draws below stay inside these ranges and needn't reach their ends.
Inputs may be any that keep to these rules, and one draw needn't show every extreme that they name: `expert_index`: each row names 6 different experts. In each aligned block of 128 rows (the rows of one device) no expert is named by more than 128 rows, a bound that some block reaches.
All inputs are finite; a program needn't handle non-finite values.
Results may differ from the reference program's by a relative error of at most 0.03.
Values may be sent and summed in bfloat16 or wider, within the bound.
No kernel may reach another device: no remote copies, remote signals or barrier semaphores. Data moves between devices by JAX's collectives and lax.ppermute only.
A program may use at most 256 MiB of HBM per device.

```python
import math
import jax
import jax.numpy as jnp
import numpy as np
from jax import lax

D = 2048
HEADS = 16
NOPE = 128
ROPE = 64
VDIM = 128
KVR = 512
EFF = 1408
SFF = 2816
EXPERTS = 8
TOP = 6
LEN = 1024
TOK_DEV = 128
TOKENS = 16384
CAP = 128


def block_levels(rng, extent, shards, least, top_value):
    factor_of, own = 1.0, jax.random.fold_in(rng, 6)
    for axis_at, parts in shards:
        draws = jnp.exp(jax.random.uniform(jax.random.fold_in(own, axis_at), (parts,), jnp.float32, least / len(shards), top_value / len(shards)))
        factor_of = factor_of * jnp.repeat(draws, extent[axis_at] // parts).reshape([-1 if axis == axis_at else 1 for axis in range(len(extent))])
    return factor_of


def deal_out(key, own, number, rows, count, top, bound, slope):
    sequence = jax.random.permutation(key, count)
    heavy_load, common = load_shares(count, rows * top, bound, slope, True), load_shares(count, rows * top, bound, slope, False)
    places = jnp.arange(count)

    def named(lengths, turn):
        used = int((lengths > 0).sum())
        fixed = max(1, used // 4)
        moved = fixed + (places - fixed + turn * (used - fixed)) % max(1, count - fixed)
        return jnp.zeros((count,), jnp.int32).at[sequence[jnp.where(places < fixed, places, moved)]].set(jnp.asarray(lengths, jnp.int32))

    lengths = jnp.where(number % 4 == 0, named(heavy_load, number // 4), named(common, number - number // 4 - 1))
    mixed = jax.random.permutation(jax.random.fold_in(own, 3), count)
    giver, receiver = mixed[0:count // 2 * 2:2], mixed[1:count // 2 * 2:2]
    margin = jnp.minimum(lengths[giver] - 1, bound - lengths[receiver]) // 2
    margin = jnp.where((giver == sequence[0]) | (receiver == sequence[0]) | (lengths[receiver] == 0), 0, jnp.maximum(margin, 0))
    moved = jax.random.randint(jax.random.fold_in(own, 4), (count // 2,), 0, 1 << 20) % (margin + 1)
    lengths = lengths.at[giver].add(-moved).at[receiver].add(moved)
    members = jnp.searchsorted(jnp.cumsum(lengths), jnp.arange(rows * top), side="right").astype(jnp.int32)
    table = members.reshape(top, rows).T
    table = table[jax.random.permutation(jax.random.fold_in(own, 1), rows)]
    turn = jax.random.randint(jax.random.fold_in(own, 2), (rows, 1), 0, top)
    return jnp.take_along_axis(table, (jnp.arange(top)[None, :] + turn) % top, axis=1)


def load_shares(count, total, most, slope, full):
    loads = [(1 << 20) // math.isqrt(grade ** slope) + 1 for grade in range(1, count + 1)]
    largest = most if full else min(most, max(-(-total // count), total * loads[0] // sum(loads)))
    least = 1 if total - largest >= count - 1 else 0
    holding, surplus = [largest] + [least] * (count - 1), total - largest - least * (count - 1)
    while surplus > 0:
        free = [i for i in range(1, count) if holding[i] < largest] or [i for i in range(1, count) if holding[i] < most]
        pool, left = sum([loads[i] for i in free]), surplus
        for i in free:
            addition = min(most - holding[i], max(1, left * loads[i] // pool), surplus)
            holding[i] = holding[i] + addition
            surplus = surplus - addition
    return np.array(holding)


def noise(rng, extent, width, reach, pieces=(), kind=jnp.bfloat16):
    array = width * jax.random.normal(rng, extent, jnp.float32)
    if pieces:
        array = array * block_levels(rng, extent, pieces, -0.22, 0.18)
    return jnp.clip(array, -reach, reach).astype(kind)


def setup_inputs(seed: int = 0) -> dict:
    arg_keys = jax.random.split(jax.random.key(seed), 18)
    tokens = noise(arg_keys[0], (TOKENS, D), 1.0, 6.0, ((0, 128),))
    expert_index_keys = jax.random.split(jax.random.fold_in(arg_keys[1], 1), TOKENS // TOK_DEV)
    expert_index_turns = jax.random.permutation(jax.random.fold_in(arg_keys[1], 3), TOKENS // TOK_DEV)
    expert_index = jax.vmap(lambda own, number: deal_out(jax.random.fold_in(arg_keys[1], 2), own, number, TOK_DEV, EXPERTS, TOP, CAP, 2))(expert_index_keys, expert_index_turns).reshape((TOKENS, TOP))
    cotangent = noise(arg_keys[2], (TOKENS, D), 1.0, 6.0, ((0, 128),))
    input_gain = jnp.clip(1.0 + 0.1 * jax.random.normal(arg_keys[3], (D,), jnp.float32), 0.5, 1.5)
    query_weight = noise(arg_keys[4], (D, HEADS * (NOPE + ROPE)), D ** -0.5, 0.125, ((1, 8),))
    latent_down = noise(arg_keys[5], (D, KVR + ROPE), D ** -0.5, 0.125)
    latent_gain = jnp.clip(1.0 + 0.1 * jax.random.normal(arg_keys[6], (KVR,), jnp.float32), 0.5, 1.5)
    latent_up = noise(arg_keys[7], (KVR, HEADS * (NOPE + VDIM)), KVR ** -0.5, 0.25, ((1, 8),))
    output_weight = noise(arg_keys[8], (D, HEADS * VDIM), (HEADS * VDIM // 128) ** -0.5, 1.5, ((1, 8),))
    mixer_gain = jnp.clip(1.0 + 0.1 * jax.random.normal(arg_keys[9], (D,), jnp.float32), 0.5, 1.5)
    router_weight = noise(arg_keys[10], (D, EXPERTS), (4 * D) ** -0.5, 0.0625)
    shared_gate = noise(arg_keys[11], (D, SFF), D ** -0.5, 0.125, ((1, 8),))
    shared_up = noise(arg_keys[12], (D, SFF), D ** -0.5, 0.125, ((1, 8),))
    shared_down = noise(arg_keys[13], (D, SFF), (SFF // 4) ** -0.5, 0.21875, ((1, 8),))
    expert_gate = noise(arg_keys[14], (D, EXPERTS, EFF), D ** -0.5, 0.125, ((1, 8),))
    expert_up = noise(arg_keys[15], (D, EXPERTS, EFF), D ** -0.5, 0.125, ((1, 8),))
    expert_down = noise(arg_keys[16], (D, EXPERTS, EFF), (EFF // 16) ** -0.5, 0.625, ((1, 8),))
    return dict(tokens=tokens, expert_index=expert_index, cotangent=cotangent, input_gain=input_gain, query_weight=query_weight, latent_down=latent_down, latent_gain=latent_gain, latent_up=latent_up, output_weight=output_weight, mixer_gain=mixer_gain, router_weight=router_weight, shared_gate=shared_gate, shared_up=shared_up, shared_down=shared_down, expert_gate=expert_gate, expert_up=expert_up, expert_down=expert_down)


EPSILON = 1e-06
HIGHEST_PRECISION = lax.Precision.HIGHEST

@jax.custom_vjp
def low(v):
    return lax.optimization_barrier(v.astype(jnp.bfloat16)).astype(jnp.float32)

@jax.custom_vjp
def low_back(v):
    return v

def low_keep(v):
    return (low(v), None)

def low_pass(kept, grad):
    return (grad,)

def back_keep(v):
    return (v, None)

def back_low(kept, grad):
    return (low(grad),)
low.defvjp(low_keep, low_pass)
low_back.defvjp(back_keep, back_low)

def rope_tables(places):
    halfwidth = ROPE // 2
    frequency = jnp.exp(-jnp.log(10000.0) * (2.0 * jnp.arange(halfwidth, dtype=jnp.float32) / ROPE))
    angles = places.astype(jnp.float32)[:, None] * frequency[None, :]
    return (jnp.cos(angles), jnp.sin(angles))

def rotate(values, cosine, sine):
    halfwidth = values.shape[-1] // 2
    first = values[..., :halfwidth]
    second = values[..., halfwidth:]
    return jnp.concatenate([first * cosine - second * sine, second * cosine + first * sine], -1)

def normalize(values, gain):
    return values * lax.rsqrt(lax.optimization_barrier(jnp.mean(values * values, -1, keepdims=True)) + EPSILON) * gain

def product(left, right):
    return jnp.dot(left, right, precision=HIGHEST_PRECISION)

def product_transposed(left, right):
    return lax.dot_general(left, right, (((1,), (1,)), ((), ())), precision=HIGHEST_PRECISION)

def attend_sequence(bundle):
    queries, key_rows, value_rows = bundle
    scores = low_back(jnp.einsum('qhd,khd->hqk', queries, key_rows, precision=HIGHEST_PRECISION) * (NOPE + ROPE) ** (-0.5))
    allowed = jnp.arange(LEN)[None, :] <= jnp.arange(LEN)[:, None]
    masked = jnp.where(allowed[None], scores, -1e+30)
    highest = lax.optimization_barrier(jnp.max(masked, -1, keepdims=True))
    weights = jnp.exp(masked - highest)
    shares = weights / lax.optimization_barrier(jnp.sum(weights, -1, keepdims=True))
    blended = jnp.einsum('hqk,khd->qhd', low(shares), value_rows, precision=HIGHEST_PRECISION)
    return low_back(low(blended))

def run_expert(bundle):
    rows_in, gate_matrix, up_matrix, down_matrix = bundle
    gated = low_back(product(rows_in, gate_matrix))
    lifted = low_back(product(rows_in, up_matrix))
    hidden = low(jax.nn.silu(gated) * lifted)
    return low_back(low(product_transposed(hidden, down_matrix)))

def routing_tables(expert_index):
    blocks = TOKENS // TOK_DEV
    chosen = expert_index.reshape(blocks, TOK_DEV * TOP)
    onehot = (chosen[..., None] == jnp.arange(EXPERTS, dtype=jnp.int32)).astype(jnp.int32)
    before = jnp.cumsum(onehot, 1) - onehot
    places = lax.optimization_barrier(jnp.sum(before * onehot, -1))
    slot_ids = (chosen * CAP + places).astype(jnp.int32)
    matches = slot_ids[:, None, :] == jnp.arange(EXPERTS * CAP, dtype=jnp.int32)[None, :, None]
    source = lax.optimization_barrier(jnp.sum(jnp.where(matches, jnp.arange(TOK_DEV * TOP, dtype=jnp.int32)[None, None, :], 0), -1)).astype(jnp.int32)
    filled = jnp.any(matches, -1)
    return (slot_ids, source, filled)

def pick_rows(block_rows, index_rows):
    return block_rows[index_rows]

def layer(inputs, weight_set, expert_index, slot_ids, source, filled):
    input_gain, query_weight, latent_down, latent_gain, latent_up, output_weight, mixer_gain, router_weight, shared_gate, shared_up, shared_down, expert_gate, expert_up, expert_down = weight_set
    blocks = TOKENS // TOK_DEV
    sequences = TOKENS // LEN
    cosine, sine = rope_tables(jnp.arange(TOKENS, dtype=jnp.int32) % LEN)
    normed = low(normalize(inputs, input_gain))
    latent = low_back(product(normed, latent_down))
    compressed = low(normalize(latent[:, :KVR], latent_gain))
    key_rope = low(rotate(latent[:, KVR:], cosine, sine))
    query_raw = low_back(product(normed, query_weight)).reshape(TOKENS, HEADS, NOPE + ROPE)
    queries = low(jnp.concatenate([query_raw[..., :NOPE], rotate(query_raw[..., NOPE:], cosine[:, None], sine[:, None])], -1))
    key_value = low_back(low(product(compressed, latent_up))).reshape(TOKENS, HEADS, NOPE + VDIM)
    key_rows = jnp.concatenate([key_value[..., :NOPE], jnp.broadcast_to(key_rope[:, None, :], (TOKENS, HEADS, ROPE))], -1)
    value_rows = key_value[..., NOPE:]
    attended = lax.map(jax.checkpoint(attend_sequence), (queries.reshape(sequences, LEN, HEADS, NOPE + ROPE), key_rows.reshape(sequences, LEN, HEADS, NOPE + ROPE), value_rows.reshape(sequences, LEN, HEADS, VDIM)))
    branch = low_back(product_transposed(attended.reshape(TOKENS, HEADS * VDIM), output_weight))
    middle = inputs + branch
    hidden_in = low(normalize(middle, mixer_gain))
    logits = low_back(product(hidden_in, router_weight))
    gate_values = jnp.take_along_axis(jax.nn.softmax(logits, -1), expert_index, 1)
    shared_hidden = low(jax.nn.silu(low_back(product(hidden_in, shared_gate))) * low_back(product(hidden_in, shared_up)))
    shared_out = low_back(product_transposed(shared_hidden, shared_down))
    by_block = hidden_in.reshape(blocks, TOK_DEV, D)
    picked = jax.vmap(pick_rows)(by_block, source // TOP)
    picked = low_back(picked * filled[..., None])
    grouped = picked.reshape(blocks, EXPERTS, CAP, D).transpose(1, 0, 2, 3).reshape(EXPERTS, blocks * CAP, D)
    produced = lax.map(run_expert, (grouped, jnp.moveaxis(expert_gate, 1, 0), jnp.moveaxis(expert_up, 1, 0), jnp.moveaxis(expert_down, 1, 0)))
    produced = produced.reshape(EXPERTS, blocks, CAP, D).transpose(1, 0, 2, 3).reshape(blocks, EXPERTS * CAP, D)
    returned = jax.vmap(pick_rows)(produced, slot_ids).reshape(TOKENS, TOP, D)
    routed = lax.optimization_barrier(jnp.sum(gate_values[..., None] * returned, 1))
    return middle + shared_out + routed

def reference(tokens, expert_index, cotangent, input_gain, query_weight, latent_down, latent_gain, latent_up, output_weight, mixer_gain, router_weight, shared_gate, shared_up, shared_down, expert_gate, expert_up, expert_down):
    slot_ids, source, filled = routing_tables(expert_index)
    filled_float = filled.astype(jnp.float32)
    weight_set = tuple((tensor_in.astype(jnp.float32) for tensor_in in (input_gain, query_weight, latent_down, latent_gain, latent_up, output_weight, mixer_gain, router_weight, shared_gate, shared_up, shared_down, expert_gate, expert_up, expert_down)))

    def forward_pass(inputs, weights_in):
        return layer(inputs, weights_in, expert_index, slot_ids, source, filled_float)
    result, pullback = jax.vjp(forward_pass, tokens.astype(jnp.float32), weight_set)
    grad_tokens, weight_grads = pullback(cotangent.astype(jnp.float32))
    return (result.astype(jnp.bfloat16), grad_tokens, weight_grads[0], weight_grads[1], weight_grads[2], weight_grads[3], weight_grads[4], weight_grads[5], weight_grads[6], weight_grads[7], weight_grads[8], weight_grads[9], weight_grads[10], weight_grads[11], weight_grads[12], weight_grads[13])
```

```python
import jax
import jax.numpy as jnp
from jax import lax
from jax.sharding import PartitionSpec as P

NOPE = 128
ROPE = 64
VDIM = 128
EPSILON = 1e-06

ORDER = ((0, 0), (0, -1), (0, 1), (1, 0), (0, 2), (1, 1), (1, -1), (1, 2))
SLOT = {rel: slot for slot, rel in enumerate(ORDER)}

LEFT = [(z * 4 + x, z * 4 + (x - 1) % 4) for z in range(2) for x in range(4)]
RIGHT = [(z * 4 + x, z * 4 + (x + 1) % 4) for z in range(2) for x in range(4)]
ACROSS = [(z * 4 + x, (1 - z) * 4 + x) for z in range(2) for x in range(4)]


def dp_pairs(move):
    pairs = []
    for y in range(4):
        for h in range(2):
            for c in range(2):
                y2, h2, c2 = move(y, h, c)
                pairs.append((y * 4 + h * 2 + c, (y2 % 4) * 4 + h2 * 2 + c2))
    return pairs


CORE = dp_pairs(lambda y, h, c: (y, h, 1 - c))
HIGH = dp_pairs(lambda y, h, c: (y, 1 - h, c))
UP = dp_pairs(lambda y, h, c: (y + 1, h, c))
DOWN = dp_pairs(lambda y, h, c: (y - 1, h, c))


def left(v):
    return lax.ppermute(v, "tensor", LEFT)


def right(v):
    return lax.ppermute(v, "tensor", RIGHT)


def across(v):
    return lax.ppermute(v, "tensor", ACROSS)


def cuts(rows):
    third = rows // 48 * 16
    return (third, 2 * third) if third else (0, 0)


def gather_blocks(own):
    one, two = cuts(own.shape[0])
    got = {(0, 0): own}
    got[0, 1] = left(own)
    got[0, -1] = right(own)
    got[1, 0] = across(own)
    got[0, 2] = right(got[0, -1])
    got[1, 1] = left(got[1, 0])
    got[1, -1] = across(got[0, -1])
    pieces = [across(got[0, 2][two:])]
    if one:
        pieces = [right(got[1, -1][:one]), left(got[1, 1][one:two])] + pieces
    got[1, 2] = jnp.concatenate(pieces, 0)
    return [got[rel] for rel in ORDER]


def add_rows(block, rows, start):
    stop = start + rows.shape[0]
    middle = plus(block[start:stop], rows)
    return jnp.concatenate([part for part in (block[:start], middle, block[stop:]) if part.shape[0]], 0)


def plus(*terms):
    total = terms[0].astype(jnp.float32)
    for term in terms[1:]:
        total = total + term.astype(jnp.float32)
    return total.astype(terms[0].dtype)


def scatter_sum(blocks):
    part = {rel: blocks[slot] for slot, rel in enumerate(ORDER)}
    far = part[1, 2]
    one, two = cuts(far.shape[0])
    third = across(far[two:])
    if one:
        first = left(far[:one])
        second = right(far[one:two])
        to_across = add_rows(part[1, -1], first, 0)
        to_right = add_rows(part[1, 1], second, one)
    else:
        to_across, to_right = part[1, -1], part[1, 1]
    from_right = left(add_rows(part[0, 2], third, two))
    from_across = across(to_across)
    from_left = right(to_right)
    last_right = left(plus(part[0, -1], from_right, from_across))
    last_across = across(plus(part[1, 0], from_left))
    last_left = right(part[0, 1])
    total = part[0, 0].astype(jnp.float32) + last_left.astype(jnp.float32)
    return total + last_across.astype(jnp.float32) + last_right.astype(jnp.float32)


def split_blocks(whole):
    rows = whole.shape[0] // 8
    return [whole[slot * rows : (slot + 1) * rows] for slot in range(8)]


def relative_blocks(whole, z, x):
    by_place = whole.reshape((8, whole.shape[0] // 8) + whole.shape[1:])
    return [
        lax.dynamic_index_in_dim(by_place, (z ^ dz) * 4 + (x + dx) % 4, 0, keepdims=False)
        for dz, dx in ORDER
    ]


def dp_scatter_sum(whole):
    index = lax.axis_index("dp")
    y, h, c = index // 4, (index // 2) % 2, index % 2
    rows = whole.shape[0] // 16
    blocks = whole.reshape((4, 2, 2, rows) + whole.shape[1:])
    other = lax.dynamic_index_in_dim(blocks, 1 - c, 2, keepdims=False)
    mine = lax.dynamic_index_in_dim(blocks, c, 2, keepdims=False)
    mine = plus(mine, lax.ppermute(other, "dp", CORE))

    def row(step):
        return lax.dynamic_index_in_dim(mine, (y + step) % 4, 0, keepdims=False)

    far = row(2)
    to_up, to_down = row(1), row(3)
    to_up = jnp.stack([plus(to_up[0], lax.ppermute(far[0], "dp", UP)), to_up[1]])
    to_down = jnp.stack([to_down[0], plus(to_down[1], lax.ppermute(far[1], "dp", DOWN))])
    column = plus(row(0), lax.ppermute(to_up, "dp", UP), lax.ppermute(to_down, "dp", DOWN))
    keep = lax.dynamic_index_in_dim(column, h, 0, keepdims=False)
    give = lax.dynamic_index_in_dim(column, 1 - h, 0, keepdims=False)
    return plus(keep, lax.ppermute(give, "dp", HIGH))


def rope_tables(places):
    halfwidth = ROPE // 2
    frequency = jnp.exp(-jnp.log(10000.0) * (2.0 * jnp.arange(halfwidth, dtype=jnp.float32) / ROPE))
    angles = places.astype(jnp.float32)[:, None] * frequency[None, :]
    return (jnp.cos(angles), jnp.sin(angles))


def rotate(values, cosine, sine):
    halfwidth = values.shape[-1] // 2
    first = values[..., :halfwidth]
    second = values[..., halfwidth:]
    return jnp.concatenate([first * cosine - second * sine, second * cosine + first * sine], -1)


def rotate_back(grads_in, cosine, sine):
    halfwidth = grads_in.shape[-1] // 2
    first = grads_in[..., :halfwidth]
    second = grads_in[..., halfwidth:]
    return jnp.concatenate([first * cosine + second * sine, second * cosine - first * sine], -1)


def normalize(values, gain):
    factor = lax.rsqrt(jnp.mean(values * values, -1, keepdims=True) + EPSILON)
    scaled = values * factor
    return (scaled * gain, scaled, factor)


def norm_backward(grads_in, scaled, factor, gain):
    weighted = grads_in * gain
    centre = jnp.mean(weighted * scaled, -1, keepdims=True)
    return (factor * (weighted - scaled * centre), jnp.sum(grads_in * scaled, 0))


def contract_rows(first, second):
    return lax.dot_general(
        first, second, (((0,), (0,)), ((), ())), preferred_element_type=jnp.float32
    )


def contract_last(first, second):
    return lax.dot_general(
        first, second, (((1,), (1,)), ((), ())), preferred_element_type=jnp.float32
    )


def matmul(first, second):
    return jnp.dot(first, second, preferred_element_type=jnp.float32)


def widen(array, width):
    return jnp.pad(array, ((0, 0), (0, width - array.shape[1])))


def on_device(
    tokens,
    expert_index,
    cotangent,
    input_gain,
    query_weight,
    latent_down,
    latent_gain,
    latent_up,
    output_weight,
    mixer_gain,
    router_weight,
    shared_gate,
    shared_up,
    shared_down,
    expert_gate,
    expert_up,
    expert_down,
):
    tok_rows, width = tokens.shape
    group = lax.axis_index("tensor")
    z, x = group // 4, group % 4
    seq_len = tok_rows * 8
    rank = latent_up.shape[0]
    heads_local = query_weight.shape[1] // (NOPE + ROPE)
    experts_all = router_weight.shape[1]
    scale = (NOPE + ROPE) ** (-0.5)
    expert_units = expert_gate.shape[2]
    shared_units = shared_gate.shape[1]
    shared_wide = -(-shared_units // 128) * 128
    units = expert_units + shared_wide
    bf16 = jnp.bfloat16

    weight_in = jnp.concatenate(
        [
            expert_gate.reshape(width, expert_units),
            widen(shared_gate, shared_wide),
            expert_up.reshape(width, expert_units),
            widen(shared_up, shared_wide),
        ],
        1,
    )
    weight_out = jnp.concatenate(
        [expert_down.reshape(width, expert_units), widen(shared_down, shared_wide)], 1
    )

    tokens_all = jnp.concatenate(gather_blocks(tokens), 0)
    places = jnp.concatenate(
        [
            ((z ^ dz) * 4 + (x + dx) % 4) * tok_rows + jnp.arange(tok_rows, dtype=jnp.int32)
            for dz, dx in ORDER
        ]
    )
    cosine, sine = rope_tables(places)
    first_normed, first_scaled, first_factor = normalize(
        tokens_all.astype(jnp.float32), input_gain
    )
    normed_all = first_normed.astype(bf16)

    chosen = (expert_index[:, :, None] == jnp.arange(experts_all, dtype=jnp.int32)).any(1)
    extra = jnp.zeros((16, width), bf16).at[:experts_all, :tok_rows].set(chosen.T.astype(bf16))
    sent = jnp.concatenate([cotangent, extra], 0)
    sent, tokens_all = lax.optimization_barrier((sent, tokens_all))
    sent_blocks = gather_blocks(sent)
    cotangent_all = jnp.concatenate([block[:tok_rows] for block in sent_blocks], 0)
    chosen_all = jnp.concatenate(
        [block[tok_rows : tok_rows + experts_all, :tok_rows].T for block in sent_blocks], 0
    ).astype(jnp.float32)

    latent = matmul(normed_all, latent_down)
    latent_normed, latent_scaled, latent_factor = normalize(latent[:, :rank], latent_gain)
    compressed = latent_normed.astype(bf16)
    key_rope = rotate(latent[:, rank:], cosine, sine).astype(bf16)
    query_raw = matmul(normed_all, query_weight).reshape(seq_len, heads_local, NOPE + ROPE)
    head_queries = jnp.concatenate(
        [
            query_raw[..., :NOPE],
            rotate(query_raw[..., NOPE:], cosine[:, None], sine[:, None]),
        ],
        -1,
    ).astype(bf16)
    key_value = (
        matmul(compressed, latent_up).astype(bf16).reshape(seq_len, heads_local, NOPE + VDIM)
    )
    head_keys = jnp.concatenate(
        [
            key_value[..., :NOPE],
            jnp.broadcast_to(key_rope[:, None, :], (seq_len, heads_local, ROPE)),
        ],
        -1,
    )
    head_values = key_value[..., NOPE:]
    allowed = (places[None, :] <= places[:, None])[None]
    scores = (
        jnp.einsum("qhd,khd->hqk", head_queries, head_keys, preferred_element_type=jnp.float32)
        * scale
    )
    masked = jnp.where(allowed, scores, -1e30)
    highest = jnp.max(masked, -1, keepdims=True)
    weights = jnp.exp(masked - highest)
    denominator = jnp.sum(weights, -1, keepdims=True)
    shares_low = (weights / denominator).astype(bf16)
    attended = (
        jnp.einsum("hqk,khd->qhd", shares_low, head_values, preferred_element_type=jnp.float32)
        .astype(bf16)
        .reshape(seq_len, heads_local * VDIM)
    )
    logsums = highest + jnp.log(denominator)
    branch = scatter_sum(split_blocks(contract_last(attended, output_weight).astype(bf16)))

    middle = tokens.astype(jnp.float32) + branch
    second_normed, second_scaled, second_factor = normalize(middle, mixer_gain)
    hidden_in = second_normed.astype(bf16)
    hidden_all = jnp.concatenate(gather_blocks(hidden_in), 0)
    out_back = matmul(cotangent_all, weight_out)
    router_probs = jax.nn.softmax(matmul(hidden_all, router_weight), -1)
    own_expert = (jnp.arange(experts_all) == group).astype(jnp.float32)
    own_chosen = jnp.sum(chosen_all * own_expert, 1, keepdims=True)
    own_prob = jnp.sum(router_probs * own_expert, 1, keepdims=True)
    own_gate = own_prob * own_chosen
    is_expert = jnp.arange(units) < expert_units
    row_scale = jnp.where(is_expert[None, :], own_gate, 1.0)
    pre = matmul(hidden_all, weight_in)
    pre_gate, pre_up = pre[:, :units], pre[:, units:]
    sigmoid = jax.nn.sigmoid(pre_gate)
    act = pre_gate * sigmoid
    slope = sigmoid * (1.0 + pre_gate * (1.0 - sigmoid))
    hidden = act * pre_up
    hidden_scaled = (hidden * row_scale).astype(bf16)
    gate_grads = (
        jnp.sum(hidden[:, :expert_units] * out_back[:, :expert_units], 1, keepdims=True)
        * own_chosen
    )
    hidden_grads = out_back * row_scale
    pre_grads = jnp.concatenate(
        [(hidden_grads * pre_up * slope).astype(bf16), (hidden_grads * act).astype(bf16)], 1
    )
    logit_grads = (gate_grads * router_probs * (own_expert - own_prob)).astype(bf16)
    mixer_part = contract_last(pre_grads, weight_in) + contract_last(logit_grads, router_weight)
    shared_back = scatter_sum(split_blocks(mixer_part.astype(bf16)))
    grad_out = contract_rows(cotangent_all, hidden_scaled).astype(bf16)
    grad_in = contract_rows(hidden_all, pre_grads).astype(bf16)
    grad_router = contract_rows(hidden_all, logit_grads)
    total_out = lax.psum_scatter(grad_out, "dp", scatter_dimension=0, tiled=True)
    total_in = lax.psum_scatter(grad_in, "dp", scatter_dimension=0, tiled=True)
    mixer_out = scatter_sum(split_blocks(contract_last(hidden_scaled, weight_out).astype(bf16)))
    layer_out = (middle + mixer_out).astype(bf16)

    upstream = cotangent.astype(jnp.float32)
    middle_from, grad_mixer_gain = norm_backward(
        shared_back, second_scaled, second_factor, mixer_gain
    )
    middle_grads = upstream + middle_from

    branch_grads = jnp.concatenate(gather_blocks(middle_grads.astype(bf16)), 0)
    attended_grads = (
        matmul(branch_grads, output_weight).astype(bf16).reshape(seq_len, heads_local, VDIM)
    )
    total_output = dp_scatter_sum(contract_rows(branch_grads, attended).astype(bf16))
    scores = (
        jnp.einsum("qhd,khd->hqk", head_queries, head_keys, preferred_element_type=jnp.float32)
        * scale
    )
    shares = jnp.where(allowed, jnp.exp(scores - logsums), 0.0)
    share_grads = jnp.einsum(
        "qhd,khd->hqk", attended_grads, head_values, preferred_element_type=jnp.float32
    )
    centre = jnp.sum(shares * share_grads, -1, keepdims=True)
    score_grads = (shares * (share_grads - centre)).astype(bf16)
    query_grads = (
        jnp.einsum("hqk,khd->qhd", score_grads, head_keys, preferred_element_type=jnp.float32)
        * scale
    )
    key_grads = (
        jnp.einsum("hqk,qhd->khd", score_grads, head_queries, preferred_element_type=jnp.float32)
        * scale
    )
    value_grads = jnp.einsum(
        "hqk,qhd->khd", shares.astype(bf16), attended_grads, preferred_element_type=jnp.float32
    )
    query_pre_grads = (
        jnp.concatenate(
            [
                query_grads[..., :NOPE],
                rotate_back(query_grads[..., NOPE:], cosine[:, None], sine[:, None]),
            ],
            -1,
        )
        .astype(bf16)
        .reshape(seq_len, heads_local * (NOPE + ROPE))
    )
    kv_grads = (
        jnp.concatenate([key_grads[..., :NOPE], value_grads], -1)
        .astype(bf16)
        .reshape(seq_len, heads_local * (NOPE + VDIM))
    )
    compressed_from, grad_latent_gain = norm_backward(
        contract_last(kv_grads, latent_up), latent_scaled, latent_factor, latent_gain
    )
    latent_grads = jnp.concatenate(
        [compressed_from, rotate_back(jnp.sum(key_grads[..., NOPE:], 1), cosine, sine)], 1
    ).astype(bf16)
    normed_part = contract_last(query_pre_grads, query_weight) + contract_last(
        latent_grads, latent_down
    )
    grad_input_gain = jnp.sum(normed_part * first_scaled, 0)
    normed_grads = scatter_sum(split_blocks(normed_part.astype(bf16)))
    input_from, _ = norm_backward(
        normed_grads, first_scaled[:tok_rows], first_factor[:tok_rows], input_gain
    )
    grad_tokens = middle_grads + input_from

    dp_rows = width // 16
    wide = latent_down.shape[1]
    gain_rows = jnp.pad(grad_latent_gain.reshape(16, 8, -1), ((0, 0), (0, 0), (0, dp_rows // 8 - rank // 128)))
    rest = jnp.concatenate(
        [
            contract_rows(normed_all, latent_grads),
            grad_router,
            grad_input_gain[:, None],
            grad_mixer_gain[:, None],
            gain_rows.reshape(width, 1),
        ],
        1,
    ).astype(bf16)
    rest_wide = -(-rest.shape[1] // 128) * 128
    query_wide = query_weight.shape[1]
    up_part = contract_rows(compressed, kv_grads).astype(bf16)
    late = jnp.concatenate(
        [
            widen(rest, rest_wide),
            contract_rows(normed_all, query_pre_grads).astype(bf16),
            up_part.reshape(width, -1),
        ],
        1,
    )
    late = dp_scatter_sum(late)
    rest = scatter_sum(relative_blocks(late[:, :rest_wide], z, x))
    f32 = jnp.float32
    total_query = late[:, rest_wide : rest_wide + query_wide].astype(f32)
    total_up = late[:, rest_wide + query_wide :].reshape(rank // 16, latent_up.shape[1]).astype(f32)
    at = wide + experts_all
    grad_in_gate, grad_in_up = total_in[:, :units].astype(f32), total_in[:, units:].astype(f32)
    total_out = total_out.astype(f32)
    stop = expert_units + shared_units
    return (
        layer_out,
        grad_tokens,
        rest[:, at],
        total_query,
        rest[:, :wide],
        rest[: rank // 128, at + 2],
        total_up,
        total_output.astype(f32),
        rest[:, at + 1],
        rest[:, wide:at],
        grad_in_gate[:, expert_units:stop],
        grad_in_up[:, expert_units:stop],
        total_out[:, expert_units:stop],
        grad_in_gate[:, None, :expert_units],
        grad_in_up[:, None, :expert_units],
        total_out[:, None, :expert_units],
    )


def solution(mesh):
    rows = P(("dp", "tensor"), None)
    columns = P(None, "tensor")
    middle = P(None, "tensor", None)
    return jax.shard_map(
        on_device,
        mesh=mesh,
        in_specs=(rows, rows, rows, P(), columns, P(), P(), columns, columns, P(), P())
        + (columns,) * 3
        + (middle,) * 3,
        out_specs=(
            rows,
            rows,
            P(("dp", "tensor")),
            P("dp", "tensor"),
            rows,
            P(("dp", "tensor")),
            P("dp", "tensor"),
            P("dp", "tensor"),
            P(("dp", "tensor")),
            rows,
        )
        + (P("dp", "tensor"),) * 3
        + (P("dp", "tensor", None),) * 3,
        check_vma=False,
    )
```

```python
import functools

import jax
import jax.numpy as jnp
from jax import lax
from jax.experimental import pallas as pl
from jax.experimental.pallas import tpu as pltpu
from jax.sharding import PartitionSpec as P

NOPE = 128
ROPE = 64
VDIM = 128
EPSILON = 1e-06

ORDER = ((0, 0), (0, -1), (0, 1), (1, 0), (0, 2), (1, 1), (1, -1), (1, 2))
SLOT = {rel: slot for slot, rel in enumerate(ORDER)}

LEFT = [(z * 4 + x, z * 4 + (x - 1) % 4) for z in range(2) for x in range(4)]
RIGHT = [(z * 4 + x, z * 4 + (x + 1) % 4) for z in range(2) for x in range(4)]
OPPOSITE = [(z * 4 + x, z * 4 + (x + 2) % 4) for z in range(2) for x in range(4)]
ACROSS = [(z * 4 + x, (1 - z) * 4 + x) for z in range(2) for x in range(4)]


def dp_pairs(move):
    pairs = []
    for y in range(4):
        for h in range(2):
            for c in range(2):
                y2, h2, c2 = move(y, h, c)
                pairs.append((y * 4 + h * 2 + c, (y2 % 4) * 4 + h2 * 2 + c2))
    return pairs


CORE = dp_pairs(lambda y, h, c: (y, h, 1 - c))
HIGH = dp_pairs(lambda y, h, c: (y, 1 - h, c))
UP = dp_pairs(lambda y, h, c: (y + 1, h, c))
DOWN = dp_pairs(lambda y, h, c: (y - 1, h, c))
FAR = dp_pairs(lambda y, h, c: (y + 2, h, c))
LEVELS = [[y * 4 + h * 2 + c for y in range(4) for c in range(2)] for h in range(2)]
BLOCKS = [y * 4 + h * 2 + c for y in range(4) for c in range(2) for h in range(2)]


def left(v):
    return lax.ppermute(v, "tensor", LEFT)


def right(v):
    return lax.ppermute(v, "tensor", RIGHT)


def across(v):
    return lax.ppermute(v, "tensor", ACROSS)


def opposite(v):
    return lax.ppermute(v, "tensor", OPPOSITE)


def cuts(rows):
    third = (rows // 3 + 8) // 16 * 16
    return third, 2 * third


def pair_gather_first(own):
    return {
        (0, 0): own,
        (0, 2): opposite(own),
        (0, 1): left(own),
        (0, -1): right(own),
        (1, 0): across(own),
    }


def pair_gather_second(got):
    new = {(1, 1): left(got[1, 0]), (1, -1): right(got[1, 0]), (1, 2): across(got[0, 2])}
    return {**got, **new}


def gather_first(own):
    return {(0, 0): own, (0, 1): left(own), (0, -1): right(own), (1, 0): across(own)}


def gather_second(got):
    new = {(0, 2): right(got[0, -1]), (1, 1): left(got[1, 0]), (1, -1): across(got[0, -1])}
    return {**got, **new}


def gather_third(got):
    half = got[0, 0].shape[0] // 2
    return {**got, (1, 2): [right(got[1, -1][:half]), left(got[1, 1][half:])]}


def listed(got, order):
    blocks = []
    for rel in order:
        blocks += got[rel] if rel == (1, 2) else [got[rel]]
    return blocks


def named(blocks, order):
    got = dict(zip(order, blocks))
    if (1, 2) in got:
        got[1, 2] = list(blocks[3:])
    return got


def fence(*values):
    return lax.optimization_barrier(values)


def plus(*terms):
    total = terms[0].astype(jnp.float32)
    for term in terms[1:]:
        total = total + term.astype(jnp.float32)
    return total.astype(terms[0].dtype)


def pair_scatter_first(part):
    return left(part[1, -1]), right(part[1, 1]), across(part[1, 2])


def pair_scatter_second(sums, part):
    from_right, from_left, from_across = sums
    return (
        across(plus(part[1, 0], from_right, from_left)),
        opposite(plus(part[0, 2], from_across)),
        left(part[0, -1]),
        right(part[0, 1]),
    )


def scatter_first(part):
    first, second, third = part[1, 2]
    return left(first), right(second), across(third)


def add_kernel(far, flipped, turned, first, second, third, to_left, to_across, to_right):
    at = 0
    for ref, block, out in ((first, flipped, to_across), (second, turned, to_right), (third, far, to_left)):
        rows = ref.shape[0]
        out[...] = block[...]
        both = block[at : at + rows, :].astype(jnp.float32) + ref[...].astype(jnp.float32)
        out[at : at + rows, :] = both.astype(out.dtype)
        at += rows


def scatter_second(pieces, part):
    block = jax.ShapeDtypeStruct(part[0, 2].shape, part[0, 2].dtype)
    to_left, to_across, to_right = pl.pallas_call(
        add_kernel, out_shape=[block] * 3, name="add_pieces"
    )(part[0, 2], part[1, -1], part[1, 1], *pieces)
    return left(to_left), across(to_across), right(to_right)


def scatter_third(sums, part):
    from_right, from_across, from_left = sums
    return (
        left(plus(part[0, -1], from_right, from_across)),
        across(plus(part[1, 0], from_left)),
    )


def scatter_total(part, ends):
    return sum(
        (end.astype(jnp.float32) for end in jax.tree.leaves(ends)), part[0, 0].astype(jnp.float32)
    )


def dp_order():
    index = lax.axis_index("dp")
    y, h, c = index // 4, (index // 2) % 2, index % 2
    return jnp.stack(
        [
            ((y + step) % 4) * 4 + (h ^ high) * 2 + (c ^ core)
            for core in range(2)
            for step in range(4)
            for high in range(2)
        ]
    ).astype(jnp.int32)


def dp_second(mine):
    return (
        mine[0:2],
        lax.ppermute(mine[2:4], "dp", UP),
        lax.ppermute(mine[6:8], "dp", DOWN),
        lax.ppermute(mine[4:6], "dp", FAR),
    )


def dp_third(terms):
    column = plus(*terms)
    return plus(column[0], lax.ppermute(column[1], "dp", HIGH))


def level_scatter_sum(whole):
    return lax.psum_scatter(
        whole, "dp", scatter_dimension=0, tiled=True, axis_index_groups=LEVELS
    )


def high_sum(pair):
    high = (lax.axis_index("dp") // 2) % 2
    give = lax.dynamic_index_in_dim(pair, 1 - high, 0, keepdims=False)
    keep = lax.dynamic_index_in_dim(pair, high, 0, keepdims=False)
    return plus(keep, lax.ppermute(give, "dp", HIGH))


def rope_tables(places):
    halfwidth = ROPE // 2
    frequency = jnp.exp(-jnp.log(10000.0) * (2.0 * jnp.arange(halfwidth, dtype=jnp.float32) / ROPE))
    angles = places.astype(jnp.float32)[:, None] * frequency[None, :]
    return (jnp.cos(angles), jnp.sin(angles))


def normalize(values, gain):
    factor = lax.rsqrt(jnp.mean(values * values, -1, keepdims=True) + EPSILON)
    scaled = values * factor
    return (scaled * gain, scaled, factor)


def norm_backward(grads_in, scaled, factor, gain):
    weighted = grads_in * gain
    centre = jnp.mean(weighted * scaled, -1, keepdims=True)
    return (factor * (weighted - scaled * centre), jnp.sum(grads_in * scaled, 0))


def contract_rows(first, second):
    return lax.dot_general(
        first, second, (((0,), (0,)), ((), ())), preferred_element_type=jnp.float32
    )


def contract_last(first, second):
    return lax.dot_general(
        first, second, (((1,), (1,)), ((), ())), preferred_element_type=jnp.float32
    )


def matmul(first, second):
    return jnp.dot(first, second, preferred_element_type=jnp.float32)


def widen(array, width):
    return jnp.pad(array, ((0, 0), (0, width - array.shape[1])))


CHUNK = 256


def grant(mebibytes):
    return pltpu.CompilerParams(vmem_limit_bytes=mebibytes * 2**20)


def split_rows(far):
    one, two = cuts(far.shape[0])
    return far[:one], far[one:two], far[two:]


def piece_rows(rows):
    one, two = cuts(rows)
    return one, two - one, rows - two


def join_refs(refs, out, width):
    at = 0
    for ref in refs:
        rows = ref.shape[0]
        out[at : at + rows, :] = ref[:, :width]
        at += rows


def split_refs(value, refs, at):
    for ref in refs:
        rows = ref.shape[0]
        ref[...] = value[at : at + rows].astype(ref.dtype)
        at += rows


def row_sizes(rows):
    return [rows] * 7 + list(piece_rows(rows))


def swap_halves(value):
    lanes = value.shape[1]
    lane = lax.broadcasted_iota(jnp.int32, value.shape, 1) % ROPE
    return jnp.where(
        lane < ROPE // 2, pltpu.roll(value, lanes - ROPE // 2, 1), pltpu.roll(value, ROPE // 2, 1)
    )


def key_places(place, rows):
    lane = lax.broadcasted_iota(jnp.int32, (1, rows), 1)
    return jnp.concatenate([place[slot] * rows + lane for slot in range(8)], 1)


def query_places(place, rows, start):
    row = lax.broadcasted_iota(jnp.int32, (rows, 1), 0)
    return jnp.concatenate([place[2 * start] * rows + row, place[2 * start + 1] * rows + row], 0)


def attention_kernel(
    heads, rank, place, *refs
):
    (blocks, refs) = refs[:8], refs[8:]
    gain, query_w, down_t, latent_gain, up_w, out_w, cosine, sine = refs[:8]
    normed, queries, keys, values, logsums, scaled, factors, compressed, attended = refs[8:17]
    branch = refs[17:25]
    latent, raw, pair = refs[25:]
    f32, bf16 = jnp.float32, jnp.bfloat16
    seq_len, width = normed.shape
    rows = seq_len // 8
    scale = (NOPE + ROPE) ** (-0.5)

    join_refs(blocks, normed, width)

    def norm_rows(step, carry):
        at = pl.ds(pl.multiple_of(step * rows, rows), rows)
        value = normed[at, :].astype(f32)
        factor = lax.rsqrt(jnp.mean(value * value, 1, keepdims=True) + EPSILON)
        normed[at, :] = (value * factor * gain[...]).astype(bf16)
        return carry

    lax.fori_loop(0, 8, norm_rows, 0)
    latent[:, : rank + ROPE] = contract_last(normed[...], down_t[...])
    raw[...] = matmul(normed[...], query_w[...])

    def project_rows(step, carry):
        at = pl.ds(pl.multiple_of(step * rows, rows), rows)
        table = pl.ds(pl.multiple_of(place[step] * rows, rows), rows)
        cos, sin = cosine[table, :], sine[table, :]
        value = latent[at, :rank]
        factor = lax.rsqrt(jnp.mean(value * value, 1, keepdims=True) + EPSILON)
        factors[at, :] = factor
        scaled[at, :] = value * factor
        compressed[at, :] = (value * factor * latent_gain[...]).astype(bf16)
        left_half = lax.broadcasted_iota(jnp.int32, (rows, NOPE), 1) < ROPE
        key_rope = latent[at, rank:]
        key_rope = jnp.where(left_half, key_rope, pltpu.roll(key_rope, ROPE, 1))
        key_rope = (key_rope * cos + swap_halves(key_rope) * sin).astype(bf16)
        one, two = raw[at, NOPE : 2 * NOPE], raw[at, 2 * NOPE :]
        plain = raw[at, :NOPE], jnp.where(left_half, pltpu.roll(one, ROPE, 1), pltpu.roll(two, ROPE, 1))
        query_rope = jnp.where(left_half, one, two)
        query_rope = query_rope * cos + swap_halves(query_rope) * sin
        for head in range(heads):
            queries[head, at, :NOPE] = plain[head].astype(bf16)
            queries[head, at, NOPE:] = jnp.where(left_half == (head == 0), query_rope, 0.0).astype(bf16)
            keys[head, at, NOPE:] = key_rope
        return carry

    lax.fori_loop(0, 8, project_rows, 0)
    key_value = matmul(compressed[...], up_w[...]).astype(bf16)
    for head in range(heads):
        start = head * (NOPE + VDIM)
        keys[head, :, :NOPE] = key_value[:, start : start + NOPE]
        values[head] = key_value[:, start + NOPE : start + NOPE + VDIM]

    key_place = key_places(place, rows)

    def attend_rows(step, carry):
        at = pl.ds(pl.multiple_of(step * 2 * rows, 2 * rows), 2 * rows)
        allowed = key_place <= query_places(place, rows, step)
        for head in range(heads):
            scores = contract_last(queries[head, at, :], keys[head]) * scale
            scores = jnp.where(allowed, scores, -1e30)
            highest = jnp.max(scores, 1, keepdims=True)
            weights = jnp.exp(scores - highest)
            denominator = jnp.sum(weights, 1, keepdims=True)
            logsums[head, at, :] = highest + jnp.log(denominator)
            shares = (weights * (1.0 / denominator)).astype(bf16)
            attended[at, head * VDIM : (head + 1) * VDIM] = matmul(shares, values[head]).astype(bf16)
        return carry

    lax.fori_loop(0, 4, attend_rows, 0)
    half = seq_len // 2
    pair[...] = contract_last(attended[:half], out_w[...])
    split_refs(pair, branch[:4], 0)
    pair[...] = contract_last(attended[half:], out_w[...])
    split_refs(pair, branch[4:], 0)


def attention(place, blocks, gain, query_w, down_t, latent_gain, up_w, out_w, cosine, sine):
    rows = blocks[0].shape[0]
    seq_len, width = rows * 8, blocks[0].shape[1]
    rank = up_w.shape[0]
    heads = up_w.shape[1] // (NOPE + VDIM)
    f32, bf16 = jnp.float32, jnp.bfloat16
    shape = jax.ShapeDtypeStruct
    vmem = pl.BlockSpec(memory_space=pltpu.VMEM)
    outs = [
        shape((seq_len, width), bf16),
        shape((heads, seq_len, 2 * NOPE), bf16),
        shape((heads, seq_len, 2 * NOPE), bf16),
        shape((heads, seq_len, VDIM), bf16),
        shape((heads, seq_len, 1), f32),
        shape((seq_len, rank), f32),
        shape((seq_len, 1), f32),
        shape((seq_len, rank), bf16),
        shape((seq_len, heads * VDIM), bf16),
    ] + [shape((rows, width), bf16)] * 8
    return pl.pallas_call(
        functools.partial(attention_kernel, heads, rank),
        in_specs=[pl.BlockSpec(memory_space=pltpu.SMEM)] + [vmem] * 16,
        out_specs=[vmem] * len(outs),
        out_shape=outs,
        scratch_shapes=[
            pltpu.VMEM((seq_len, rank + NOPE), f32),
            pltpu.VMEM((seq_len, query_w.shape[1]), f32),
            pltpu.VMEM((seq_len // 2, width), f32),
        ],
        compiler_params=grant(56),
        cost_estimate=pl.CostEstimate(
            flops=20 * seq_len * width * width // 4, bytes_accessed=30 * 2**20, transcendentals=0
        ),
        name="attention",
    )(place, *blocks, gain, query_w, down_t, latent_gain, up_w, out_w, cosine, sine)


def attention_grad_kernel(heads, place, *refs):
    (blocks, refs) = refs[:8], refs[8:]
    out_w, cosine, sine, queries, keys, values, logsums = refs[:7]
    branch_grads, query_grads, kv_grads, rope_grads = refs[7:11]
    out_grads, key_grads, value_grads = refs[11:]
    f32, bf16 = jnp.float32, jnp.bfloat16
    seq_len, width = branch_grads.shape
    rows = seq_len // 8
    scale = (NOPE + ROPE) ** (-0.5)

    join_refs(blocks, branch_grads, width)
    out_grads[...] = matmul(branch_grads[...], out_w[...]).astype(bf16)
    key_grads[...] = jnp.zeros_like(key_grads)
    value_grads[...] = jnp.zeros_like(value_grads)
    key_place = key_places(place, rows)

    def attend_rows(step, carry):
        at = pl.ds(pl.multiple_of(step * 2 * rows, 2 * rows), 2 * rows)
        allowed = key_place <= query_places(place, rows, step)
        plain, ropes = [], []
        for head in range(heads):
            query = queries[head, at, :]
            out_grad = out_grads[at, head * VDIM : (head + 1) * VDIM]
            scores = contract_last(query, keys[head]) * scale
            shares = jnp.where(allowed, jnp.exp(scores - logsums[head, at, :]), 0.0)
            share_grads = contract_last(out_grad, values[head])
            centre = jnp.sum(shares * share_grads, 1, keepdims=True)
            score_grads = (shares * (share_grads - centre)).astype(bf16)
            value_grads[head] += contract_rows(shares.astype(bf16), out_grad)
            key_grads[head] += contract_rows(score_grads, query)
            query_grad = matmul(score_grads, keys[head]) * scale
            plain.append(query_grad[:, :NOPE])
            ropes.append(query_grad[:, NOPE:])
        left_half = lax.broadcasted_iota(jnp.int32, ropes[0].shape, 1) < ROPE
        rope = jnp.where(left_half, ropes[0], ropes[1])
        tables = [
            pl.ds(pl.multiple_of(place[2 * step + k] * rows, rows), rows) for k in range(2)
        ]
        cos = jnp.concatenate([cosine[table, :] for table in tables], 0)
        sin = jnp.concatenate([sine[table, :] for table in tables], 0)
        rope = rope * cos - swap_halves(rope) * sin
        turned = pltpu.roll(plain[1], ROPE, 1)
        query_grads[at, :NOPE] = plain[0].astype(bf16)
        query_grads[at, NOPE : 2 * NOPE] = jnp.where(left_half, rope, turned).astype(bf16)
        query_grads[at, 2 * NOPE :] = jnp.where(left_half, turned, rope).astype(bf16)
        return carry

    lax.fori_loop(0, 4, attend_rows, 0)
    for head in range(heads):
        start = head * (NOPE + VDIM)
        kv_grads[:, start : start + NOPE] = (key_grads[head, :, :NOPE] * scale).astype(bf16)
        kv_grads[:, start + NOPE : start + NOPE + VDIM] = value_grads[head].astype(bf16)

    def rope_rows(step, carry):
        at = pl.ds(pl.multiple_of(step * rows, rows), rows)
        table = pl.ds(pl.multiple_of(place[step] * rows, rows), rows)
        rope = sum(key_grads[head, at, NOPE:] for head in range(heads)) * scale
        for turn in range(1, NOPE // ROPE):
            rope = rope + pltpu.roll(rope, turn * ROPE, 1)
        rope = rope * cosine[table, :] - swap_halves(rope) * sine[table, :]
        lane = lax.broadcasted_iota(jnp.int32, rope.shape, 1)
        rope_grads[at, :] = jnp.where(lane < ROPE, rope, 0.0).astype(bf16)
        return carry

    lax.fori_loop(0, 8, rope_rows, 0)


def attention_grad(place, blocks, out_w, cosine, sine, queries, keys, values, logsums):
    seq_len, width = queries.shape[1], blocks[0].shape[1]
    heads = queries.shape[0]
    f32, bf16 = jnp.float32, jnp.bfloat16
    shape = jax.ShapeDtypeStruct
    vmem = pl.BlockSpec(memory_space=pltpu.VMEM)
    return pl.pallas_call(
        functools.partial(attention_grad_kernel, heads),
        in_specs=[pl.BlockSpec(memory_space=pltpu.SMEM)] + [vmem] * 15,
        out_specs=[vmem] * 4,
        out_shape=[
            shape((seq_len, width), bf16),
            shape((seq_len, heads * (NOPE + ROPE)), bf16),
            shape((seq_len, heads * (NOPE + VDIM)), bf16),
            shape((seq_len, NOPE), bf16),
        ],
        scratch_shapes=[
            pltpu.VMEM((seq_len, heads * VDIM), bf16),
            pltpu.VMEM((heads, seq_len, 2 * NOPE), f32),
            pltpu.VMEM((heads, seq_len, VDIM), f32),
        ],
        compiler_params=grant(56),
        cost_estimate=pl.CostEstimate(
            flops=8 * seq_len * width * width // 4, bytes_accessed=20 * 2**20, transcendentals=0
        ),
        name="attention_grad",
    )(place, *blocks, out_w, cosine, sine, queries, keys, values, logsums)


def input_kernel(rank, *refs):
    query_grads, kv_grads, rope_grads, gain, query_w, down_t, latent_gain, up_w = refs[:8]
    normed, scaled, factors = refs[8:11]
    lhs, input_gain, latent_gains = refs[11:14]
    parts, pair = refs[14:24], refs[24]
    f32, bf16 = jnp.float32, jnp.bfloat16
    seq_len, width = normed.shape
    rows = seq_len // 8
    lhs[:, rank:] = rope_grads[...]
    latent_gains[...] = jnp.zeros_like(latent_gains)

    def latent_rows(step, carry):
        at = pl.ds(pl.multiple_of(step * 4 * rows, 4 * rows), 4 * rows)
        back = contract_last(kv_grads[at, :], up_w[...])
        value = scaled[at, :]
        latent_gains[...] += jnp.sum(back * value, 0, keepdims=True)
        weighted = back * latent_gain[...]
        centre = jnp.mean(weighted * value, 1, keepdims=True)
        lhs[at, :rank] = (
            factors[at, :] * (weighted - value * centre)
        ).astype(bf16)
        return carry

    lax.fori_loop(0, 2, latent_rows, 0)
    input_gain[...] = jnp.zeros_like(input_gain)
    half = seq_len // 2
    for order in (1, 0):
        start = order * half
        at = slice(start, start + half)
        pair[...] = contract_last(query_grads[at, :], query_w[...]) + matmul(lhs[at, : rank + ROPE], down_t[...])
        split_refs(pair, parts[4:] if order else parts[:4], 0)
        for step in range(4):
            spot = slice(step * rows, (step + 1) * rows)
            input_gain[...] += jnp.sum(
                pair[spot, :] * normed[start + step * rows : start + (step + 1) * rows, :].astype(f32),
                0,
                keepdims=True,
            )
    input_gain[...] = input_gain[...] / gain[...]


def input_grads(query_grads, kv_grads, rope_grads, gain, query_w, down_t, latent_gain, up_w, normed, scaled, factors, sizes):
    seq_len, width = normed.shape
    rank = up_w.shape[0]
    f32, bf16 = jnp.float32, jnp.bfloat16
    shape = jax.ShapeDtypeStruct
    vmem = pl.BlockSpec(memory_space=pltpu.VMEM)
    outs = [
        shape((seq_len, rank + NOPE), bf16),
        shape((1, width), f32),
        shape((1, rank), f32),
    ] + [shape((size, width), bf16) for size in sizes]
    return pl.pallas_call(
        functools.partial(input_kernel, rank),
        in_specs=[vmem] * 11,
        out_specs=[vmem] * len(outs),
        out_shape=outs,
        scratch_shapes=[pltpu.VMEM((seq_len // 2, width), f32)],
        compiler_params=grant(56),
        cost_estimate=pl.CostEstimate(
            flops=6 * seq_len * width * width // 4, bytes_accessed=20 * 2**20, transcendentals=0
        ),
        name="input_grads",
    )(query_grads, kv_grads, rope_grads, gain, query_w, down_t, latent_gain, up_w, normed, scaled, factors)


def forward_kernel(blocks, expert_units, *refs):
    hid_blocks, cot_blocks, refs = refs[:blocks], refs[blocks : blocks + 4], refs[blocks + 4 :]
    own, router, gate_w, up_w, down_w, scaled, gate_g, up_g, logit_g, hid, cot, probs, gate, chosen, total = refs
    j = pl.program_id(0)
    width = hid.shape[1]
    experts = own.shape[1]

    @pl.when(j == 0)
    def _():
        join_refs(hid_blocks, hid, width)
        join_refs(cot_blocks, cot, width)
        for slot, ref in enumerate(cot_blocks):
            rows = ref.shape[0]
            mask = ref[:, width : width + experts].astype(jnp.float32)
            chosen[slot * rows : (slot + 1) * rows, :] = jnp.sum(mask * own[...], 1, keepdims=True)
        logits = matmul(hid[...], router[...])
        powers = jnp.exp(logits - jnp.max(logits, 1, keepdims=True))
        probs[...] = powers / jnp.sum(powers, 1, keepdims=True)
        gate[...] = jnp.sum(probs[...] * own[...], 1, keepdims=True) * chosen[...]
        total[...] = jnp.zeros_like(total)

    column = j * gate_w.shape[1] + lax.broadcasted_iota(jnp.int32, (1, gate_w.shape[1]), 1)
    is_expert = column < expert_units
    pre_gate = matmul(hid[...], gate_w[...])
    pre_up = matmul(hid[...], up_w[...])
    back = matmul(cot[...], down_w[...])
    sigmoid = 1.0 / (1.0 + jnp.exp(-pre_gate))
    act = pre_gate * sigmoid
    slope = sigmoid * (1.0 + pre_gate * (1.0 - sigmoid))
    hidden = act * pre_up
    scale = jnp.where(is_expert, gate[...], 1.0)
    scaled[...] = (hidden * scale).astype(scaled.dtype)
    total[...] += jnp.sum(jnp.where(is_expert, hidden * back, 0.0), 1, keepdims=True)
    back = back * scale
    gate_g[...] = (back * pre_up * slope).astype(gate_g.dtype)
    up_g[...] = (back * act).astype(up_g.dtype)

    @pl.when(j == pl.num_programs(0) - 1)
    def _():
        own_prob = jnp.sum(probs[...] * own[...], 1, keepdims=True)
        logit_g[...] = (total[...] * chosen[...] * probs[...] * (own[...] - own_prob)).astype(logit_g.dtype)


def feed_forward(hid, cot, own, router, gate_w, up_w, weight_out, expert_units):
    rows, width = sum(block.shape[0] for block in hid), hid[0].shape[1]
    units = weight_out.shape[1]
    steps = units // CHUNK
    experts = own.shape[1]
    out = pl.BlockSpec((rows, CHUNK), lambda j: (0, j))
    whole = pl.BlockSpec(memory_space=pltpu.VMEM)
    wide = jax.ShapeDtypeStruct((rows, units), jnp.bfloat16)
    joined = jax.ShapeDtypeStruct((rows, width), jnp.bfloat16)
    column = pltpu.VMEM((rows, 1), jnp.float32)
    return pl.pallas_call(
        functools.partial(forward_kernel, len(hid), expert_units),
        grid=(steps,),
        in_specs=[whole] * (len(hid) + 6)
        + [
            pl.BlockSpec((width, CHUNK), lambda j: (0, j)),
            pl.BlockSpec((width, CHUNK), lambda j: (0, j)),
            pl.BlockSpec((width, CHUNK), lambda j: (0, j)),
        ],
        out_specs=[out, out, out, whole, whole, whole],
        out_shape=[wide, wide, wide, jax.ShapeDtypeStruct((rows, experts), jnp.bfloat16), joined, joined],
        scratch_shapes=[pltpu.VMEM((rows, experts), jnp.float32), column, column, column],
        compiler_params=grant(56),
        cost_estimate=pl.CostEstimate(
            flops=6 * rows * width * units, bytes_accessed=6 * width * units, transcendentals=rows * units
        ),
        name="feed_forward",
    )(*hid, *cot, own, router, gate_w, up_w, weight_out)


def input_grad_kernel(gate_g, up_g, logit_g, gate_w, up_w, router, *outs):
    total = contract_last(gate_g[...], gate_w[...]) + contract_last(up_g[...], up_w[...])
    split_refs(total + contract_last(logit_g[...], router[...]), outs, 0)


def input_grad(gate_g, up_g, logit_g, gate_w, up_w, router, sizes):
    rows, units = gate_g.shape
    width, experts = router.shape
    part = min(512, width)
    whole = pl.BlockSpec(memory_space=pltpu.VMEM)
    return pl.pallas_call(
        input_grad_kernel,
        grid=(width // part,),
        in_specs=[
            whole,
            whole,
            whole,
            pl.BlockSpec((part, units), lambda j: (j, 0)),
            pl.BlockSpec((part, units), lambda j: (j, 0)),
            pl.BlockSpec((part, experts), lambda j: (j, 0)),
        ],
        out_specs=[pl.BlockSpec((size, part), lambda j: (0, j)) for size in sizes],
        out_shape=[jax.ShapeDtypeStruct((size, width), jnp.bfloat16) for size in sizes],
        compiler_params=grant(56),
        cost_estimate=pl.CostEstimate(
            flops=4 * rows * width * units, bytes_accessed=4 * width * units, transcendentals=0
        ),
        name="input_grad",
    )(gate_g, up_g, logit_g, gate_w, up_w, router)


def output_kernel(first, second, down_w, *outs):
    scaled = jnp.concatenate([first[...], second[...]], 0)
    split_refs(contract_last(scaled, down_w[...]), outs, 0)


def mixer_output(scaled, weight_out, sizes):
    rows, units = scaled[0].shape
    width = weight_out.shape[0]
    part = min(512, width)
    return pl.pallas_call(
        output_kernel,
        grid=(width // part,),
        in_specs=[
            pl.BlockSpec(memory_space=pltpu.VMEM),
            pl.BlockSpec(memory_space=pltpu.VMEM),
            pl.BlockSpec((part, units), lambda j: (j, 0)),
        ],
        out_specs=[pl.BlockSpec((size, part), lambda j: (0, j)) for size in sizes],
        out_shape=[jax.ShapeDtypeStruct((size, width), jnp.bfloat16) for size in sizes],
        compiler_params=grant(56),
        cost_estimate=pl.CostEstimate(
            flops=4 * rows * width * units, bytes_accessed=2 * width * units, transcendentals=0
        ),
        name="mixer_output",
    )(*scaled, weight_out)


def store_blocks(out, product, at=0):
    rows = product.shape[0]
    lanes = out.shape[2]
    for slot, block in enumerate(BLOCKS):
        out[slot, at : at + rows, :] = product[:, block * lanes : (block + 1) * lanes].astype(out.dtype)


def mixer_weight_kernel(la, lb, ra, rb, *refs):
    store_blocks(refs[-1], contract_rows(la[...], ra[...]) + contract_rows(lb[...], rb[...]))


def mixer_weights(order, lhs, rhs, kept):
    rows, units = lhs[0].shape
    width = rhs[0].shape[1]
    steps = units // CHUNK
    part = pl.BlockSpec((rows, CHUNK), lambda j: (0, j))
    whole = pl.BlockSpec(memory_space=pltpu.VMEM)
    kept = [] if kept is None else [kept]
    return pl.pallas_call(
        mixer_weight_kernel,
        grid=(steps,),
        in_specs=[part, part, whole, whole] + [pl.BlockSpec(memory_space=pl.ANY)] * len(kept),
        out_specs=pl.BlockSpec((16, CHUNK, width // 16), lambda j: (0, j + order * steps, 0)),
        out_shape=jax.ShapeDtypeStruct((16, 3 * units, width // 16), jnp.bfloat16),
        input_output_aliases={4: 0} if kept else {},
        compiler_params=grant(56),
        cost_estimate=pl.CostEstimate(
            flops=4 * rows * width * units, bytes_accessed=2 * width * units, transcendentals=0
        ),
        name="mixer_weights",
    )(*lhs, *rhs, *kept)


def latent_weight_kernel(spare, order, lhs, normed, compressed, kv_grads, router, input_gain, mixer_gain, latent_gain, mine, other, wide):
    lanes = mine.shape[2]
    columns = lhs.shape[1]
    wide[:columns, :] = contract_rows(lhs[...], normed[...])
    at = spare + router.shape[0]
    wide[spare:at, :] = router[...]
    wide[at : at + 1, :] = input_gain[...]
    wide[at + 1 : at + 2, :] = mixer_gain[...]
    rank, width = latent_gain.shape[1], wide.shape[1]
    share = rank // 16
    entry = lax.broadcasted_iota(jnp.int32, (rank, width), 0)
    lane = lax.broadcasted_iota(jnp.int32, (rank, width), 1)
    each = share // 8
    spot = entry // share * lanes + entry % share // each * (lanes // 8) + entry % each
    wide[at + 2 : at + 3, :] = matmul(latent_gain[...], (spot == lane).astype(jnp.float32))
    product = contract_rows(compressed[...], kv_grads[...])
    for block in range(16):
        for step in range(product.shape[1] // lanes):
            start = columns + step * share
            wide[start : start + share, block * lanes : (block + 1) * lanes] = product[
                block * share : (block + 1) * share, step * lanes : (step + 1) * lanes
            ]
    for slot in range(16):
        at = pl.multiple_of(order[slot] * lanes, lanes)
        block = wide[:, pl.ds(at, lanes)].astype(mine.dtype)
        if slot < 8:
            mine[slot] = block
        else:
            other[slot - 8] = block


def latent_weights(order, lhs, spare, normed, compressed, kv_grads, *small):
    rows, columns = lhs.shape
    width = normed.shape[1]
    lanes = width // 16
    total = columns + compressed.shape[1] // 16 * kv_grads.shape[1] // lanes
    vmem = pl.BlockSpec(memory_space=pltpu.VMEM)
    return pl.pallas_call(
        functools.partial(latent_weight_kernel, spare),
        in_specs=[pl.BlockSpec(memory_space=pltpu.SMEM)] + [vmem] * 8,
        out_specs=[vmem] * 2,
        out_shape=[jax.ShapeDtypeStruct((8, total, lanes), jnp.bfloat16)] * 2,
        scratch_shapes=[pltpu.VMEM((total, width), jnp.float32)],
        compiler_params=grant(56),
        cost_estimate=pl.CostEstimate(
            flops=2 * rows * width * columns, bytes_accessed=4 * width * columns, transcendentals=0
        ),
        name="latent_weights",
    )(order, lhs, normed, compressed, kv_grads, *small)


def head_weight_kernel(query_grads, normed, attended, branch_grads, out):
    store_blocks(out, contract_rows(query_grads[...], normed[...]))
    store_blocks(out, contract_rows(attended[...], branch_grads[...]), query_grads.shape[1])


def head_weights(query_grads, normed, attended, branch_grads):
    rows, width = normed.shape
    total = query_grads.shape[1] + attended.shape[1]
    vmem = pl.BlockSpec(memory_space=pltpu.VMEM)
    return pl.pallas_call(
        head_weight_kernel,
        in_specs=[vmem] * 4,
        out_specs=vmem,
        out_shape=jax.ShapeDtypeStruct((16, total, width // 16), jnp.bfloat16),
        compiler_params=grant(56),
        cost_estimate=pl.CostEstimate(
            flops=2 * rows * width * total, bytes_accessed=4 * width * rows, transcendentals=0
        ),
        name="head_weights",
    )(query_grads, normed, attended, branch_grads)


def latent_finish_kernel(columns, late, rest, up):
    lanes, share = late.shape[1], up.shape[0]
    rest[...] = late[:columns, :].astype(jnp.float32).T.astype(rest.dtype)
    for step in range(up.shape[1] // lanes):
        start = columns + step * share
        up[:, step * lanes : (step + 1) * lanes] = late[start : start + share, :].astype(jnp.float32)


def latent_finish(late, columns, up_shape):
    return pl.pallas_call(
        functools.partial(latent_finish_kernel, columns),
        out_shape=[
            jax.ShapeDtypeStruct((late.shape[1], columns), jnp.bfloat16),
            jax.ShapeDtypeStruct(up_shape, jnp.float32),
        ],
        compiler_params=grant(8),
        name="latent_finish",
    )(late)


def head_finish_kernel(query_wide, late, query, output):
    query[...] = late[:query_wide, :].astype(jnp.float32).T
    output[...] = late[query_wide:, :].astype(jnp.float32).T


def head_finish(late, query_wide):
    rows, lanes = late.shape
    f32 = jnp.float32
    return pl.pallas_call(
        functools.partial(head_finish_kernel, query_wide),
        out_shape=[
            jax.ShapeDtypeStruct((lanes, query_wide), f32),
            jax.ShapeDtypeStruct((lanes, rows - query_wide), f32),
        ],
        compiler_params=grant(8),
        name="head_finish",
    )(late)


def mixer_finish_kernel(expert_units, shared_units, units, totals, *outs):
    for order in range(3):
        start = order * units
        expert = totals[start : start + expert_units, :].astype(jnp.float32)
        outs[order][:, 0, :] = expert.T
        start += expert_units
        outs[3 + order][...] = totals[start : start + shared_units, :].astype(jnp.float32)


def mixer_finish(totals, expert_units, shared_units, units):
    lanes = totals.shape[1]
    f32 = jnp.float32
    return pl.pallas_call(
        functools.partial(mixer_finish_kernel, expert_units, shared_units, units),
        out_shape=[jax.ShapeDtypeStruct((lanes, 1, expert_units), f32)] * 3
        + [jax.ShapeDtypeStruct((shared_units, lanes), f32)] * 3,
        compiler_params=grant(16),
        name="mixer_finish",
    )(totals)


def on_device(
    tokens,
    expert_index,
    cotangent,
    input_gain,
    query_weight,
    latent_down,
    latent_gain,
    latent_up,
    output_weight,
    mixer_gain,
    router_weight,
    shared_gate,
    shared_up,
    shared_down,
    expert_gate,
    expert_up,
    expert_down,
):
    tok_rows, width = tokens.shape
    group = lax.axis_index("tensor")
    z, x = group // 4, group % 4
    rank = latent_up.shape[0]
    heads_local = query_weight.shape[1] // (NOPE + ROPE)
    experts_all = router_weight.shape[1]
    scale = (NOPE + ROPE) ** (-0.5)
    expert_units = expert_gate.shape[2]
    shared_units = shared_gate.shape[1]
    shared_wide = -(-shared_units // 128) * 128
    units = expert_units + shared_wide
    bf16, f32 = jnp.bfloat16, jnp.float32

    first_order, second_order = ORDER[:4], ORDER[4:]
    sizes = row_sizes(tok_rows)
    seq_len = tok_rows * 8

    cosine, sine = rope_tables(jnp.arange(seq_len, dtype=jnp.int32))
    cosine = jnp.concatenate([cosine] * (2 * NOPE // ROPE), 1)
    sine = jnp.concatenate([-sine, sine] * (NOPE // ROPE), 1)
    chosen = (expert_index[:, :, None] == jnp.arange(experts_all, dtype=jnp.int32)).any(1)
    sent = jnp.concatenate([cotangent, widen(chosen.astype(bf16), 128)], 1)
    shared_gate, shared_up, shared_down = (
        widen(part, shared_wide) for part in (shared_gate, shared_up, shared_down)
    )
    got = pair_gather_first(tokens)
    got, cosine, sine, sent, shared_gate, shared_up, shared_down = fence(
        got, cosine, sine, sent, shared_gate, shared_up, shared_down
    )
    got = pair_gather_second(got)
    weight_out = jnp.concatenate([expert_down.reshape(width, expert_units), shared_down], 1)
    got, weight_out, sent = fence(got, weight_out, sent)

    upstream = pair_gather_first(sent)

    place = jnp.stack([(z ^ dz) * 4 + (x + dx) % 4 for dz, dx in ORDER]).astype(jnp.int32)
    outs = attention(
        place,
        [got[rel] for rel in ORDER],
        input_gain[None],
        query_weight,
        latent_down.T,
        latent_gain[None],
        latent_up,
        output_weight,
        cosine,
        sine,
    )
    normed_all, queries, keys, values, logsums, latent_scaled, latent_factor = outs[:7]
    compressed, attended = outs[7:9]
    part = dict(zip(ORDER, outs[9:]))
    part, upstream = fence(part, upstream)
    sums = pair_scatter_first(part)
    gate_w = jnp.concatenate([expert_gate.reshape(width, expert_units), shared_gate], 1)
    sums, part, gate_w, expert_up, shared_up = fence(sums, part, gate_w, expert_up, shared_up)
    ends = pair_scatter_second(sums, part)
    up_w = jnp.concatenate([expert_up.reshape(width, expert_units), shared_up], 1)
    ends, up_w = fence(ends, up_w)
    branch = scatter_total(part, ends)

    middle = tokens.astype(f32) + branch
    second_normed, second_scaled, second_factor = normalize(middle, mixer_gain)
    own_expert = (jnp.arange(experts_all) == group).astype(f32)[None, :]

    def feed(got, order):
        return feed_forward(
            listed(got, order),
            [upstream[rel] for rel in order],
            own_expert,
            router_weight,
            gate_w,
            up_w,
            weight_out,
            expert_units,
        )

    def input_part(fed):
        return input_grad(*fed[1:4], gate_w, up_w, router_weight, [tok_rows] * 4)

    got = gather_second(gather_first(second_normed.astype(bf16)))
    fed_first = feed(got, first_order)
    got, fed_first, upstream = fence(got, fed_first, upstream)
    got, upstream = gather_third(got), pair_gather_second(upstream)
    first_part = input_part(fed_first)
    got, upstream, first_part = fence(got, upstream, first_part)
    fed_second = feed(got, second_order)
    hidden_scaled, gate_grads, up_grads, logit_grads, hidden, upstream = zip(fed_first, fed_second)
    part = dict(zip(second_order, input_part(fed_second)))
    sums = pair_scatter_first(part)
    weight_parts = mixer_weights(0, gate_grads, hidden, None)
    sums, weight_parts = fence(sums, weight_parts)
    part.update(zip(first_order, first_part))
    ends = pair_scatter_second(sums, part)
    weight_parts = mixer_weights(1, up_grads, hidden, weight_parts)
    weight_parts = mixer_weights(2, hidden_scaled, upstream, weight_parts)
    ends, weight_parts = fence(ends, weight_parts)
    weight_totals = level_scatter_sum(weight_parts)
    mixer_back = scatter_total(part, ends)
    middle_from, grad_mixer_gain = norm_backward(
        mixer_back, second_scaled, second_factor, mixer_gain
    )
    middle_grads = cotangent.astype(f32) + middle_from
    got = pair_gather_first(middle_grads.astype(bf16))
    out_blocks = mixer_output(hidden_scaled, weight_out, sizes)
    grad_router = sum(contract_rows(g, hid) for g, hid in zip(logit_grads, hidden))
    got, out_blocks, grad_router = fence(got, out_blocks, grad_router)
    got = pair_gather_second(got)

    out = {**named(out_blocks[:4], first_order), **named(out_blocks[4:], second_order)}
    out_pieces, out_last = scatter_first(out), right(out[0, 1])
    grads = attention_grad(
        place, [got[rel] for rel in ORDER], output_weight, cosine, sine, queries, keys, values, logsums
    )
    out_pieces, out_last, grads = fence(out_pieces, out_last, grads)
    branch_all, query_grads, kv_grads, rope_grads = grads
    out_sums = scatter_second(out_pieces, out)
    grads = input_grads(
        query_grads,
        kv_grads,
        rope_grads,
        input_gain[None],
        query_weight,
        latent_down.T,
        latent_gain[None],
        latent_up,
        normed_all,
        latent_scaled,
        latent_factor,
        sizes,
    )
    out_sums, grads = fence(out_sums, grads)
    latent_grads, grad_input_gain, grad_latent_gain = grads[:3]
    part = {**named(grads[3:7], first_order), **named(grads[7:], second_order)}
    out_ends = scatter_third(out_sums, out)
    pieces = scatter_first(part)

    wide = latent_down.shape[1]
    query_wide = query_weight.shape[1]
    lanes = width // 16
    share = rank // 16
    mine, other = latent_weights(
        dp_order(),
        latent_grads,
        wide,
        normed_all,
        compressed,
        kv_grads,
        grad_router,
        grad_input_gain,
        grad_mixer_gain[None],
        grad_latent_gain,
    )
    pieces, out_ends, mine, other = fence(pieces, out_ends, mine, other)
    layer_out = (middle + scatter_total(out, (out_ends, out_last))).astype(bf16)
    sums, last = scatter_second(pieces, part), right(part[0, 1])
    other = lax.ppermute(other, "dp", CORE)
    head_parts = head_weights(query_grads, normed_all, attended, branch_all)
    sums, last, other, head_parts = fence(sums, last, other, head_parts)
    head_totals = level_scatter_sum(head_parts)
    terms = dp_second(plus(mine, other))
    to_left, to_across = plus(part[0, -1], sums[0], sums[1]), plus(part[1, 0], sums[2])
    end_left = left(to_left)
    weight_total = high_sum(weight_totals)
    terms, end_left, to_across, weight_total = fence(terms, end_left, to_across, weight_total)
    late = dp_third(terms)
    ends = end_left, across(to_across)
    normed_grads = scatter_total(part, (ends, last))
    _, first_scaled, first_factor = normalize(tokens.astype(f32), input_gain)
    input_from, _ = norm_backward(normed_grads, first_scaled, first_factor, input_gain)
    grad_tokens = middle_grads + input_from
    columns = latent_grads.shape[1]
    rest, total_up = latent_finish(late, columns, (share, latent_up.shape[1]))
    rest = rest.reshape(8, lanes // 8, -1)
    rest = jnp.sum(lax.all_to_all(rest, "tensor", 0, 0, tiled=True).astype(f32), 0)
    at = wide + experts_all
    expert_outs = mixer_finish(weight_total, expert_units, shared_units, units)
    total_query, total_output = head_finish(high_sum(head_totals), query_wide)
    return (
        layer_out,
        grad_tokens,
        rest[:, at],
        total_query,
        rest[:, :wide],
        rest[: share // 8, at + 2],
        total_up,
        total_output,
        rest[:, at + 1],
        rest[:, wide:at],
        *[shared.T for shared in expert_outs[3:]],
        *expert_outs[:3],
    )


def solution(mesh):
    rows = P(("dp", "tensor"), None)
    columns = P(None, "tensor")
    middle = P(None, "tensor", None)
    return jax.shard_map(
        on_device,
        mesh=mesh,
        in_specs=(rows, rows, rows, P(), columns, P(), P(), columns, columns, P(), P())
        + (columns,) * 3
        + (middle,) * 3,
        out_specs=(
            rows,
            rows,
            P(("dp", "tensor")),
            P("dp", "tensor"),
            rows,
            P(("dp", "tensor")),
            P("dp", "tensor"),
            P("dp", "tensor"),
            P(("dp", "tensor")),
            rows,
        )
        + (P("dp", "tensor"),) * 3
        + (P("dp", "tensor", None),) * 3,
        check_vma=False,
    )
```

```python
import functools

import jax
import jax.numpy as jnp
from jax import lax
from jax.experimental import pallas as pl
from jax.experimental.pallas import tpu as pltpu
from jax.sharding import PartitionSpec as P

NOPE = 128
ROPE = 64
VDIM = 128
EPSILON = 1e-06

ORDER = ((0, 0), (0, -1), (0, 1), (1, 0), (0, 2), (1, 1), (1, -1), (1, 2))
SLOT = {rel: slot for slot, rel in enumerate(ORDER)}

LEFT = [(z * 4 + x, z * 4 + (x - 1) % 4) for z in range(2) for x in range(4)]
RIGHT = [(z * 4 + x, z * 4 + (x + 1) % 4) for z in range(2) for x in range(4)]
OPPOSITE = [(z * 4 + x, z * 4 + (x + 2) % 4) for z in range(2) for x in range(4)]
ACROSS = [(z * 4 + x, (1 - z) * 4 + x) for z in range(2) for x in range(4)]


def dp_pairs(move):
    pairs = []
    for y in range(4):
        for h in range(2):
            for c in range(2):
                y2, h2, c2 = move(y, h, c)
                pairs.append((y * 4 + h * 2 + c, (y2 % 4) * 4 + h2 * 2 + c2))
    return pairs


CORE = dp_pairs(lambda y, h, c: (y, h, 1 - c))
HIGH = dp_pairs(lambda y, h, c: (y, 1 - h, c))
UP = dp_pairs(lambda y, h, c: (y + 1, h, c))
DOWN = dp_pairs(lambda y, h, c: (y - 1, h, c))
FAR = dp_pairs(lambda y, h, c: (y + 2, h, c))
LEVELS = [[y * 4 + h * 2 + c for y in range(4) for c in range(2)] for h in range(2)]
BLOCKS = [y * 4 + h * 2 + c for y in range(4) for c in range(2) for h in range(2)]


def left(v):
    return lax.ppermute(v, "tensor", LEFT)


def right(v):
    return lax.ppermute(v, "tensor", RIGHT)


def across(v):
    return lax.ppermute(v, "tensor", ACROSS)


def opposite(v):
    return lax.ppermute(v, "tensor", OPPOSITE)


def pair_gather_first(own):
    return {
        (0, 0): own,
        (0, 2): opposite(own),
        (0, 1): left(own),
        (0, -1): right(own),
        (1, 0): across(own),
    }


def pair_gather_second(got):
    new = {(1, 1): left(got[1, 0]), (1, -1): right(got[1, 0]), (1, 2): across(got[0, 2])}
    return {**got, **new}


def gather_first(own):
    return {(0, 0): own, (0, 1): left(own), (0, -1): right(own), (1, 0): across(own)}


def gather_second(got):
    new = {(0, 2): right(got[0, -1]), (1, 1): left(got[1, 0]), (1, -1): across(got[0, -1])}
    return {**got, **new}


def gather_third(got):
    half = got[0, 0].shape[0] // 2
    return {**got, (1, 2): [right(got[1, -1][:half]), left(got[1, 1][half:])]}


def listed(got, order):
    blocks = []
    for rel in order:
        blocks += got[rel] if rel == (1, 2) else [got[rel]]
    return blocks


def fence(*values):
    return lax.optimization_barrier(values)


def plus(*terms):
    total = terms[0].astype(jnp.float32)
    for term in terms[1:]:
        total = total + term.astype(jnp.float32)
    return total.astype(terms[0].dtype)


def pair_scatter_first(part):
    return left(part[1, -1]), right(part[1, 1]), across(part[1, 2])


def pair_scatter_second(sums, part):
    from_right, from_left, from_across = sums
    return (
        across(plus(part[1, 0], from_right, from_left)),
        opposite(plus(part[0, 2], from_across)),
    )


def scatter_total(part, ends):
    return sum(
        (end.astype(jnp.float32) for end in jax.tree.leaves(ends)), part[0, 0].astype(jnp.float32)
    )


def dp_order():
    index = lax.axis_index("dp")
    y, h, c = index // 4, (index // 2) % 2, index % 2
    return jnp.stack(
        [
            ((y + step) % 4) * 4 + (h ^ high) * 2 + (c ^ core)
            for core in range(2)
            for step in range(4)
            for high in range(2)
        ]
    ).astype(jnp.int32)


def dp_second(mine):
    return (
        mine[0:2],
        lax.ppermute(mine[2:4], "dp", UP),
        lax.ppermute(mine[6:8], "dp", DOWN),
        lax.ppermute(mine[4:6], "dp", FAR),
    )


def dp_third(terms):
    column = plus(*terms)
    return plus(column[0], lax.ppermute(column[1], "dp", HIGH))


def level_scatter_sum(whole):
    return lax.psum_scatter(
        whole, "dp", scatter_dimension=0, tiled=True, axis_index_groups=LEVELS
    )


def high_sum(pair):
    high = (lax.axis_index("dp") // 2) % 2
    give = lax.dynamic_index_in_dim(pair, 1 - high, 0, keepdims=False)
    keep = lax.dynamic_index_in_dim(pair, high, 0, keepdims=False)
    return plus(keep, lax.ppermute(give, "dp", HIGH))


def rope_tables(places):
    halfwidth = ROPE // 2
    frequency = jnp.exp(-jnp.log(10000.0) * (2.0 * jnp.arange(halfwidth, dtype=jnp.float32) / ROPE))
    angles = places.astype(jnp.float32)[:, None] * frequency[None, :]
    return (jnp.cos(angles), jnp.sin(angles))


def normalize(values, gain):
    factor = lax.rsqrt(jnp.mean(values * values, -1, keepdims=True) + EPSILON)
    scaled = values * factor
    return (scaled * gain, scaled, factor)


def norm_backward(grads_in, scaled, factor, gain):
    weighted = grads_in * gain
    centre = jnp.mean(weighted * scaled, -1, keepdims=True)
    return (factor * (weighted - scaled * centre), jnp.sum(grads_in * scaled, 0))


def contract_rows(first, second):
    return lax.dot_general(
        first, second, (((0,), (0,)), ((), ())), preferred_element_type=jnp.float32
    )


def contract_last(first, second):
    return lax.dot_general(
        first, second, (((1,), (1,)), ((), ())), preferred_element_type=jnp.float32
    )


def matmul(first, second):
    return jnp.dot(first, second, preferred_element_type=jnp.float32)


def widen(array, width):
    return jnp.pad(array, ((0, 0), (0, width - array.shape[1])))


CHUNK = 256


def grant(mebibytes):
    return pltpu.CompilerParams(vmem_limit_bytes=mebibytes * 2**20)


def join_refs(refs, out, width):
    at = 0
    for ref in refs:
        rows = ref.shape[0]
        out[at : at + rows, :] = ref[:, :width]
        at += rows


def split_refs(value, refs, at):
    for ref in refs:
        rows = ref.shape[0]
        ref[...] = value[at : at + rows].astype(ref.dtype)
        at += rows


def swap_halves(value):
    lanes = value.shape[1]
    lane = lax.broadcasted_iota(jnp.int32, value.shape, 1) % ROPE
    return jnp.where(
        lane < ROPE // 2, pltpu.roll(value, lanes - ROPE // 2, 1), pltpu.roll(value, ROPE // 2, 1)
    )


def loads(pairs, sems):
    copies = [
        pltpu.make_async_copy(source, target, sems.at[at]) for at, (source, target) in enumerate(pairs)
    ]
    for copy in copies:
        copy.start()
    return copies


def attention_kernel(heads, rank, place, *refs):
    blocks, refs = refs[:8], refs[8:]
    gain, latent_gain, cosine, sine, query_far, down_far, up_far, out_far = refs[:8]
    logsums, factors = refs[8:10]
    far_outs, refs = refs[10:25], refs[25:]
    query_w, down_t, up_w, out_w = refs[:4]
    normed, queries, keys, values, scaled, compressed, attended, branch = refs[4:12]
    latent, raw, pair, turned, load_sems, store_sems = refs[12:]
    normed_far, queries_far, keys_far, values_far, scaled_far, compressed_far, attended_far = far_outs[:7]
    f32, bf16 = jnp.float32, jnp.bfloat16
    seq_len, width = normed.shape
    rows = seq_len // 8
    half = seq_len // 2
    scale = (NOPE + ROPE) ** (-0.5)

    weights = loads(
        [(down_far, down_t), (query_far, query_w), (up_far, up_w), (out_far, out_w)], load_sems
    )
    stores = []

    def store(source, target):
        copy = pltpu.make_async_copy(source, target, store_sems.at[len(stores)])
        copy.start()
        stores.append(copy)

    def slot_rows(slot):
        return pl.ds(pl.multiple_of(place[slot] * rows, rows), rows)

    join_refs(blocks, normed, width)

    def norm_rows(step, carry):
        at = pl.ds(pl.multiple_of(step * rows, rows), rows)
        value = normed[at, :].astype(f32)
        factor = lax.rsqrt(jnp.mean(value * value, 1, keepdims=True) + EPSILON)
        normed[at, :] = (value * factor * gain[...]).astype(bf16)
        return carry

    lax.fori_loop(0, 8, norm_rows, 0)
    store(normed, normed_far)
    weights[0].wait()
    latent[:, : rank + ROPE] = contract_last(normed[...], down_t[...])
    weights[1].wait()
    raw[...] = matmul(normed[...], query_w[...])

    def project_rows(step, carry):
        at = pl.ds(pl.multiple_of(step * rows, rows), rows)
        own = slot_rows(step)
        cos, sin = cosine[own, :], sine[own, :]
        value = latent[at, :rank]
        factor = lax.rsqrt(jnp.mean(value * value, 1, keepdims=True) + EPSILON)
        factors[at, :] = factor
        scaled[at, :] = value * factor
        compressed[at, :] = (value * factor * latent_gain[...]).astype(bf16)
        left_half = lax.broadcasted_iota(jnp.int32, (rows, NOPE), 1) < ROPE
        key_rope = latent[at, rank:]
        key_rope = jnp.where(left_half, key_rope, pltpu.roll(key_rope, ROPE, 1))
        key_rope = (key_rope * cos + swap_halves(key_rope) * sin).astype(bf16)
        one, two = raw[at, NOPE : 2 * NOPE], raw[at, 2 * NOPE :]
        plain = raw[at, :NOPE], jnp.where(left_half, pltpu.roll(one, ROPE, 1), pltpu.roll(two, ROPE, 1))
        query_rope = jnp.where(left_half, one, two)
        query_rope = query_rope * cos + swap_halves(query_rope) * sin
        for head in range(heads):
            queries[head, own, :NOPE] = plain[head].astype(bf16)
            queries[head, own, NOPE:] = jnp.where(left_half == (head == 0), query_rope, 0.0).astype(bf16)
            keys[head, own, NOPE:] = key_rope
        return carry

    lax.fori_loop(0, 8, project_rows, 0)
    store(scaled, scaled_far)
    store(compressed, compressed_far)
    store(queries, queries_far)
    weights[2].wait()
    raw_wide = (NOPE + VDIM) * heads
    pair[:, :raw_wide] = matmul(compressed[:half], up_w[...])
    pair[:, raw_wide : 2 * raw_wide] = matmul(compressed[half:], up_w[...])
    for slot in range(8):
        own = slot_rows(slot)
        at = slice(slot % 4 * rows, (slot % 4 + 1) * rows)
        for head in range(heads):
            start = slot // 4 * raw_wide + head * (NOPE + VDIM)
            keys[head, own, :NOPE] = pair[at, start : start + NOPE].astype(bf16)
            values[head, own, :] = pair[at, start + NOPE : start + NOPE + VDIM].astype(bf16)
    store(keys, keys_far)
    store(values, values_far)

    for step in range(4):
        at = slice(step * 2 * rows, (step + 1) * 2 * rows)
        stop = (step + 1) * 2 * rows
        row = lax.broadcasted_iota(jnp.int32, (2 * rows, stop), 0) + step * 2 * rows
        allowed = lax.broadcasted_iota(jnp.int32, (2 * rows, stop), 1) <= row
        for head in range(heads):
            scores = contract_last(queries[head, at, :], keys[head, :stop, :]) * scale
            scores = jnp.where(allowed, scores, -1e30)
            highest = jnp.max(scores, 1, keepdims=True)
            weight = jnp.exp(scores - highest)
            denominator = jnp.sum(weight, 1, keepdims=True)
            logsums[head, at, :] = highest + jnp.log(denominator)
            shares = (weight * (1.0 / denominator)).astype(bf16)
            turned[at, head * VDIM : (head + 1) * VDIM] = matmul(shares, values[head, :stop, :]).astype(bf16)
    for slot in range(8):
        attended[slot * rows : (slot + 1) * rows, :] = turned[slot_rows(slot), :]
    store(attended, attended_far)
    weights[3].wait()
    for order in (1, 0):
        at = slice(order * half, (order + 1) * half)
        branch[at, :] = contract_last(attended[at, :], out_w[...]).astype(bf16)
        for slot in range(4 * order, 4 * order + 4):
            store(branch.at[slot * rows : (slot + 1) * rows, :], far_outs[7 + slot])
    for copy in stores:
        copy.wait()


def attention(place, blocks, gain, query_w, down_t, latent_gain, up_w, out_w, cosine, sine):
    rows = blocks[0].shape[0]
    seq_len, width = rows * 8, blocks[0].shape[1]
    rank = up_w.shape[0]
    heads = up_w.shape[1] // (NOPE + VDIM)
    f32, bf16 = jnp.float32, jnp.bfloat16
    shape = jax.ShapeDtypeStruct
    vmem, far = pl.BlockSpec(memory_space=pltpu.VMEM), pl.BlockSpec(memory_space=pl.ANY)
    kept = [
        shape((seq_len, width), bf16),
        shape((heads, seq_len, 2 * NOPE), bf16),
        shape((heads, seq_len, 2 * NOPE), bf16),
        shape((heads, seq_len, VDIM), bf16),
        shape((seq_len, rank), f32),
        shape((seq_len, rank), bf16),
        shape((seq_len, heads * VDIM), bf16),
    ]
    weights = [query_w, down_t, up_w, out_w]
    return pl.pallas_call(
        functools.partial(attention_kernel, heads, rank),
        in_specs=[pl.BlockSpec(memory_space=pltpu.SMEM)] + [vmem] * 12 + [far] * 4,
        out_specs=[vmem] * 2 + [far] * 15,
        out_shape=[shape((heads, seq_len, 1), f32), shape((seq_len, 1), f32)]
        + kept
        + [shape((rows, width), bf16)] * 8,
        scratch_shapes=[pltpu.VMEM(a.shape, a.dtype) for a in weights + kept]
        + [
            pltpu.VMEM((seq_len, width), bf16),
            pltpu.VMEM((seq_len, rank + NOPE), f32),
            pltpu.VMEM((seq_len, query_w.shape[1]), f32),
            pltpu.VMEM((seq_len // 2, 2 * heads * (NOPE + VDIM)), f32),
            pltpu.VMEM((seq_len, heads * VDIM), bf16),
            pltpu.SemaphoreType.DMA((4,)),
            pltpu.SemaphoreType.DMA((15,)),
        ],
        compiler_params=grant(56),
        cost_estimate=pl.CostEstimate(
            flops=20 * seq_len * width * width // 4, bytes_accessed=30 * 2**20, transcendentals=0
        ),
        name="attention",
    )(place, *blocks, gain, latent_gain, cosine, sine, *weights)


def attention_grad_kernel(heads, place, *refs):
    blocks, refs = refs[:8], refs[8:]
    out_w, cosine, sine, logsums, queries_far, keys_far, values_far = refs[:7]
    branch_far, query_grads, kv_grads, rope_grads = refs[7:11]
    queries, keys, values, branch_grads = refs[11:15]
    out_grads, key_grads, value_grads, turned, load_sems, store_sem = refs[15:]
    f32, bf16 = jnp.float32, jnp.bfloat16
    seq_len, width = branch_grads.shape
    rows = seq_len // 8
    scale = (NOPE + ROPE) ** (-0.5)

    arrays = loads([(queries_far, queries), (keys_far, keys), (values_far, values)], load_sems)
    join_refs(blocks, branch_grads, width)
    (stored,) = loads([(branch_grads, branch_far)], store_sem)

    def slot_rows(slot):
        return pl.ds(pl.multiple_of(place[slot] * rows, rows), rows)

    grads = matmul(branch_grads[...], out_w[...]).astype(bf16)
    for slot in range(8):
        out_grads[slot_rows(slot), :] = grads[slot * rows : (slot + 1) * rows, :]
    key_grads[...] = jnp.zeros_like(key_grads)
    value_grads[...] = jnp.zeros_like(value_grads)
    for array in arrays:
        array.wait()

    left_half = lax.broadcasted_iota(jnp.int32, (2 * rows, NOPE), 1) < ROPE
    for step in range(4):
        at = slice(step * 2 * rows, (step + 1) * 2 * rows)
        stop = (step + 1) * 2 * rows
        row = lax.broadcasted_iota(jnp.int32, (2 * rows, stop), 0) + step * 2 * rows
        allowed = lax.broadcasted_iota(jnp.int32, (2 * rows, stop), 1) <= row
        plain, ropes = [], []
        for head in range(heads):
            query, key = queries[head, at, :], keys[head, :stop, :]
            out_grad = out_grads[at, head * VDIM : (head + 1) * VDIM]
            scores = contract_last(query, key) * scale
            shares = jnp.where(allowed, jnp.exp(scores - logsums[head, at, :]), 0.0)
            share_grads = contract_last(out_grad, values[head, :stop, :])
            centre = jnp.sum(shares * share_grads, 1, keepdims=True)
            score_grads = (shares * (share_grads - centre)).astype(bf16)
            value_grads[head, :stop, :] += contract_rows(shares.astype(bf16), out_grad)
            key_grads[head, :stop, :] += contract_rows(score_grads, query)
            query_grad = matmul(score_grads, key) * scale
            plain.append(query_grad[:, :NOPE])
            ropes.append(query_grad[:, NOPE:])
        rope = jnp.where(left_half, ropes[0], ropes[1])
        rope = rope * cosine[at, :] - swap_halves(rope) * sine[at, :]
        moved = pltpu.roll(plain[1], ROPE, 1)
        turned[at, :NOPE] = plain[0].astype(bf16)
        turned[at, NOPE : 2 * NOPE] = jnp.where(left_half, rope, moved).astype(bf16)
        turned[at, 2 * NOPE :] = jnp.where(left_half, moved, rope).astype(bf16)

    for slot in range(8):
        own, at = slot_rows(slot), slice(slot * rows, (slot + 1) * rows)
        query_grads[at, :] = turned[own, :]
        for head in range(heads):
            start = head * (NOPE + VDIM)
            kv_grads[at, start : start + NOPE] = (key_grads[head, own, :NOPE] * scale).astype(bf16)
            kv_grads[at, start + NOPE : start + NOPE + VDIM] = value_grads[head, own, :].astype(bf16)
        rope = sum(key_grads[head, own, NOPE:] for head in range(heads)) * scale
        rope = rope + pltpu.roll(rope, ROPE, 1)
        rope = rope * cosine[own, :] - swap_halves(rope) * sine[own, :]
        lane = lax.broadcasted_iota(jnp.int32, rope.shape, 1)
        rope_grads[at, :] = jnp.where(lane < ROPE, rope, 0.0).astype(bf16)
    stored.wait()


def attention_grad(place, blocks, out_w, cosine, sine, queries, keys, values, logsums):
    seq_len, width = queries.shape[1], blocks[0].shape[1]
    heads = queries.shape[0]
    f32, bf16 = jnp.float32, jnp.bfloat16
    shape = jax.ShapeDtypeStruct
    vmem, far = pl.BlockSpec(memory_space=pltpu.VMEM), pl.BlockSpec(memory_space=pl.ANY)
    return pl.pallas_call(
        functools.partial(attention_grad_kernel, heads),
        in_specs=[pl.BlockSpec(memory_space=pltpu.SMEM)] + [vmem] * 12 + [far] * 3,
        out_specs=[far] + [vmem] * 3,
        out_shape=[
            shape((seq_len, width), bf16),
            shape((seq_len, heads * (NOPE + ROPE)), bf16),
            shape((seq_len, heads * (NOPE + VDIM)), bf16),
            shape((seq_len, NOPE), bf16),
        ],
        scratch_shapes=[pltpu.VMEM(a.shape, a.dtype) for a in (queries, keys, values)]
        + [
            pltpu.VMEM((seq_len, width), bf16),
            pltpu.VMEM((seq_len, heads * VDIM), bf16),
            pltpu.VMEM((heads, seq_len, 2 * NOPE), f32),
            pltpu.VMEM((heads, seq_len, VDIM), f32),
            pltpu.VMEM((seq_len, heads * (NOPE + ROPE)), bf16),
            pltpu.SemaphoreType.DMA((3,)),
            pltpu.SemaphoreType.DMA((1,)),
        ],
        compiler_params=grant(56),
        cost_estimate=pl.CostEstimate(
            flops=8 * seq_len * width * width // 4, bytes_accessed=20 * 2**20, transcendentals=0
        ),
        name="attention_grad",
    )(place, *blocks, out_w, cosine, sine, logsums, queries, keys, values)


def input_kernel(rank, *refs):
    query_grads, kv_grads, rope_grads, gain, latent_gain, up_w, factors = refs[:7]
    query_far, down_far, normed_far, scaled_far = refs[7:11]
    lhs, input_gain, latent_gains = refs[11:14]
    parts_far = refs[14:22]
    query_w, down_t, normed, scaled, pair, parts, load_sems, store_sems = refs[22:]
    f32, bf16 = jnp.float32, jnp.bfloat16
    seq_len, width = normed.shape
    rows = seq_len // 8
    arrays = loads(
        [(scaled_far, scaled), (query_far, query_w), (down_far, down_t), (normed_far, normed)], load_sems
    )
    lhs[:, rank:] = rope_grads[...]
    latent_gains[...] = jnp.zeros_like(latent_gains)
    arrays[0].wait()

    def latent_rows(step, carry):
        at = pl.ds(pl.multiple_of(step * 4 * rows, 4 * rows), 4 * rows)
        back = contract_last(kv_grads[at, :], up_w[...])
        value = scaled[at, :]
        latent_gains[...] += jnp.sum(back * value, 0, keepdims=True)
        weighted = back * latent_gain[...]
        centre = jnp.mean(weighted * value, 1, keepdims=True)
        lhs[at, :rank] = (factors[at, :] * (weighted - value * centre)).astype(bf16)
        return carry

    lax.fori_loop(0, 2, latent_rows, 0)
    input_gain[...] = jnp.zeros_like(input_gain)
    half = seq_len // 2
    stores = []
    for order in (1, 0):
        start = order * half
        at = slice(start, start + half)
        if order:
            arrays[1].wait()
            arrays[2].wait()
        pair[...] = contract_last(query_grads[at, :], query_w[...]) + matmul(lhs[at, : rank + ROPE], down_t[...])
        if order:
            arrays[3].wait()
        for step in range(4):
            spot = slice(step * rows, (step + 1) * rows)
            block = pair[spot, :]
            slot = 4 * order + step
            parts[slot] = block.astype(bf16)
            copy = pltpu.make_async_copy(parts.at[slot], parts_far[slot], store_sems.at[slot])
            copy.start()
            stores.append(copy)
            input_gain[...] += jnp.sum(
                block * normed[start + step * rows : start + (step + 1) * rows, :].astype(f32),
                0,
                keepdims=True,
            )
    input_gain[...] = input_gain[...] / gain[...]
    for copy in stores:
        copy.wait()


def input_grads(query_grads, kv_grads, rope_grads, gain, query_w, down_t, latent_gain, up_w, normed, scaled, factors):
    seq_len, width = normed.shape
    rank = up_w.shape[0]
    f32, bf16 = jnp.float32, jnp.bfloat16
    shape = jax.ShapeDtypeStruct
    vmem, far = pl.BlockSpec(memory_space=pltpu.VMEM), pl.BlockSpec(memory_space=pl.ANY)
    arrays = [query_w, down_t, normed, scaled]
    return pl.pallas_call(
        functools.partial(input_kernel, rank),
        in_specs=[vmem] * 7 + [far] * 4,
        out_specs=[vmem] * 3 + [far] * 8,
        out_shape=[
            shape((seq_len, rank + NOPE), bf16),
            shape((1, width), f32),
            shape((1, rank), f32),
        ]
        + [shape((seq_len // 8, width), bf16)] * 8,
        scratch_shapes=[pltpu.VMEM(a.shape, a.dtype) for a in arrays]
        + [
            pltpu.VMEM((seq_len // 2, width), f32),
            pltpu.VMEM((8, seq_len // 8, width), bf16),
            pltpu.SemaphoreType.DMA((4,)),
            pltpu.SemaphoreType.DMA((8,)),
        ],
        compiler_params=grant(56),
        cost_estimate=pl.CostEstimate(
            flops=6 * seq_len * width * width // 4, bytes_accessed=20 * 2**20, transcendentals=0
        ),
        name="input_grads",
    )(query_grads, kv_grads, rope_grads, gain, latent_gain, up_w, factors, *arrays)


def forward_kernel(blocks, expert_units, *refs):
    hid_blocks, cot_blocks, refs = refs[:blocks], refs[blocks : blocks + 4], refs[blocks + 4 :]
    own, router, gate_w, up_w, down_w, scaled, gate_g, up_g, logit_g, hid, cot, probs, gate, chosen, total = refs
    j = pl.program_id(0)
    width = hid.shape[1]
    experts = own.shape[1]

    @pl.when(j == 0)
    def _():
        join_refs(hid_blocks, hid, width)
        join_refs(cot_blocks, cot, width)
        for slot, ref in enumerate(cot_blocks):
            rows = ref.shape[0]
            mask = ref[:, width : width + experts].astype(jnp.float32)
            chosen[slot * rows : (slot + 1) * rows, :] = jnp.sum(mask * own[...], 1, keepdims=True)
        logits = matmul(hid[...], router[...])
        powers = jnp.exp(logits - jnp.max(logits, 1, keepdims=True))
        probs[...] = powers / jnp.sum(powers, 1, keepdims=True)
        gate[...] = jnp.sum(probs[...] * own[...], 1, keepdims=True) * chosen[...]
        total[...] = jnp.zeros_like(total)

    column = j * gate_w.shape[1] + lax.broadcasted_iota(jnp.int32, (1, gate_w.shape[1]), 1)
    is_expert = column < expert_units
    pre_gate = matmul(hid[...], gate_w[...])
    pre_up = matmul(hid[...], up_w[...])
    back = matmul(cot[...], down_w[...])
    sigmoid = 1.0 / (1.0 + jnp.exp(-pre_gate))
    act = pre_gate * sigmoid
    slope = sigmoid * (1.0 + pre_gate * (1.0 - sigmoid))
    hidden = act * pre_up
    scale = jnp.where(is_expert, gate[...], 1.0)
    scaled[...] = (hidden * scale).astype(scaled.dtype)
    total[...] += jnp.sum(jnp.where(is_expert, hidden * back, 0.0), 1, keepdims=True)
    back = back * scale
    gate_g[...] = (back * pre_up * slope).astype(gate_g.dtype)
    up_g[...] = (back * act).astype(up_g.dtype)

    @pl.when(j == pl.num_programs(0) - 1)
    def _():
        own_prob = jnp.sum(probs[...] * own[...], 1, keepdims=True)
        logit_g[...] = (total[...] * chosen[...] * probs[...] * (own[...] - own_prob)).astype(logit_g.dtype)


def feed_forward(hid, cot, own, router, gate_w, up_w, weight_out, expert_units):
    rows, width = sum(block.shape[0] for block in hid), hid[0].shape[1]
    units = weight_out.shape[1]
    steps = units // CHUNK
    experts = own.shape[1]
    out = pl.BlockSpec((rows, CHUNK), lambda j: (0, j))
    whole = pl.BlockSpec(memory_space=pltpu.VMEM)
    wide = jax.ShapeDtypeStruct((rows, units), jnp.bfloat16)
    joined = jax.ShapeDtypeStruct((rows, width), jnp.bfloat16)
    column = pltpu.VMEM((rows, 1), jnp.float32)
    return pl.pallas_call(
        functools.partial(forward_kernel, len(hid), expert_units),
        grid=(steps,),
        in_specs=[whole] * (len(hid) + 6)
        + [
            pl.BlockSpec((width, CHUNK), lambda j: (0, j)),
            pl.BlockSpec((width, CHUNK), lambda j: (0, j)),
            pl.BlockSpec((width, CHUNK), lambda j: (0, j)),
        ],
        out_specs=[out, out, out, whole, whole, whole],
        out_shape=[wide, wide, wide, jax.ShapeDtypeStruct((rows, experts), jnp.bfloat16), joined, joined],
        scratch_shapes=[pltpu.VMEM((rows, experts), jnp.float32), column, column, column],
        compiler_params=grant(56),
        cost_estimate=pl.CostEstimate(
            flops=6 * rows * width * units, bytes_accessed=6 * width * units, transcendentals=rows * units
        ),
        name="feed_forward",
    )(*hid, *cot, own, router, gate_w, up_w, weight_out)


def input_grad_kernel(gate_g, up_g, logit_g, gate_w, up_w, router, *outs):
    total = contract_last(gate_g[...], gate_w[...]) + contract_last(up_g[...], up_w[...])
    split_refs(total + contract_last(logit_g[...], router[...]), outs, 0)


def input_grad(gate_g, up_g, logit_g, gate_w, up_w, router):
    rows, units = gate_g.shape
    sizes = [rows // 4] * 4
    width, experts = router.shape
    part = min(512, width)
    whole = pl.BlockSpec(memory_space=pltpu.VMEM)
    return pl.pallas_call(
        input_grad_kernel,
        grid=(width // part,),
        in_specs=[
            whole,
            whole,
            whole,
            pl.BlockSpec((part, units), lambda j: (j, 0)),
            pl.BlockSpec((part, units), lambda j: (j, 0)),
            pl.BlockSpec((part, experts), lambda j: (j, 0)),
        ],
        out_specs=[pl.BlockSpec((size, part), lambda j: (0, j)) for size in sizes],
        out_shape=[jax.ShapeDtypeStruct((size, width), jnp.bfloat16) for size in sizes],
        compiler_params=grant(56),
        cost_estimate=pl.CostEstimate(
            flops=4 * rows * width * units, bytes_accessed=4 * width * units, transcendentals=0
        ),
        name="input_grad",
    )(gate_g, up_g, logit_g, gate_w, up_w, router)


def output_kernel(first, second, down_w, *outs):
    scaled = jnp.concatenate([first[...], second[...]], 0)
    split_refs(contract_last(scaled, down_w[...]), outs, 0)


def mixer_output(scaled, weight_out):
    rows, units = scaled[0].shape
    sizes = [rows // 4] * 8
    width = weight_out.shape[0]
    part = min(512, width)
    return pl.pallas_call(
        output_kernel,
        grid=(width // part,),
        in_specs=[
            pl.BlockSpec(memory_space=pltpu.VMEM),
            pl.BlockSpec(memory_space=pltpu.VMEM),
            pl.BlockSpec((part, units), lambda j: (j, 0)),
        ],
        out_specs=[pl.BlockSpec((size, part), lambda j: (0, j)) for size in sizes],
        out_shape=[jax.ShapeDtypeStruct((size, width), jnp.bfloat16) for size in sizes],
        compiler_params=grant(56),
        cost_estimate=pl.CostEstimate(
            flops=4 * rows * width * units, bytes_accessed=2 * width * units, transcendentals=0
        ),
        name="mixer_output",
    )(*scaled, weight_out)


def store_blocks(out, product, at=0):
    rows = product.shape[0]
    lanes = out.shape[2]
    for slot, block in enumerate(BLOCKS):
        out[slot, at : at + rows, :] = product[:, block * lanes : (block + 1) * lanes].astype(out.dtype)


def mixer_weight_kernel(la, lb, ra, rb, *refs):
    store_blocks(refs[-1], contract_rows(la[...], ra[...]) + contract_rows(lb[...], rb[...]))


def mixer_weights(order, parts, lhs, rhs, kept=None):
    rows, units = lhs[0].shape
    width = rhs[0].shape[1]
    steps = units // CHUNK
    part = pl.BlockSpec((rows, CHUNK), lambda j: (0, j))
    whole = pl.BlockSpec(memory_space=pltpu.VMEM)
    kept = [] if kept is None else [kept]
    return pl.pallas_call(
        mixer_weight_kernel,
        grid=(steps,),
        in_specs=[part, part, whole, whole] + [pl.BlockSpec(memory_space=pl.ANY)] * len(kept),
        out_specs=pl.BlockSpec((16, CHUNK, width // 16), lambda j: (0, j + order * steps, 0)),
        out_shape=jax.ShapeDtypeStruct((16, parts * units, width // 16), jnp.bfloat16),
        input_output_aliases={4: 0} if kept else {},
        compiler_params=grant(56),
        cost_estimate=pl.CostEstimate(
            flops=4 * rows * width * units, bytes_accessed=2 * width * units, transcendentals=0
        ),
        name="mixer_weights",
    )(*lhs, *rhs, *kept)


def latent_weight_kernel(spare, order, lhs, normed, router, input_gain, mixer_gain, latent_gain, mine, other, wide):
    lanes = mine.shape[2]
    wide[...] = contract_rows(lhs[...], normed[...])
    at = spare + router.shape[0]
    wide[spare:at, :] = router[...]
    wide[at : at + 1, :] = input_gain[...]
    wide[at + 1 : at + 2, :] = mixer_gain[...]
    rank, width = latent_gain.shape[1], wide.shape[1]
    share = rank // 16
    entry = lax.broadcasted_iota(jnp.int32, (rank, width), 0)
    lane = lax.broadcasted_iota(jnp.int32, (rank, width), 1)
    each = share // 8
    spot = entry // share * lanes + entry % share // each * (lanes // 8) + entry % each
    wide[at + 2 : at + 3, :] = matmul(latent_gain[...], (spot == lane).astype(jnp.float32))
    for slot in range(16):
        at = pl.multiple_of(order[slot] * lanes, lanes)
        block = wide[:, pl.ds(at, lanes)].astype(mine.dtype)
        if slot < 8:
            mine[slot] = block
        else:
            other[slot - 8] = block


def latent_weights(order, lhs, spare, normed, *small):
    rows, columns = lhs.shape
    width = normed.shape[1]
    vmem = pl.BlockSpec(memory_space=pltpu.VMEM)
    return pl.pallas_call(
        functools.partial(latent_weight_kernel, spare),
        in_specs=[pl.BlockSpec(memory_space=pltpu.SMEM)] + [vmem] * 6,
        out_specs=[vmem] * 2,
        out_shape=[jax.ShapeDtypeStruct((8, columns, width // 16), jnp.bfloat16)] * 2,
        scratch_shapes=[pltpu.VMEM((columns, width), jnp.float32)],
        compiler_params=grant(56),
        cost_estimate=pl.CostEstimate(
            flops=2 * rows * width * columns, bytes_accessed=4 * width * columns, transcendentals=0
        ),
        name="latent_weights",
    )(order, lhs, normed, *small)


def head_weight_kernel(query_grads, normed, attended, branch_grads, compressed, kv_grads, out):
    store_blocks(out, contract_rows(query_grads[...], normed[...]))
    at = query_grads.shape[1]
    store_blocks(out, contract_rows(attended[...], branch_grads[...]), at)
    at += attended.shape[1]
    lanes = out.shape[2]
    product = contract_rows(compressed[...], kv_grads[...]).astype(out.dtype)
    share = product.shape[0] // 16
    for slot, block in enumerate(BLOCKS):
        for step in range(product.shape[1] // lanes):
            start = at + step * share
            out[slot, start : start + share, :] = product[
                block * share : (block + 1) * share, step * lanes : (step + 1) * lanes
            ]


def head_weights(query_grads, normed, attended, branch_grads, compressed, kv_grads):
    rows, width = normed.shape
    lanes = width // 16
    total = query_grads.shape[1] + attended.shape[1]
    total += compressed.shape[1] // 16 * kv_grads.shape[1] // lanes
    vmem = pl.BlockSpec(memory_space=pltpu.VMEM)
    return pl.pallas_call(
        head_weight_kernel,
        in_specs=[vmem] * 6,
        out_specs=vmem,
        out_shape=jax.ShapeDtypeStruct((16, total, lanes), jnp.bfloat16),
        compiler_params=grant(56),
        cost_estimate=pl.CostEstimate(
            flops=2 * rows * width * total, bytes_accessed=4 * width * rows, transcendentals=0
        ),
        name="head_weights",
    )(query_grads, normed, attended, branch_grads, compressed, kv_grads)


def latent_finish_kernel(late, rest):
    rest[...] = late[...].astype(jnp.float32).T.astype(rest.dtype)


def latent_finish(late):
    return pl.pallas_call(
        latent_finish_kernel,
        out_shape=jax.ShapeDtypeStruct(late.shape[::-1], late.dtype),
        compiler_params=grant(8),
        name="latent_finish",
    )(late)


def head_finish_kernel(query_wide, late, query, output, up):
    query[...] = late[:query_wide, :].astype(jnp.float32).T
    at = query_wide + output.shape[1]
    output[...] = late[query_wide:at, :].astype(jnp.float32).T
    lanes, share = late.shape[1], up.shape[0]
    for step in range(up.shape[1] // lanes):
        start = at + step * share
        up[:, step * lanes : (step + 1) * lanes] = late[start : start + share, :].astype(jnp.float32)


def head_finish(late, query_wide, value_wide, up_shape):
    lanes = late.shape[1]
    f32 = jnp.float32
    return pl.pallas_call(
        functools.partial(head_finish_kernel, query_wide),
        out_shape=[
            jax.ShapeDtypeStruct((lanes, query_wide), f32),
            jax.ShapeDtypeStruct((lanes, value_wide), f32),
            jax.ShapeDtypeStruct(up_shape, f32),
        ],
        compiler_params=grant(8),
        name="head_finish",
    )(late)


def mixer_finish_kernel(expert_units, shared_units, gate, other, *outs):
    units = gate.shape[0]
    for order, (totals, start) in enumerate(((gate, 0), (other, 0), (other, units))):
        expert = totals[start : start + expert_units, :].astype(jnp.float32)
        outs[order][:, 0, :] = expert.T
        start += expert_units
        outs[3 + order][...] = totals[start : start + shared_units, :].astype(jnp.float32)


def mixer_finish(gate, other, expert_units, shared_units):
    lanes = gate.shape[1]
    f32 = jnp.float32
    return pl.pallas_call(
        functools.partial(mixer_finish_kernel, expert_units, shared_units),
        out_shape=[jax.ShapeDtypeStruct((lanes, 1, expert_units), f32)] * 3
        + [jax.ShapeDtypeStruct((shared_units, lanes), f32)] * 3,
        compiler_params=grant(16),
        name="mixer_finish",
    )(gate, other)


def on_device(
    tokens,
    expert_index,
    cotangent,
    input_gain,
    query_weight,
    latent_down,
    latent_gain,
    latent_up,
    output_weight,
    mixer_gain,
    router_weight,
    shared_gate,
    shared_up,
    shared_down,
    expert_gate,
    expert_up,
    expert_down,
):
    tok_rows, width = tokens.shape
    group = lax.axis_index("tensor")
    z, x = group // 4, group % 4
    rank = latent_up.shape[0]
    heads_local = query_weight.shape[1] // (NOPE + ROPE)
    experts_all = router_weight.shape[1]
    scale = (NOPE + ROPE) ** (-0.5)
    expert_units = expert_gate.shape[2]
    shared_units = shared_gate.shape[1]
    shared_wide = -(-shared_units // 128) * 128
    units = expert_units + shared_wide
    bf16, f32 = jnp.bfloat16, jnp.float32

    first_order, second_order = ORDER[:4], ORDER[4:]
    seq_len = tok_rows * 8

    cosine, sine = rope_tables(jnp.arange(seq_len, dtype=jnp.int32))
    cosine = jnp.concatenate([cosine] * (2 * NOPE // ROPE), 1)
    sine = jnp.concatenate([-sine, sine] * (NOPE // ROPE), 1)
    chosen = (expert_index[:, :, None] == jnp.arange(experts_all, dtype=jnp.int32)).any(1)
    sent = jnp.concatenate([cotangent, widen(chosen.astype(bf16), 128)], 1)
    shared_gate, shared_up, shared_down = (
        widen(part, shared_wide) for part in (shared_gate, shared_up, shared_down)
    )
    got = pair_gather_first(tokens)
    got, cosine, sine, sent, shared_gate, shared_up, shared_down = fence(
        got, cosine, sine, sent, shared_gate, shared_up, shared_down
    )
    got = pair_gather_second(got)
    weight_out = jnp.concatenate([expert_down.reshape(width, expert_units), shared_down], 1)
    got, weight_out, sent = fence(got, weight_out, sent)

    upstream = pair_gather_first(sent)

    place = jnp.stack([(z ^ dz) * 4 + (x + dx) % 4 for dz, dx in ORDER]).astype(jnp.int32)
    outs = attention(
        place,
        [got[rel] for rel in ORDER],
        input_gain[None],
        query_weight,
        latent_down.T,
        latent_gain[None],
        latent_up,
        output_weight,
        cosine,
        sine,
    )
    logsums, latent_factor, normed_all, queries, keys, values, latent_scaled = outs[:7]
    compressed, attended = outs[7:9]
    part = dict(zip(ORDER, outs[9:]))
    part, upstream = fence(part, upstream)
    sums = pair_scatter_first(part)
    gate_w = jnp.concatenate([expert_gate.reshape(width, expert_units), shared_gate], 1)
    sums, part, gate_w, expert_up, shared_up = fence(sums, part, gate_w, expert_up, shared_up)
    ends = pair_scatter_second(sums, part), left(part[0, -1]), right(part[0, 1])
    up_w = jnp.concatenate([expert_up.reshape(width, expert_units), shared_up], 1)
    ends, up_w = fence(ends, up_w)
    branch = scatter_total(part, ends)

    middle = tokens.astype(f32) + branch
    second_normed, second_scaled, second_factor = normalize(middle, mixer_gain)
    own_expert = (jnp.arange(experts_all) == group).astype(f32)[None, :]

    def feed(got, order):
        return feed_forward(
            listed(got, order),
            [upstream[rel] for rel in order],
            own_expert,
            router_weight,
            gate_w,
            up_w,
            weight_out,
            expert_units,
        )

    def input_part(fed):
        return input_grad(*fed[1:4], gate_w, up_w, router_weight)

    got = gather_second(gather_first(second_normed.astype(bf16)))
    fed_first = feed(got, first_order)
    got, fed_first, upstream = fence(got, fed_first, upstream)
    got, upstream = gather_third(got), pair_gather_second(upstream)
    first_part = input_part(fed_first)
    got, upstream, first_part = fence(got, upstream, first_part)
    fed_second = feed(got, second_order)
    hidden_scaled, gate_grads, up_grads, logit_grads, hidden, upstream = zip(fed_first, fed_second)
    part = dict(zip(second_order, input_part(fed_second)))
    sums = pair_scatter_first(part)
    gate_parts = mixer_weights(0, 1, gate_grads, hidden)
    sums, gate_parts = fence(sums, gate_parts)
    gate_totals = level_scatter_sum(gate_parts)
    part.update(zip(first_order, first_part))
    ends = pair_scatter_second(sums, part), left(part[0, -1]), right(part[0, 1])
    other_parts = mixer_weights(0, 2, up_grads, hidden)
    ends, other_parts = fence(ends, other_parts)
    mixer_back = scatter_total(part, ends)
    middle_from, grad_mixer_gain = norm_backward(
        mixer_back, second_scaled, second_factor, mixer_gain
    )
    middle_grads = cotangent.astype(f32) + middle_from
    got = pair_gather_first(middle_grads.astype(bf16))
    other_parts = mixer_weights(1, 2, hidden_scaled, upstream, other_parts)
    grad_router = sum(contract_rows(g, hid) for g, hid in zip(logit_grads, hidden))
    got, other_parts, grad_router = fence(got, other_parts, grad_router)
    other_totals = level_scatter_sum(other_parts)
    got = pair_gather_second(got)
    out_blocks = mixer_output(hidden_scaled, weight_out)
    got, out_blocks, gate_totals = fence(got, out_blocks, gate_totals)

    out = dict(zip(ORDER, out_blocks))
    out_sums, out_left = pair_scatter_first(out), left(out[0, -1])
    gate_total = high_sum(gate_totals)
    grads = attention_grad(
        place, [got[rel] for rel in ORDER], output_weight, cosine, sine, queries, keys, values, logsums
    )
    out_sums, grads = fence(out_sums, grads)
    branch_all, query_grads, kv_grads, rope_grads = grads
    out_ends, out_right = pair_scatter_second(out_sums, out), right(out[0, 1])
    grads = input_grads(
        query_grads,
        kv_grads,
        rope_grads,
        input_gain[None],
        query_weight,
        latent_down.T,
        latent_gain[None],
        latent_up,
        normed_all,
        latent_scaled,
        latent_factor,
    )
    head_parts = head_weights(query_grads, normed_all, attended, branch_all, compressed, kv_grads)
    out_ends, out_left, out_right, grads, gate_total, head_parts = fence(
        out_ends, out_left, out_right, grads, gate_total, head_parts
    )
    latent_grads, grad_input_gain, grad_latent_gain = grads[:3]
    part = dict(zip(ORDER, grads[3:]))
    sums = pair_scatter_first(part)

    wide = latent_down.shape[1]
    lanes = width // 16
    share = rank // 16
    mine, other = latent_weights(
        dp_order(),
        latent_grads,
        wide,
        normed_all,
        grad_router,
        grad_input_gain,
        grad_mixer_gain[None],
        grad_latent_gain,
    )
    sums, mine, other, head_parts, other_totals = fence(sums, mine, other, head_parts, other_totals)
    head_totals = level_scatter_sum(head_parts)
    ends = pair_scatter_second(sums, part)
    other = lax.ppermute(other, "dp", CORE)
    ends, other = fence(ends, other)
    terms = dp_second(plus(mine, other))
    other_total = high_sum(other_totals)
    last_left = left(part[0, -1])
    terms, other_total, last_left, last = fence(terms, other_total, last_left, part[0, 1])
    last_right = right(last)
    normed_grads = scatter_total(part, (ends, last_left, last_right))
    _, first_scaled, first_factor = normalize(tokens.astype(f32), input_gain)
    input_from, _ = norm_backward(normed_grads, first_scaled, first_factor, input_gain)
    grad_tokens = middle_grads + input_from
    rest = latent_finish(dp_third(terms)).reshape(8, lanes // 8, -1)
    rest = lax.all_to_all(rest, "tensor", 0, 0, tiled=True)
    head_total = high_sum(head_totals)
    layer_out = (middle + scatter_total(out, (out_ends, out_left, out_right))).astype(bf16)
    rest, head_total, layer_out, grad_tokens = fence(rest, head_total, layer_out, grad_tokens)
    rest = jnp.sum(rest.astype(f32), 0)
    at = wide + experts_all
    expert_outs = mixer_finish(gate_total, other_total, expert_units, shared_units)
    total_query, total_output, total_up = head_finish(
        head_total, query_weight.shape[1], attended.shape[1], (share, latent_up.shape[1])
    )
    return (
        layer_out,
        grad_tokens,
        rest[:, at],
        total_query,
        rest[:, :wide],
        rest[: share // 8, at + 2],
        total_up,
        total_output,
        rest[:, at + 1],
        rest[:, wide:at],
        *[shared.T for shared in expert_outs[3:]],
        *expert_outs[:3],
    )


def solution(mesh):
    rows = P(("dp", "tensor"), None)
    columns = P(None, "tensor")
    middle = P(None, "tensor", None)
    return jax.shard_map(
        on_device,
        mesh=mesh,
        in_specs=(rows, rows, rows, P(), columns, P(), P(), columns, columns, P(), P())
        + (columns,) * 3
        + (middle,) * 3,
        out_specs=(
            rows,
            rows,
            P(("dp", "tensor")),
            P("dp", "tensor"),
            rows,
            P(("dp", "tensor")),
            P("dp", "tensor"),
            P("dp", "tensor"),
            P(("dp", "tensor")),
            rows,
        )
        + (P("dp", "tensor"),) * 3
        + (P("dp", "tensor", None),) * 3,
        check_vma=False,
    )
```

```python
import functools

import jax
import jax.numpy as jnp
from jax import lax
from jax.experimental import pallas as pl
from jax.experimental.pallas import tpu as pltpu
from jax.sharding import PartitionSpec as P

NOPE = 128
ROPE = 64
VDIM = 128
EPSILON = 1e-06

ORDER = ((0, 0), (0, -1), (0, 1), (1, 0), (0, 2), (1, 1), (1, -1), (1, 2))
SLOT = {rel: slot for slot, rel in enumerate(ORDER)}

LEFT = [(z * 4 + x, z * 4 + (x - 1) % 4) for z in range(2) for x in range(4)]
RIGHT = [(z * 4 + x, z * 4 + (x + 1) % 4) for z in range(2) for x in range(4)]
OPPOSITE = [(z * 4 + x, z * 4 + (x + 2) % 4) for z in range(2) for x in range(4)]
ACROSS = [(z * 4 + x, (1 - z) * 4 + x) for z in range(2) for x in range(4)]


def dp_pairs(move):
    pairs = []
    for y in range(4):
        for h in range(2):
            for c in range(2):
                y2, h2, c2 = move(y, h, c)
                pairs.append((y * 4 + h * 2 + c, (y2 % 4) * 4 + h2 * 2 + c2))
    return pairs


CORE = dp_pairs(lambda y, h, c: (y, h, 1 - c))
HIGH = dp_pairs(lambda y, h, c: (y, 1 - h, c))
COLUMNS = [[y * 4 + h * 2 + c for y in range(4)] for h in range(2) for c in range(2)]
LEVELS = [[y * 4 + h * 2 + c for y in range(4) for c in range(2)] for h in range(2)]
BLOCKS = [y * 4 + h * 2 + c for y in range(4) for c in range(2) for h in range(2)]


def left(v):
    return lax.ppermute(v, "tensor", LEFT)


def right(v):
    return lax.ppermute(v, "tensor", RIGHT)


def across(v):
    return lax.ppermute(v, "tensor", ACROSS)


def opposite(v):
    return lax.ppermute(v, "tensor", OPPOSITE)


def pair_gather_first(own):
    return {
        (0, 0): own,
        (0, 2): opposite(own),
        (0, 1): left(own),
        (0, -1): right(own),
        (1, 0): across(own),
    }


def pair_gather_second(got):
    new = {(1, 1): left(got[1, 0]), (1, -1): right(got[1, 0]), (1, 2): across(got[0, 2])}
    return {**got, **new}


def gather_first(own):
    return {(0, 0): own, (0, 1): left(own), (0, -1): right(own), (1, 0): across(own)}


def gather_second(got):
    new = {(0, 2): right(got[0, -1]), (1, 1): left(got[1, 0]), (1, -1): across(got[0, -1])}
    return {**got, **new}


def gather_third(got):
    half = got[0, 0].shape[0] // 2
    return {**got, (1, 2): [right(got[1, -1][:half]), left(got[1, 1][half:])]}


def listed(got, order):
    blocks = []
    for rel in order:
        blocks += got[rel] if rel == (1, 2) else [got[rel]]
    return blocks


def fence(*values):
    return lax.optimization_barrier(values)


def plus(*terms):
    total = terms[0].astype(jnp.float32)
    for term in terms[1:]:
        total = total + term.astype(jnp.float32)
    return total.astype(terms[0].dtype)


def pair_scatter_first(part):
    return left(part[1, -1]), right(part[1, 1]), across(part[1, 2])


def pair_scatter_second(sums, part):
    from_right, from_left, from_across = sums
    return (
        across(plus(part[1, 0], from_right, from_left)),
        opposite(plus(part[0, 2], from_across)),
    )


def scatter_total(part, ends):
    return sum(
        (end.astype(jnp.float32) for end in jax.tree.leaves(ends)), part[0, 0].astype(jnp.float32)
    )


def dp_order():
    index = lax.axis_index("dp")
    h, c = (index // 2) % 2, index % 2
    return jnp.stack(
        [
            y * 4 + (h ^ high) * 2 + (c ^ core)
            for core in range(2)
            for y in range(4)
            for high in range(2)
        ]
    ).astype(jnp.int32)


def column_exchange(mine):
    blocks = mine.reshape((4, 2) + mine.shape[1:])
    return lax.all_to_all(blocks, "dp", 0, 0, axis_index_groups=COLUMNS, tiled=True)


def dp_third(terms):
    column = jnp.sum(terms.astype(jnp.float32), 0).astype(terms.dtype)
    return plus(column[0], lax.ppermute(column[1], "dp", HIGH))


def level_scatter_sum(whole):
    return lax.psum_scatter(
        whole, "dp", scatter_dimension=0, tiled=True, axis_index_groups=LEVELS
    )


def high_sum(pair):
    high = (lax.axis_index("dp") // 2) % 2
    give = lax.dynamic_index_in_dim(pair, 1 - high, 0, keepdims=False)
    keep = lax.dynamic_index_in_dim(pair, high, 0, keepdims=False)
    return plus(keep, lax.ppermute(give, "dp", HIGH))


def rope_tables(places):
    halfwidth = ROPE // 2
    frequency = jnp.exp(-jnp.log(10000.0) * (2.0 * jnp.arange(halfwidth, dtype=jnp.float32) / ROPE))
    angles = places.astype(jnp.float32)[:, None] * frequency[None, :]
    return (jnp.cos(angles), jnp.sin(angles))


def normalize(values, gain):
    factor = lax.rsqrt(jnp.mean(values * values, -1, keepdims=True) + EPSILON)
    scaled = values * factor
    return (scaled * gain, scaled, factor)


def norm_backward(grads_in, scaled, factor, gain):
    weighted = grads_in * gain
    centre = jnp.mean(weighted * scaled, -1, keepdims=True)
    return (factor * (weighted - scaled * centre), jnp.sum(grads_in * scaled, 0))


def contract_rows(first, second):
    return lax.dot_general(
        first, second, (((0,), (0,)), ((), ())), preferred_element_type=jnp.float32
    )


def contract_last(first, second):
    return lax.dot_general(
        first, second, (((1,), (1,)), ((), ())), preferred_element_type=jnp.float32
    )


def matmul(first, second):
    return jnp.dot(first, second, preferred_element_type=jnp.float32)


def widen(array, width):
    return jnp.pad(array, ((0, 0), (0, width - array.shape[1])))


CHUNK = 256


def grant(mebibytes):
    return pltpu.CompilerParams(vmem_limit_bytes=mebibytes * 2**20)


def join_refs(refs, out, width):
    at = 0
    for ref in refs:
        rows = ref.shape[0]
        out[at : at + rows, :] = ref[:, :width]
        at += rows


def split_refs(value, refs, at):
    for ref in refs:
        rows = ref.shape[0]
        ref[...] = value[at : at + rows].astype(ref.dtype)
        at += rows


def swap_halves(value):
    lanes = value.shape[1]
    lane = lax.broadcasted_iota(jnp.int32, value.shape, 1) % ROPE
    return jnp.where(
        lane < ROPE // 2, pltpu.roll(value, lanes - ROPE // 2, 1), pltpu.roll(value, ROPE // 2, 1)
    )


def loads(pairs, sems):
    copies = [
        pltpu.make_async_copy(source, target, sems.at[at]) for at, (source, target) in enumerate(pairs)
    ]
    for copy in copies:
        copy.start()
    return copies


def attention_kernel(heads, rank, place, *refs):
    blocks, refs = refs[:8], refs[8:]
    gain, latent_gain, cosine, sine, query_far, down_far, up_far, out_far = refs[:8]
    logsums, factors = refs[8:10]
    far_outs, refs = refs[10:25], refs[25:]
    query_w, down_t, up_w, out_w = refs[:4]
    normed, queries, keys, values, scaled, compressed, attended, branch = refs[4:12]
    latent, raw, pair, turned, load_sems, store_sems = refs[12:]
    normed_far, queries_far, keys_far, values_far, scaled_far, compressed_far, attended_far = far_outs[:7]
    f32, bf16 = jnp.float32, jnp.bfloat16
    seq_len, width = normed.shape
    rows = seq_len // 8
    half = seq_len // 2
    scale = (NOPE + ROPE) ** (-0.5)

    weights = loads(
        [(down_far, down_t), (query_far, query_w), (up_far, up_w), (out_far, out_w)], load_sems
    )
    stores = []

    def store(source, target):
        copy = pltpu.make_async_copy(source, target, store_sems.at[len(stores)])
        copy.start()
        stores.append(copy)

    def slot_rows(slot):
        return pl.ds(pl.multiple_of(place[slot] * rows, rows), rows)

    join_refs(blocks, normed, width)

    def norm_rows(step, carry):
        at = pl.ds(pl.multiple_of(step * rows, rows), rows)
        value = normed[at, :].astype(f32)
        factor = lax.rsqrt(jnp.mean(value * value, 1, keepdims=True) + EPSILON)
        normed[at, :] = (value * factor * gain[...]).astype(bf16)
        return carry

    lax.fori_loop(0, 8, norm_rows, 0)
    store(normed, normed_far)
    weights[0].wait()
    latent[:, : rank + ROPE] = contract_last(normed[...], down_t[...])
    weights[1].wait()
    raw[...] = matmul(normed[...], query_w[...])

    def project_rows(step, carry):
        at = pl.ds(pl.multiple_of(step * rows, rows), rows)
        own = slot_rows(step)
        cos, sin = cosine[own, :], sine[own, :]
        value = latent[at, :rank]
        factor = lax.rsqrt(jnp.mean(value * value, 1, keepdims=True) + EPSILON)
        factors[at, :] = factor
        scaled[at, :] = value * factor
        compressed[at, :] = (value * factor * latent_gain[...]).astype(bf16)
        left_half = lax.broadcasted_iota(jnp.int32, (rows, NOPE), 1) < ROPE
        key_rope = latent[at, rank:]
        key_rope = jnp.where(left_half, key_rope, pltpu.roll(key_rope, ROPE, 1))
        key_rope = (key_rope * cos + swap_halves(key_rope) * sin).astype(bf16)
        one, two = raw[at, NOPE : 2 * NOPE], raw[at, 2 * NOPE :]
        plain = raw[at, :NOPE], jnp.where(left_half, pltpu.roll(one, ROPE, 1), pltpu.roll(two, ROPE, 1))
        query_rope = jnp.where(left_half, one, two)
        query_rope = query_rope * cos + swap_halves(query_rope) * sin
        for head in range(heads):
            queries[head, own, :NOPE] = plain[head].astype(bf16)
            queries[head, own, NOPE:] = jnp.where(left_half == (head == 0), query_rope, 0.0).astype(bf16)
            keys[head, own, NOPE:] = key_rope
        return carry

    lax.fori_loop(0, 8, project_rows, 0)
    store(scaled, scaled_far)
    store(compressed, compressed_far)
    store(queries, queries_far)
    weights[2].wait()
    raw_wide = (NOPE + VDIM) * heads
    pair[:, :raw_wide] = matmul(compressed[:half], up_w[...])
    pair[:, raw_wide : 2 * raw_wide] = matmul(compressed[half:], up_w[...])
    for slot in range(8):
        own = slot_rows(slot)
        at = slice(slot % 4 * rows, (slot % 4 + 1) * rows)
        for head in range(heads):
            start = slot // 4 * raw_wide + head * (NOPE + VDIM)
            keys[head, own, :NOPE] = pair[at, start : start + NOPE].astype(bf16)
            values[head, own, :] = pair[at, start + NOPE : start + NOPE + VDIM].astype(bf16)
    store(keys, keys_far)
    store(values, values_far)

    for step in range(4):
        at = slice(step * 2 * rows, (step + 1) * 2 * rows)
        stop = (step + 1) * 2 * rows
        row = lax.broadcasted_iota(jnp.int32, (2 * rows, stop), 0) + step * 2 * rows
        allowed = lax.broadcasted_iota(jnp.int32, (2 * rows, stop), 1) <= row
        for head in range(heads):
            scores = contract_last(queries[head, at, :], keys[head, :stop, :]) * scale
            scores = jnp.where(allowed, scores, -1e30)
            highest = jnp.max(scores, 1, keepdims=True)
            weight = jnp.exp(scores - highest)
            denominator = jnp.sum(weight, 1, keepdims=True)
            logsums[head, at, :] = highest + jnp.log(denominator)
            shares = (weight * (1.0 / denominator)).astype(bf16)
            turned[at, head * VDIM : (head + 1) * VDIM] = matmul(shares, values[head, :stop, :]).astype(bf16)
    for slot in range(8):
        attended[slot * rows : (slot + 1) * rows, :] = turned[slot_rows(slot), :]
    store(attended, attended_far)
    weights[3].wait()
    for order in (1, 0):
        at = slice(order * half, (order + 1) * half)
        branch[at, :] = contract_last(attended[at, :], out_w[...]).astype(bf16)
        for slot in range(4 * order, 4 * order + 4):
            store(branch.at[slot * rows : (slot + 1) * rows, :], far_outs[7 + slot])
    for copy in stores:
        copy.wait()


def attention(place, blocks, gain, query_w, down_t, latent_gain, up_w, out_w, cosine, sine):
    rows = blocks[0].shape[0]
    seq_len, width = rows * 8, blocks[0].shape[1]
    rank = up_w.shape[0]
    heads = up_w.shape[1] // (NOPE + VDIM)
    f32, bf16 = jnp.float32, jnp.bfloat16
    shape = jax.ShapeDtypeStruct
    vmem, far = pl.BlockSpec(memory_space=pltpu.VMEM), pl.BlockSpec(memory_space=pl.ANY)
    kept = [
        shape((seq_len, width), bf16),
        shape((heads, seq_len, 2 * NOPE), bf16),
        shape((heads, seq_len, 2 * NOPE), bf16),
        shape((heads, seq_len, VDIM), bf16),
        shape((seq_len, rank), f32),
        shape((seq_len, rank), bf16),
        shape((seq_len, heads * VDIM), bf16),
    ]
    weights = [query_w, down_t, up_w, out_w]
    return pl.pallas_call(
        functools.partial(attention_kernel, heads, rank),
        in_specs=[pl.BlockSpec(memory_space=pltpu.SMEM)] + [vmem] * 12 + [far] * 4,
        out_specs=[vmem] * 2 + [far] * 15,
        out_shape=[shape((heads, seq_len, 1), f32), shape((seq_len, 1), f32)]
        + kept
        + [shape((rows, width), bf16)] * 8,
        scratch_shapes=[pltpu.VMEM(a.shape, a.dtype) for a in weights + kept]
        + [
            pltpu.VMEM((seq_len, width), bf16),
            pltpu.VMEM((seq_len, rank + NOPE), f32),
            pltpu.VMEM((seq_len, query_w.shape[1]), f32),
            pltpu.VMEM((seq_len // 2, 2 * heads * (NOPE + VDIM)), f32),
            pltpu.VMEM((seq_len, heads * VDIM), bf16),
            pltpu.SemaphoreType.DMA((4,)),
            pltpu.SemaphoreType.DMA((15,)),
        ],
        compiler_params=grant(56),
        cost_estimate=pl.CostEstimate(
            flops=20 * seq_len * width * width // 4, bytes_accessed=30 * 2**20, transcendentals=0
        ),
        name="attention",
    )(place, *blocks, gain, latent_gain, cosine, sine, *weights)


def attention_grad_kernel(heads, place, *refs):
    blocks, refs = refs[:8], refs[8:]
    out_w, cosine, sine, logsums, queries_far, keys_far, values_far = refs[:7]
    branch_far, query_grads, kv_grads, rope_grads = refs[7:11]
    queries, keys, values, branch_grads = refs[11:15]
    out_grads, key_grads, value_grads, turned, load_sems, store_sem = refs[15:]
    f32, bf16 = jnp.float32, jnp.bfloat16
    seq_len, width = branch_grads.shape
    rows = seq_len // 8
    scale = (NOPE + ROPE) ** (-0.5)

    arrays = loads([(queries_far, queries), (keys_far, keys), (values_far, values)], load_sems)
    join_refs(blocks, branch_grads, width)
    (stored,) = loads([(branch_grads, branch_far)], store_sem)

    def slot_rows(slot):
        return pl.ds(pl.multiple_of(place[slot] * rows, rows), rows)

    grads = matmul(branch_grads[...], out_w[...]).astype(bf16)
    for slot in range(8):
        out_grads[slot_rows(slot), :] = grads[slot * rows : (slot + 1) * rows, :]
    key_grads[...] = jnp.zeros_like(key_grads)
    value_grads[...] = jnp.zeros_like(value_grads)
    for array in arrays:
        array.wait()

    left_half = lax.broadcasted_iota(jnp.int32, (2 * rows, NOPE), 1) < ROPE
    for step in range(4):
        at = slice(step * 2 * rows, (step + 1) * 2 * rows)
        stop = (step + 1) * 2 * rows
        row = lax.broadcasted_iota(jnp.int32, (2 * rows, stop), 0) + step * 2 * rows
        allowed = lax.broadcasted_iota(jnp.int32, (2 * rows, stop), 1) <= row
        plain, ropes = [], []
        for head in range(heads):
            query, key = queries[head, at, :], keys[head, :stop, :]
            out_grad = out_grads[at, head * VDIM : (head + 1) * VDIM]
            scores = contract_last(query, key) * scale
            shares = jnp.where(allowed, jnp.exp(scores - logsums[head, at, :]), 0.0)
            share_grads = contract_last(out_grad, values[head, :stop, :])
            centre = jnp.sum(shares * share_grads, 1, keepdims=True)
            score_grads = (shares * (share_grads - centre)).astype(bf16)
            value_grads[head, :stop, :] += contract_rows(shares.astype(bf16), out_grad)
            key_grads[head, :stop, :] += contract_rows(score_grads, query)
            query_grad = matmul(score_grads, key) * scale
            plain.append(query_grad[:, :NOPE])
            ropes.append(query_grad[:, NOPE:])
        rope = jnp.where(left_half, ropes[0], ropes[1])
        rope = rope * cosine[at, :] - swap_halves(rope) * sine[at, :]
        moved = pltpu.roll(plain[1], ROPE, 1)
        turned[at, :NOPE] = plain[0].astype(bf16)
        turned[at, NOPE : 2 * NOPE] = jnp.where(left_half, rope, moved).astype(bf16)
        turned[at, 2 * NOPE :] = jnp.where(left_half, moved, rope).astype(bf16)

    for slot in range(8):
        own, at = slot_rows(slot), slice(slot * rows, (slot + 1) * rows)
        query_grads[at, :] = turned[own, :]
        for head in range(heads):
            start = head * (NOPE + VDIM)
            kv_grads[at, start : start + NOPE] = (key_grads[head, own, :NOPE] * scale).astype(bf16)
            kv_grads[at, start + NOPE : start + NOPE + VDIM] = value_grads[head, own, :].astype(bf16)
        rope = sum(key_grads[head, own, NOPE:] for head in range(heads)) * scale
        rope = rope + pltpu.roll(rope, ROPE, 1)
        rope = rope * cosine[own, :] - swap_halves(rope) * sine[own, :]
        lane = lax.broadcasted_iota(jnp.int32, rope.shape, 1)
        rope_grads[at, :] = jnp.where(lane < ROPE, rope, 0.0).astype(bf16)
    stored.wait()


def attention_grad(place, blocks, out_w, cosine, sine, queries, keys, values, logsums):
    seq_len, width = queries.shape[1], blocks[0].shape[1]
    heads = queries.shape[0]
    f32, bf16 = jnp.float32, jnp.bfloat16
    shape = jax.ShapeDtypeStruct
    vmem, far = pl.BlockSpec(memory_space=pltpu.VMEM), pl.BlockSpec(memory_space=pl.ANY)
    return pl.pallas_call(
        functools.partial(attention_grad_kernel, heads),
        in_specs=[pl.BlockSpec(memory_space=pltpu.SMEM)] + [vmem] * 12 + [far] * 3,
        out_specs=[far] + [vmem] * 3,
        out_shape=[
            shape((seq_len, width), bf16),
            shape((seq_len, heads * (NOPE + ROPE)), bf16),
            shape((seq_len, heads * (NOPE + VDIM)), bf16),
            shape((seq_len, NOPE), bf16),
        ],
        scratch_shapes=[pltpu.VMEM(a.shape, a.dtype) for a in (queries, keys, values)]
        + [
            pltpu.VMEM((seq_len, width), bf16),
            pltpu.VMEM((seq_len, heads * VDIM), bf16),
            pltpu.VMEM((heads, seq_len, 2 * NOPE), f32),
            pltpu.VMEM((heads, seq_len, VDIM), f32),
            pltpu.VMEM((seq_len, heads * (NOPE + ROPE)), bf16),
            pltpu.SemaphoreType.DMA((3,)),
            pltpu.SemaphoreType.DMA((1,)),
        ],
        compiler_params=grant(56),
        cost_estimate=pl.CostEstimate(
            flops=8 * seq_len * width * width // 4, bytes_accessed=20 * 2**20, transcendentals=0
        ),
        name="attention_grad",
    )(place, *blocks, out_w, cosine, sine, logsums, queries, keys, values)


def input_kernel(rank, spare, order, *refs):
    query_grads, kv_grads, rope_grads, gain, latent_gain, up_w, factors, router, mixer_gain = refs[:9]
    query_far, down_far, normed_far, scaled_far = refs[9:13]
    mine, other = refs[13:15]
    parts_far = refs[15:23]
    query_w, down_t, normed, scaled, pair, parts, lhs, wide, input_gain, load_sems, store_sems = refs[23:]
    f32, bf16 = jnp.float32, jnp.bfloat16
    seq_len, width = normed.shape
    rows = seq_len // 8
    arrays = loads(
        [(scaled_far, scaled), (query_far, query_w), (down_far, down_t), (normed_far, normed)], load_sems
    )
    lhs[:, rank:] = rope_grads[...]
    latent_total = jnp.zeros((1, rank), f32)
    arrays[0].wait()
    half = seq_len // 2
    for step in range(2):
        at = slice(step * half, (step + 1) * half)
        back = contract_last(kv_grads[at, :], up_w[...])
        value = scaled[at, :]
        latent_total = latent_total + jnp.sum(back * value, 0, keepdims=True)
        weighted = back * latent_gain[...]
        centre = jnp.mean(weighted * value, 1, keepdims=True)
        lhs[at, :rank] = (factors[at, :] * (weighted - value * centre)).astype(bf16)

    input_gain[...] = jnp.zeros_like(input_gain)
    stores = []
    for turn in (1, 0):
        start = turn * half
        at = slice(start, start + half)
        if turn:
            arrays[1].wait()
            arrays[2].wait()
        pair[...] = contract_last(query_grads[at, :], query_w[...]) + matmul(lhs[at, : rank + ROPE], down_t[...])
        if turn:
            arrays[3].wait()
        for step in range(4):
            spot = slice(step * rows, (step + 1) * rows)
            block = pair[spot, :]
            slot = 4 * turn + step
            parts[slot] = block.astype(bf16)
            copy = pltpu.make_async_copy(parts.at[slot], parts_far[slot], store_sems.at[slot])
            copy.start()
            stores.append(copy)
            input_gain[...] += jnp.sum(
                block * normed[start + step * rows : start + (step + 1) * rows, :].astype(f32),
                0,
                keepdims=True,
            )

    wide[...] = contract_rows(lhs[...], normed[...])
    lanes = mine.shape[2]
    at = spare + router.shape[0]
    wide[spare:at, :] = router[...]
    wide[at : at + 1, :] = input_gain[...] / gain[...]
    wide[at + 1 : at + 2, :] = mixer_gain[...]
    share = rank // 16
    entry = lax.broadcasted_iota(jnp.int32, (rank, width), 0)
    lane = lax.broadcasted_iota(jnp.int32, (rank, width), 1)
    each = share // 8
    spot = entry // share * lanes + entry % share // each * (lanes // 8) + entry % each
    wide[at + 2 : at + 3, :] = matmul(latent_total, (spot == lane).astype(f32))
    for slot in range(16):
        at = pl.multiple_of(order[slot] * lanes, lanes)
        block = wide[:, pl.ds(at, lanes)].astype(bf16)
        if slot < 8:
            mine[slot] = block
        else:
            other[slot - 8] = block
    for copy in stores:
        copy.wait()


def input_grads(order, spare, query_grads, kv_grads, rope_grads, gain, query_w, down_t, latent_gain, up_w, normed, scaled, factors, router, mixer_gain):
    seq_len, width = normed.shape
    rank = up_w.shape[0]
    columns = rank + NOPE
    f32, bf16 = jnp.float32, jnp.bfloat16
    shape = jax.ShapeDtypeStruct
    vmem, far = pl.BlockSpec(memory_space=pltpu.VMEM), pl.BlockSpec(memory_space=pl.ANY)
    arrays = [query_w, down_t, normed, scaled]
    return pl.pallas_call(
        functools.partial(input_kernel, rank, spare),
        in_specs=[pl.BlockSpec(memory_space=pltpu.SMEM)] + [vmem] * 9 + [far] * 4,
        out_specs=[vmem] * 2 + [far] * 8,
        out_shape=[shape((8, columns, width // 16), bf16)] * 2 + [shape((seq_len // 8, width), bf16)] * 8,
        scratch_shapes=[pltpu.VMEM(a.shape, a.dtype) for a in arrays]
        + [
            pltpu.VMEM((seq_len // 2, width), f32),
            pltpu.VMEM((8, seq_len // 8, width), bf16),
            pltpu.VMEM((seq_len, columns), bf16),
            pltpu.VMEM((columns, width), f32),
            pltpu.VMEM((1, width), f32),
            pltpu.SemaphoreType.DMA((4,)),
            pltpu.SemaphoreType.DMA((8,)),
        ],
        compiler_params=grant(56),
        cost_estimate=pl.CostEstimate(
            flops=8 * seq_len * width * width // 4, bytes_accessed=20 * 2**20, transcendentals=0
        ),
        name="input_grads",
    )(order, query_grads, kv_grads, rope_grads, gain, latent_gain, up_w, factors, router, mixer_gain, *arrays)


def forward_kernel(blocks, steps, expert_units, fused, *refs):
    hid_far, cot_far, refs = refs[:blocks], refs[blocks : blocks + 4], refs[blocks + 4 :]
    own, router, gate_w, up_w, down_w = refs[:5]
    refs = refs[5:]
    if fused:
        (gate_rows, up_rows, router_rows), refs = refs[:3], refs[3:]
    scaled, gate_g, up_g, logit_g, hid_out, cot_out = refs[:6]
    refs = refs[6:]
    if fused:
        parts, refs = refs[:4], refs[4:]
    hid, cot, probs, gate, total, chosen, load_sems, store_sems = refs[:8]
    j = pl.program_id(0)
    width, experts = hid.shape[1], own.shape[1]

    def stores():
        return [
            pltpu.make_async_copy(hid, hid_out, store_sems.at[0]),
            pltpu.make_async_copy(cot.at[:, :width], cot_out, store_sems.at[1]),
        ]

    @pl.when(j == 0)
    def _():
        pairs = []
        for sources, target in ((hid_far, hid), (cot_far, cot)):
            at = 0
            for source in sources:
                pairs.append((source, target.at[at : at + source.shape[0], :]))
                at += source.shape[0]
        for copy in loads(pairs, load_sems):
            copy.wait()
        for copy in stores():
            copy.start()
        mask = cot[:, width : width + experts].astype(jnp.float32)
        chosen[...] = jnp.sum(mask * own[...], 1, keepdims=True)
        logits = matmul(hid[...], router[...])
        powers = jnp.exp(logits - jnp.max(logits, 1, keepdims=True))
        probs[...] = powers / jnp.sum(powers, 1, keepdims=True)
        gate[...] = jnp.sum(probs[...] * own[...], 1, keepdims=True) * chosen[...]
        total[...] = jnp.zeros_like(total)

    def chunk():
        lanes = gate_w.shape[1]
        column = j * lanes + lax.broadcasted_iota(jnp.int32, (1, lanes), 1)
        is_expert = column < expert_units
        pre_gate = matmul(hid[...], gate_w[...])
        pre_up = matmul(hid[...], up_w[...])
        back = matmul(cot[:, :width], down_w[...])
        sigmoid = 1.0 / (1.0 + jnp.exp(-pre_gate))
        act = pre_gate * sigmoid
        slope = sigmoid * (1.0 + pre_gate * (1.0 - sigmoid))
        hidden = act * pre_up
        scale = jnp.where(is_expert, gate[...], 1.0)
        scaled[...] = (hidden * scale).astype(scaled.dtype)
        total[...] += jnp.sum(jnp.where(is_expert, hidden * back, 0.0), 1, keepdims=True)
        back = back * scale
        gate_grad = (back * pre_up * slope).astype(gate_g.dtype)
        up_grad = (back * act).astype(up_g.dtype)
        gate_g[...] = gate_grad
        up_g[...] = up_grad
        if fused:
            at = pl.ds(pl.multiple_of(j * lanes, lanes), lanes)
            gate_all, up_all = refs[8:]
            gate_all[:, at] = gate_grad
            up_all[:, at] = up_grad

    if fused:
        pl.when(j < steps)(chunk)
    else:
        chunk()

    @pl.when(j == steps - 1)
    def _():
        own_prob = jnp.sum(probs[...] * own[...], 1, keepdims=True)
        logit_g[...] = (total[...] * chosen[...] * probs[...] * (own[...] - own_prob)).astype(logit_g.dtype)
        for copy in stores():
            copy.wait()

    if fused:

        @pl.when(j >= steps)
        def _():
            gate_all, up_all = refs[8:]
            grad = contract_last(gate_all[...], gate_rows[...]) + contract_last(up_all[...], up_rows[...])
            split_refs(grad + contract_last(logit_g[...], router_rows[...]), parts, 0)


def feed_forward(hid, cot, own, router, gate_w, up_w, weight_out, expert_units, fused):
    rows, width = sum(block.shape[0] for block in hid), hid[0].shape[1]
    units = gate_w.shape[1]
    steps = units // CHUNK
    experts = own.shape[1]
    bf16, f32 = jnp.bfloat16, jnp.float32
    shape = jax.ShapeDtypeStruct
    part = pl.BlockSpec((rows, CHUNK), lambda j: (0, jnp.minimum(j, steps - 1)))
    weight = pl.BlockSpec((width, CHUNK), lambda j: (0, jnp.minimum(j, steps - 1)))
    whole, far = pl.BlockSpec(memory_space=pltpu.VMEM), pl.BlockSpec(memory_space=pl.ANY)
    column = pltpu.VMEM((rows, 1), f32)
    operands = [*hid, *cot, own, router, gate_w, up_w, weight_out]
    in_specs = [far] * (len(hid) + 4) + [whole] * 2 + [weight] * 3
    out_specs = [part, part, part, whole, far, far]
    out_shape = [shape((rows, units), bf16)] * 3 + [shape((rows, experts), bf16)]
    out_shape += [shape((rows, width), bf16)] * 2
    scratch = [
        pltpu.VMEM((rows, width), bf16),
        pltpu.VMEM((rows, cot[0].shape[1]), bf16),
        pltpu.VMEM((rows, experts), f32),
        column,
        column,
        column,
        pltpu.SemaphoreType.DMA((len(hid) + 4,)),
        pltpu.SemaphoreType.DMA((2,)),
    ]
    grid = steps
    if fused:
        deep = min(512, width)
        grid += width // deep
        operands += [gate_w, up_w, router]
        in_specs += [pl.BlockSpec((deep, units), lambda j: (jnp.maximum(j - steps, 0), 0))] * 2
        in_specs += [pl.BlockSpec((deep, experts), lambda j: (jnp.maximum(j - steps, 0), 0))]
        out_specs += [pl.BlockSpec((rows // 4, deep), lambda j: (0, jnp.maximum(j - steps, 0)))] * 4
        out_shape += [shape((rows // 4, width), bf16)] * 4
        scratch += [pltpu.VMEM((rows, units), bf16)] * 2
    return pl.pallas_call(
        functools.partial(forward_kernel, len(hid), steps, expert_units, fused),
        grid=(grid,),
        in_specs=in_specs,
        out_specs=out_specs,
        out_shape=out_shape,
        scratch_shapes=scratch,
        compiler_params=grant(56),
        cost_estimate=pl.CostEstimate(
            flops=(10 if fused else 6) * rows * width * units,
            bytes_accessed=6 * width * units,
            transcendentals=rows * units,
        ),
        name="feed_forward",
    )(*operands)


def input_grad_kernel(gate_g, up_g, logit_g, gate_w, up_w, router, *outs):
    total = contract_last(gate_g[...], gate_w[...]) + contract_last(up_g[...], up_w[...])
    split_refs(total + contract_last(logit_g[...], router[...]), outs, 0)


def input_grad(gate_g, up_g, logit_g, gate_w, up_w, router):
    rows, units = gate_g.shape
    sizes = [rows // 4] * 4
    width, experts = router.shape
    part = min(512, width)
    whole = pl.BlockSpec(memory_space=pltpu.VMEM)
    return pl.pallas_call(
        input_grad_kernel,
        grid=(width // part,),
        in_specs=[
            whole,
            whole,
            whole,
            pl.BlockSpec((part, units), lambda j: (j, 0)),
            pl.BlockSpec((part, units), lambda j: (j, 0)),
            pl.BlockSpec((part, experts), lambda j: (j, 0)),
        ],
        out_specs=[pl.BlockSpec((size, part), lambda j: (0, j)) for size in sizes],
        out_shape=[jax.ShapeDtypeStruct((size, width), jnp.bfloat16) for size in sizes],
        compiler_params=grant(56),
        cost_estimate=pl.CostEstimate(
            flops=4 * rows * width * units, bytes_accessed=4 * width * units, transcendentals=0
        ),
        name="input_grad",
    )(gate_g, up_g, logit_g, gate_w, up_w, router)


def output_kernel(first, second, down_w, *outs):
    scaled = jnp.concatenate([first[...], second[...]], 0)
    split_refs(contract_last(scaled, down_w[...]), outs, 0)


def mixer_output(scaled, weight_out):
    rows, units = scaled[0].shape
    sizes = [rows // 4] * 8
    width = weight_out.shape[0]
    part = min(512, width)
    return pl.pallas_call(
        output_kernel,
        grid=(width // part,),
        in_specs=[
            pl.BlockSpec(memory_space=pltpu.VMEM),
            pl.BlockSpec(memory_space=pltpu.VMEM),
            pl.BlockSpec((part, units), lambda j: (j, 0)),
        ],
        out_specs=[pl.BlockSpec((size, part), lambda j: (0, j)) for size in sizes],
        out_shape=[jax.ShapeDtypeStruct((size, width), jnp.bfloat16) for size in sizes],
        compiler_params=grant(56),
        cost_estimate=pl.CostEstimate(
            flops=4 * rows * width * units, bytes_accessed=2 * width * units, transcendentals=0
        ),
        name="mixer_output",
    )(*scaled, weight_out)


def store_blocks(out, product, at=0):
    rows = product.shape[0]
    lanes = out.shape[2]
    for slot, block in enumerate(BLOCKS):
        out[slot, at : at + rows, :] = product[:, block * lanes : (block + 1) * lanes].astype(out.dtype)


def mixer_weight_kernel(la, lb, ra, rb, *refs):
    store_blocks(refs[-1], contract_rows(la[...], ra[...]) + contract_rows(lb[...], rb[...]))


def mixer_weights(order, parts, lhs, rhs, kept=None):
    rows, units = lhs[0].shape
    width = rhs[0].shape[1]
    steps = units // CHUNK
    part = pl.BlockSpec((rows, CHUNK), lambda j: (0, j))
    whole = pl.BlockSpec(memory_space=pltpu.VMEM)
    kept = [] if kept is None else [kept]
    return pl.pallas_call(
        mixer_weight_kernel,
        grid=(steps,),
        in_specs=[part, part, whole, whole] + [pl.BlockSpec(memory_space=pl.ANY)] * len(kept),
        out_specs=pl.BlockSpec((16, CHUNK, width // 16), lambda j: (0, j + order * steps, 0)),
        out_shape=jax.ShapeDtypeStruct((16, parts * units, width // 16), jnp.bfloat16),
        input_output_aliases={4: 0} if kept else {},
        compiler_params=grant(56),
        cost_estimate=pl.CostEstimate(
            flops=4 * rows * width * units, bytes_accessed=2 * width * units, transcendentals=0
        ),
        name="mixer_weights",
    )(*lhs, *rhs, *kept)


def head_weight_kernel(query_grads, normed, attended, branch_grads, compressed, kv_grads, out):
    store_blocks(out, contract_rows(query_grads[...], normed[...]))
    at = query_grads.shape[1]
    store_blocks(out, contract_rows(attended[...], branch_grads[...]), at)
    at += attended.shape[1]
    lanes = out.shape[2]
    product = contract_rows(compressed[...], kv_grads[...]).astype(out.dtype)
    share = product.shape[0] // 16
    for slot, block in enumerate(BLOCKS):
        for step in range(product.shape[1] // lanes):
            start = at + step * share
            out[slot, start : start + share, :] = product[
                block * share : (block + 1) * share, step * lanes : (step + 1) * lanes
            ]


def head_weights(query_grads, normed, attended, branch_grads, compressed, kv_grads):
    rows, width = normed.shape
    lanes = width // 16
    total = query_grads.shape[1] + attended.shape[1]
    total += compressed.shape[1] // 16 * kv_grads.shape[1] // lanes
    vmem = pl.BlockSpec(memory_space=pltpu.VMEM)
    return pl.pallas_call(
        head_weight_kernel,
        in_specs=[vmem] * 6,
        out_specs=vmem,
        out_shape=jax.ShapeDtypeStruct((16, total, lanes), jnp.bfloat16),
        compiler_params=grant(56),
        cost_estimate=pl.CostEstimate(
            flops=2 * rows * width * total, bytes_accessed=4 * width * rows, transcendentals=0
        ),
        name="head_weights",
    )(query_grads, normed, attended, branch_grads, compressed, kv_grads)


def latent_finish_kernel(late, rest):
    rest[...] = late[...].astype(jnp.float32).T.astype(rest.dtype)


def latent_finish(late):
    return pl.pallas_call(
        latent_finish_kernel,
        out_shape=jax.ShapeDtypeStruct(late.shape[::-1], late.dtype),
        compiler_params=grant(8),
        name="latent_finish",
    )(late)


def head_finish_kernel(query_wide, late, query, output, up):
    query[...] = late[:query_wide, :].astype(jnp.float32).T
    at = query_wide + output.shape[1]
    output[...] = late[query_wide:at, :].astype(jnp.float32).T
    lanes, share = late.shape[1], up.shape[0]
    for step in range(up.shape[1] // lanes):
        start = at + step * share
        up[:, step * lanes : (step + 1) * lanes] = late[start : start + share, :].astype(jnp.float32)


def head_finish(late, query_wide, value_wide, up_shape):
    lanes = late.shape[1]
    f32 = jnp.float32
    return pl.pallas_call(
        functools.partial(head_finish_kernel, query_wide),
        out_shape=[
            jax.ShapeDtypeStruct((lanes, query_wide), f32),
            jax.ShapeDtypeStruct((lanes, value_wide), f32),
            jax.ShapeDtypeStruct(up_shape, f32),
        ],
        compiler_params=grant(8),
        name="head_finish",
    )(late)


def mixer_finish_kernel(expert_units, shared_units, gate, other, *outs):
    units = gate.shape[0]
    for order, (totals, start) in enumerate(((gate, 0), (other, 0), (other, units))):
        expert = totals[start : start + expert_units, :].astype(jnp.float32)
        outs[order][:, 0, :] = expert.T
        start += expert_units
        outs[3 + order][...] = totals[start : start + shared_units, :].astype(jnp.float32)


def mixer_finish(gate, other, expert_units, shared_units):
    lanes = gate.shape[1]
    f32 = jnp.float32
    return pl.pallas_call(
        functools.partial(mixer_finish_kernel, expert_units, shared_units),
        out_shape=[jax.ShapeDtypeStruct((lanes, 1, expert_units), f32)] * 3
        + [jax.ShapeDtypeStruct((shared_units, lanes), f32)] * 3,
        compiler_params=grant(16),
        name="mixer_finish",
    )(gate, other)


def on_device(
    tokens,
    expert_index,
    cotangent,
    input_gain,
    query_weight,
    latent_down,
    latent_gain,
    latent_up,
    output_weight,
    mixer_gain,
    router_weight,
    shared_gate,
    shared_up,
    shared_down,
    expert_gate,
    expert_up,
    expert_down,
):
    tok_rows, width = tokens.shape
    group = lax.axis_index("tensor")
    z, x = group // 4, group % 4
    rank = latent_up.shape[0]
    heads_local = query_weight.shape[1] // (NOPE + ROPE)
    experts_all = router_weight.shape[1]
    scale = (NOPE + ROPE) ** (-0.5)
    expert_units = expert_gate.shape[2]
    shared_units = shared_gate.shape[1]
    shared_wide = -(-shared_units // 128) * 128
    units = expert_units + shared_wide
    bf16, f32 = jnp.bfloat16, jnp.float32

    first_order, second_order = ORDER[:4], ORDER[4:]
    seq_len = tok_rows * 8

    cosine, sine = rope_tables(jnp.arange(seq_len, dtype=jnp.int32))
    cosine = jnp.concatenate([cosine] * (2 * NOPE // ROPE), 1)
    sine = jnp.concatenate([-sine, sine] * (NOPE // ROPE), 1)
    chosen = (expert_index[:, :, None] == jnp.arange(experts_all, dtype=jnp.int32)).any(1)
    sent = jnp.concatenate([cotangent, widen(chosen.astype(bf16), 128)], 1)
    shared_gate, shared_up, shared_down = (
        widen(part, shared_wide) for part in (shared_gate, shared_up, shared_down)
    )
    got = pair_gather_first(tokens)
    got, cosine, sine, sent, shared_gate, shared_up, shared_down = fence(
        got, cosine, sine, sent, shared_gate, shared_up, shared_down
    )
    got = pair_gather_second(got)
    weight_out = jnp.concatenate([expert_down.reshape(width, expert_units), shared_down], 1)
    got, weight_out, sent = fence(got, weight_out, sent)

    upstream = pair_gather_first(sent)

    place = jnp.stack([(z ^ dz) * 4 + (x + dx) % 4 for dz, dx in ORDER]).astype(jnp.int32)
    outs = attention(
        place,
        [got[rel] for rel in ORDER],
        input_gain[None],
        query_weight,
        latent_down.T,
        latent_gain[None],
        latent_up,
        output_weight,
        cosine,
        sine,
    )
    logsums, latent_factor, normed_all, queries, keys, values, latent_scaled = outs[:7]
    compressed, attended = outs[7:9]
    part = dict(zip(ORDER, outs[9:]))
    part, upstream = fence(part, upstream)
    sums = pair_scatter_first(part)
    gate_w = jnp.concatenate([expert_gate.reshape(width, expert_units), shared_gate], 1)
    sums, part, gate_w, expert_up, shared_up = fence(sums, part, gate_w, expert_up, shared_up)
    ends = pair_scatter_second(sums, part), left(part[0, -1]), right(part[0, 1])
    up_w = jnp.concatenate([expert_up.reshape(width, expert_units), shared_up], 1)
    ends, up_w = fence(ends, up_w)
    branch = scatter_total(part, ends)

    middle = tokens.astype(f32) + branch
    second_normed, second_scaled, second_factor = normalize(middle, mixer_gain)
    own_expert = (jnp.arange(experts_all) == group).astype(f32)[None, :]

    def feed(got, order, fused):
        return feed_forward(
            listed(got, order),
            [upstream[rel] for rel in order],
            own_expert,
            router_weight,
            gate_w,
            up_w,
            weight_out,
            expert_units,
            fused,
        )

    got = gather_second(gather_first(second_normed.astype(bf16)))
    fed_first = feed(got, first_order, False)
    got, fed_first, upstream = fence(got, fed_first, upstream)
    got, upstream = gather_third(got), pair_gather_second(upstream)
    first_part = input_grad(*fed_first[1:4], gate_w, up_w, router_weight)
    got, upstream, first_part = fence(got, upstream, first_part)
    fed_second = feed(got, second_order, True)
    hidden_scaled, gate_grads, up_grads, logit_grads, hidden, upstream = zip(
        fed_first, fed_second[:6]
    )
    part = dict(zip(second_order, fed_second[6:]))
    sums = pair_scatter_first(part)
    gate_parts = mixer_weights(0, 1, gate_grads, hidden)
    sums, gate_parts = fence(sums, gate_parts)
    gate_totals = level_scatter_sum(gate_parts)
    part.update(zip(first_order, first_part))
    ends = pair_scatter_second(sums, part), left(part[0, -1]), right(part[0, 1])
    other_parts = mixer_weights(0, 2, up_grads, hidden)
    ends, other_parts = fence(ends, other_parts)
    mixer_back = scatter_total(part, ends)
    middle_from, grad_mixer_gain = norm_backward(
        mixer_back, second_scaled, second_factor, mixer_gain
    )
    middle_grads = cotangent.astype(f32) + middle_from
    got = pair_gather_first(middle_grads.astype(bf16))
    other_parts = mixer_weights(1, 2, hidden_scaled, upstream, other_parts)
    grad_router = sum(contract_rows(g, hid) for g, hid in zip(logit_grads, hidden))
    got, other_parts, grad_router = fence(got, other_parts, grad_router)
    other_totals = level_scatter_sum(other_parts)
    got = pair_gather_second(got)
    out_blocks = mixer_output(hidden_scaled, weight_out)
    got, out_blocks, gate_totals = fence(got, out_blocks, gate_totals)

    out = dict(zip(ORDER, out_blocks))
    out_sums, out_left = pair_scatter_first(out), left(out[0, -1])
    gate_total = high_sum(gate_totals)
    grads = attention_grad(
        place, [got[rel] for rel in ORDER], output_weight, cosine, sine, queries, keys, values, logsums
    )
    out_sums, grads, gate_total = fence(out_sums, grads, gate_total)
    branch_all, query_grads, kv_grads, rope_grads = grads
    out_ends, out_right = pair_scatter_second(out_sums, out), right(out[0, 1])
    wide = latent_down.shape[1]
    lanes = width // 16
    share = rank // 16
    grads = input_grads(
        dp_order(),
        wide,
        query_grads,
        kv_grads,
        rope_grads,
        input_gain[None],
        query_weight,
        latent_down.T,
        latent_gain[None],
        latent_up,
        normed_all,
        latent_scaled,
        latent_factor,
        grad_router,
        grad_mixer_gain[None],
    )
    head_parts = head_weights(query_grads, normed_all, attended, branch_all, compressed, kv_grads)
    out_ends, out_left, out_right, grads, head_parts = fence(
        out_ends, out_left, out_right, grads, head_parts
    )
    mine, other = grads[:2]
    part = dict(zip(ORDER, grads[2:]))

    sums = pair_scatter_first(part)
    other = lax.ppermute(other, "dp", CORE)
    other, head_parts, other_totals = fence(plus(mine, other), head_parts, other_totals)
    terms = column_exchange(other)
    head_totals = level_scatter_sum(head_parts)
    other_total = high_sum(other_totals)
    sums, terms = fence(sums, terms)
    late = dp_third(terms)
    ends = *pair_scatter_second(sums, part), left(part[0, -1]), right(part[0, 1])
    late, other_total = fence(late, other_total)
    normed_grads = scatter_total(part, ends)
    _, first_scaled, first_factor = normalize(tokens.astype(f32), input_gain)
    input_from, _ = norm_backward(normed_grads, first_scaled, first_factor, input_gain)
    grad_tokens = middle_grads + input_from
    rest = latent_finish(late).reshape(8, lanes // 8, -1)
    rest = lax.all_to_all(rest, "tensor", 0, 0, tiled=True)
    head_total = high_sum(head_totals)
    layer_out = (middle + scatter_total(out, (out_ends, out_left, out_right))).astype(bf16)
    rest, head_total, layer_out, grad_tokens = fence(rest, head_total, layer_out, grad_tokens)
    rest = jnp.sum(rest.astype(f32), 0)
    at = wide + experts_all
    expert_outs = mixer_finish(gate_total, other_total, expert_units, shared_units)
    total_query, total_output, total_up = head_finish(
        head_total, query_weight.shape[1], attended.shape[1], (share, latent_up.shape[1])
    )
    return (
        layer_out,
        grad_tokens,
        rest[:, at],
        total_query,
        rest[:, :wide],
        rest[: share // 8, at + 2],
        total_up,
        total_output,
        rest[:, at + 1],
        rest[:, wide:at],
        *[shared.T for shared in expert_outs[3:]],
        *expert_outs[:3],
    )


def solution(mesh):
    rows = P(("dp", "tensor"), None)
    columns = P(None, "tensor")
    middle = P(None, "tensor", None)
    return jax.shard_map(
        on_device,
        mesh=mesh,
        in_specs=(rows, rows, rows, P(), columns, P(), P(), columns, columns, P(), P())
        + (columns,) * 3
        + (middle,) * 3,
        out_specs=(
            rows,
            rows,
            P(("dp", "tensor")),
            P("dp", "tensor"),
            rows,
            P(("dp", "tensor")),
            P("dp", "tensor"),
            P("dp", "tensor"),
            P(("dp", "tensor")),
            rows,
        )
        + (P("dp", "tensor"),) * 3
        + (P("dp", "tensor", None),) * 3,
        check_vma=False,
    )
```

```python
import functools

import jax
import jax.numpy as jnp
from jax import lax
from jax.experimental import pallas as pl
from jax.experimental.pallas import tpu as pltpu
from jax.sharding import PartitionSpec as P

NOPE = 128
ROPE = 64
VDIM = 128
EPSILON = 1e-06

ORDER = ((0, 0), (0, -1), (0, 1), (1, 0), (0, 2), (1, 1), (1, -1), (1, 2))
SLOT = {rel: slot for slot, rel in enumerate(ORDER)}

LEFT = [(z * 4 + x, z * 4 + (x - 1) % 4) for z in range(2) for x in range(4)]
RIGHT = [(z * 4 + x, z * 4 + (x + 1) % 4) for z in range(2) for x in range(4)]
OPPOSITE = [(z * 4 + x, z * 4 + (x + 2) % 4) for z in range(2) for x in range(4)]
ACROSS = [(z * 4 + x, (1 - z) * 4 + x) for z in range(2) for x in range(4)]


def dp_pairs(move):
    pairs = []
    for y in range(4):
        for h in range(2):
            for c in range(2):
                y2, h2, c2 = move(y, h, c)
                pairs.append((y * 4 + h * 2 + c, (y2 % 4) * 4 + h2 * 2 + c2))
    return pairs


CORE = dp_pairs(lambda y, h, c: (y, h, 1 - c))
HIGH = dp_pairs(lambda y, h, c: (y, 1 - h, c))
COLUMNS = [[y * 4 + h * 2 + c for y in range(4)] for h in range(2) for c in range(2)]
LEVELS = [[y * 4 + h * 2 + c for y in range(4) for c in range(2)] for h in range(2)]
BLOCKS = [y * 4 + h * 2 + c for y in range(4) for c in range(2) for h in range(2)]


def left(v):
    return lax.ppermute(v, "tensor", LEFT)


def right(v):
    return lax.ppermute(v, "tensor", RIGHT)


def across(v):
    return lax.ppermute(v, "tensor", ACROSS)


def opposite(v):
    return lax.ppermute(v, "tensor", OPPOSITE)


def pair_gather_first(own):
    return {
        (0, 0): own,
        (0, 2): opposite(own),
        (0, 1): left(own),
        (0, -1): right(own),
        (1, 0): across(own),
    }


def pair_gather_second(got):
    new = {(1, 1): left(got[1, 0]), (1, -1): right(got[1, 0]), (1, 2): across(got[0, 2])}
    return {**got, **new}


def gather_first(own):
    return {(0, 0): own, (0, 1): left(own), (0, -1): right(own), (1, 0): across(own)}


def gather_second(got):
    new = {(0, 2): right(got[0, -1]), (1, 1): left(got[1, 0]), (1, -1): across(got[0, -1])}
    return {**got, **new}


def gather_third(got):
    half = got[0, 0].shape[0] // 2
    return {**got, (1, 2): [right(got[1, -1][:half]), left(got[1, 1][half:])]}


def listed(got, order):
    blocks = []
    for rel in order:
        blocks += got[rel] if rel == (1, 2) else [got[rel]]
    return blocks


def fence(*values):
    return lax.optimization_barrier(values)


def plus(*terms):
    total = terms[0].astype(jnp.float32)
    for term in terms[1:]:
        total = total + term.astype(jnp.float32)
    return total.astype(terms[0].dtype)


def pair_scatter_first(part):
    return left(part[1, -1]), right(part[1, 1]), across(part[1, 2])


def pair_scatter_second(sums, part):
    from_right, from_left, from_across = sums
    return (
        across(plus(part[1, 0], from_right, from_left)),
        opposite(plus(part[0, 2], from_across)),
    )


def scatter_total(part, ends):
    return sum(
        (end.astype(jnp.float32) for end in jax.tree.leaves(ends)), part[0, 0].astype(jnp.float32)
    )


def dp_order():
    index = lax.axis_index("dp")
    h, c = (index // 2) % 2, index % 2
    return jnp.stack(
        [
            y * 4 + (h ^ high) * 2 + (c ^ core)
            for core in range(2)
            for y in range(4)
            for high in range(2)
        ]
    ).astype(jnp.int32)


def column_exchange(mine):
    blocks = mine.reshape((4, 2) + mine.shape[1:])
    return lax.all_to_all(blocks, "dp", 0, 0, axis_index_groups=COLUMNS, tiled=True)


def dp_third(terms):
    column = jnp.sum(terms.astype(jnp.float32), 0).astype(terms.dtype)
    return plus(column[0], lax.ppermute(column[1], "dp", HIGH))


def level_scatter_sum(whole):
    return lax.psum_scatter(
        whole, "dp", scatter_dimension=0, tiled=True, axis_index_groups=LEVELS
    )


def high_sum(pair):
    high = (lax.axis_index("dp") // 2) % 2
    give = lax.dynamic_index_in_dim(pair, 1 - high, 0, keepdims=False)
    keep = lax.dynamic_index_in_dim(pair, high, 0, keepdims=False)
    return plus(keep, lax.ppermute(give, "dp", HIGH))


def rope_tables(places):
    halfwidth = ROPE // 2
    frequency = jnp.exp(-jnp.log(10000.0) * (2.0 * jnp.arange(halfwidth, dtype=jnp.float32) / ROPE))
    angles = places.astype(jnp.float32)[:, None] * frequency[None, :]
    return (jnp.cos(angles), jnp.sin(angles))


def normalize(values, gain):
    factor = lax.rsqrt(jnp.mean(values * values, -1, keepdims=True) + EPSILON)
    scaled = values * factor
    return (scaled * gain, scaled, factor)


def norm_backward(grads_in, scaled, factor, gain):
    weighted = grads_in * gain
    centre = jnp.mean(weighted * scaled, -1, keepdims=True)
    return (factor * (weighted - scaled * centre), jnp.sum(grads_in * scaled, 0))


def contract_rows(first, second):
    return lax.dot_general(
        first, second, (((0,), (0,)), ((), ())), preferred_element_type=jnp.float32
    )


def contract_last(first, second):
    return lax.dot_general(
        first, second, (((1,), (1,)), ((), ())), preferred_element_type=jnp.float32
    )


def matmul(first, second):
    return jnp.dot(first, second, preferred_element_type=jnp.float32)


def widen(array, width):
    return jnp.pad(array, ((0, 0), (0, width - array.shape[1])))


CHUNK = 256


def grant(mebibytes):
    return pltpu.CompilerParams(vmem_limit_bytes=mebibytes * 2**20)


def join_refs(refs, out, width):
    at = 0
    for ref in refs:
        rows = ref.shape[0]
        out[at : at + rows, :] = ref[:, :width]
        at += rows


def split_refs(value, refs, at):
    for ref in refs:
        rows = ref.shape[0]
        ref[...] = value[at : at + rows].astype(ref.dtype)
        at += rows


def swap_halves(value):
    lanes = value.shape[1]
    lane = lax.broadcasted_iota(jnp.int32, value.shape, 1) % ROPE
    return jnp.where(
        lane < ROPE // 2, pltpu.roll(value, lanes - ROPE // 2, 1), pltpu.roll(value, ROPE // 2, 1)
    )


def loads(pairs, sems):
    copies = [
        pltpu.make_async_copy(source, target, sems.at[at]) for at, (source, target) in enumerate(pairs)
    ]
    for copy in copies:
        copy.start()
    return copies


def attention_kernel(heads, rank, place, *refs):
    blocks, refs = refs[:8], refs[8:]
    gain, latent_gain, cosine, sine, query_far, down_far, up_far, out_far = refs[:8]
    logsums, factors = refs[8:10]
    far_outs, refs = refs[10:25], refs[25:]
    query_w, down_t, up_w, out_w = refs[:4]
    normed, queries, keys, values, scaled, compressed, attended, branch = refs[4:12]
    latent, raw, pair, turned, load_sems, store_sems = refs[12:]
    normed_far, queries_far, keys_far, values_far, scaled_far, compressed_far, attended_far = far_outs[:7]
    f32, bf16 = jnp.float32, jnp.bfloat16
    seq_len, width = normed.shape
    rows = seq_len // 8
    half = seq_len // 2
    scale = (NOPE + ROPE) ** (-0.5)

    weights = loads(
        [(down_far, down_t), (query_far, query_w), (up_far, up_w), (out_far, out_w)], load_sems
    )
    stores = []

    def store(source, target):
        copy = pltpu.make_async_copy(source, target, store_sems.at[len(stores)])
        copy.start()
        stores.append(copy)

    def slot_rows(slot):
        return pl.ds(pl.multiple_of(place[slot] * rows, rows), rows)

    join_refs(blocks, normed, width)

    def norm_rows(step, carry):
        at = pl.ds(pl.multiple_of(step * rows, rows), rows)
        value = normed[at, :].astype(f32)
        factor = lax.rsqrt(jnp.mean(value * value, 1, keepdims=True) + EPSILON)
        normed[at, :] = (value * factor * gain[...]).astype(bf16)
        return carry

    lax.fori_loop(0, 8, norm_rows, 0)
    store(normed, normed_far)
    weights[0].wait()
    latent[:, : rank + ROPE] = contract_last(normed[...], down_t[...])
    weights[1].wait()
    raw[...] = matmul(normed[...], query_w[...])

    def project_rows(step, carry):
        at = pl.ds(pl.multiple_of(step * rows, rows), rows)
        own = slot_rows(step)
        cos, sin = cosine[own, :], sine[own, :]
        value = latent[at, :rank]
        factor = lax.rsqrt(jnp.mean(value * value, 1, keepdims=True) + EPSILON)
        factors[at, :] = factor
        scaled[at, :] = value * factor
        compressed[at, :] = (value * factor * latent_gain[...]).astype(bf16)
        left_half = lax.broadcasted_iota(jnp.int32, (rows, NOPE), 1) < ROPE
        key_rope = latent[at, rank:]
        key_rope = jnp.where(left_half, key_rope, pltpu.roll(key_rope, ROPE, 1))
        key_rope = (key_rope * cos + swap_halves(key_rope) * sin).astype(bf16)
        one, two = raw[at, NOPE : 2 * NOPE], raw[at, 2 * NOPE :]
        plain = raw[at, :NOPE], jnp.where(left_half, pltpu.roll(one, ROPE, 1), pltpu.roll(two, ROPE, 1))
        query_rope = jnp.where(left_half, one, two)
        query_rope = query_rope * cos + swap_halves(query_rope) * sin
        for head in range(heads):
            queries[head, own, :NOPE] = plain[head].astype(bf16)
            queries[head, own, NOPE:] = jnp.where(left_half == (head == 0), query_rope, 0.0).astype(bf16)
            keys[head, own, NOPE:] = key_rope
        return carry

    lax.fori_loop(0, 8, project_rows, 0)
    store(scaled, scaled_far)
    store(compressed, compressed_far)
    store(queries, queries_far)
    weights[2].wait()
    raw_wide = (NOPE + VDIM) * heads
    pair[:, :raw_wide] = matmul(compressed[:half], up_w[...])
    pair[:, raw_wide : 2 * raw_wide] = matmul(compressed[half:], up_w[...])
    for slot in range(8):
        own = slot_rows(slot)
        at = slice(slot % 4 * rows, (slot % 4 + 1) * rows)
        for head in range(heads):
            start = slot // 4 * raw_wide + head * (NOPE + VDIM)
            keys[head, own, :NOPE] = pair[at, start : start + NOPE].astype(bf16)
            values[head, own, :] = pair[at, start + NOPE : start + NOPE + VDIM].astype(bf16)
    store(keys, keys_far)
    store(values, values_far)

    for step in range(4):
        at = slice(step * 2 * rows, (step + 1) * 2 * rows)
        stop = (step + 1) * 2 * rows
        row = lax.broadcasted_iota(jnp.int32, (2 * rows, stop), 0) + step * 2 * rows
        allowed = lax.broadcasted_iota(jnp.int32, (2 * rows, stop), 1) <= row
        for head in range(heads):
            scores = contract_last(queries[head, at, :], keys[head, :stop, :]) * scale
            scores = jnp.where(allowed, scores, -1e30)
            highest = jnp.max(scores, 1, keepdims=True)
            weight = jnp.exp(scores - highest)
            denominator = jnp.sum(weight, 1, keepdims=True)
            logsums[head, at, :] = highest + jnp.log(denominator)
            shares = (weight * (1.0 / denominator)).astype(bf16)
            turned[at, head * VDIM : (head + 1) * VDIM] = matmul(shares, values[head, :stop, :]).astype(bf16)
    for slot in range(8):
        attended[slot * rows : (slot + 1) * rows, :] = turned[slot_rows(slot), :]
    store(attended, attended_far)
    weights[3].wait()
    for order in (1, 0):
        at = slice(order * half, (order + 1) * half)
        branch[at, :] = contract_last(attended[at, :], out_w[...]).astype(bf16)
        for slot in range(4 * order, 4 * order + 4):
            store(branch.at[slot * rows : (slot + 1) * rows, :], far_outs[7 + slot])
    for copy in stores:
        copy.wait()


def attention(place, blocks, gain, query_w, down_t, latent_gain, up_w, out_w, cosine, sine):
    rows = blocks[0].shape[0]
    seq_len, width = rows * 8, blocks[0].shape[1]
    rank = up_w.shape[0]
    heads = up_w.shape[1] // (NOPE + VDIM)
    f32, bf16 = jnp.float32, jnp.bfloat16
    shape = jax.ShapeDtypeStruct
    vmem, far = pl.BlockSpec(memory_space=pltpu.VMEM), pl.BlockSpec(memory_space=pl.ANY)
    kept = [
        shape((seq_len, width), bf16),
        shape((heads, seq_len, 2 * NOPE), bf16),
        shape((heads, seq_len, 2 * NOPE), bf16),
        shape((heads, seq_len, VDIM), bf16),
        shape((seq_len, rank), f32),
        shape((seq_len, rank), bf16),
        shape((seq_len, heads * VDIM), bf16),
    ]
    weights = [query_w, down_t, up_w, out_w]
    return pl.pallas_call(
        functools.partial(attention_kernel, heads, rank),
        in_specs=[pl.BlockSpec(memory_space=pltpu.SMEM)] + [vmem] * 12 + [far] * 4,
        out_specs=[vmem] * 2 + [far] * 15,
        out_shape=[shape((heads, seq_len, 1), f32), shape((seq_len, 1), f32)]
        + kept
        + [shape((rows, width), bf16)] * 8,
        scratch_shapes=[pltpu.VMEM(a.shape, a.dtype) for a in weights + kept]
        + [
            pltpu.VMEM((seq_len, width), bf16),
            pltpu.VMEM((seq_len, rank + NOPE), f32),
            pltpu.VMEM((seq_len, query_w.shape[1]), f32),
            pltpu.VMEM((seq_len // 2, 2 * heads * (NOPE + VDIM)), f32),
            pltpu.VMEM((seq_len, heads * VDIM), bf16),
            pltpu.SemaphoreType.DMA((4,)),
            pltpu.SemaphoreType.DMA((15,)),
        ],
        compiler_params=grant(56),
        cost_estimate=pl.CostEstimate(
            flops=20 * seq_len * width * width // 4, bytes_accessed=30 * 2**20, transcendentals=0
        ),
        name="attention",
    )(place, *blocks, gain, latent_gain, cosine, sine, *weights)


def attention_grad_kernel(heads, place, *refs):
    blocks, refs = refs[:8], refs[8:]
    out_w, cosine, sine, logsums, queries_far, keys_far, values_far = refs[:7]
    branch_far, query_grads, kv_grads, rope_grads = refs[7:11]
    queries, keys, values, branch_grads = refs[11:15]
    out_grads, key_grads, value_grads, turned, load_sems, store_sem = refs[15:]
    f32, bf16 = jnp.float32, jnp.bfloat16
    seq_len, width = branch_grads.shape
    rows = seq_len // 8
    scale = (NOPE + ROPE) ** (-0.5)

    arrays = loads([(queries_far, queries), (keys_far, keys), (values_far, values)], load_sems)
    join_refs(blocks, branch_grads, width)
    (stored,) = loads([(branch_grads, branch_far)], store_sem)

    def slot_rows(slot):
        return pl.ds(pl.multiple_of(place[slot] * rows, rows), rows)

    grads = matmul(branch_grads[...], out_w[...]).astype(bf16)
    for slot in range(8):
        out_grads[slot_rows(slot), :] = grads[slot * rows : (slot + 1) * rows, :]
    key_grads[...] = jnp.zeros_like(key_grads)
    value_grads[...] = jnp.zeros_like(value_grads)
    for array in arrays:
        array.wait()

    left_half = lax.broadcasted_iota(jnp.int32, (2 * rows, NOPE), 1) < ROPE
    for step in range(4):
        at = slice(step * 2 * rows, (step + 1) * 2 * rows)
        stop = (step + 1) * 2 * rows
        row = lax.broadcasted_iota(jnp.int32, (2 * rows, stop), 0) + step * 2 * rows
        allowed = lax.broadcasted_iota(jnp.int32, (2 * rows, stop), 1) <= row
        plain, ropes = [], []
        for head in range(heads):
            query, key = queries[head, at, :], keys[head, :stop, :]
            out_grad = out_grads[at, head * VDIM : (head + 1) * VDIM]
            scores = contract_last(query, key) * scale
            shares = jnp.where(allowed, jnp.exp(scores - logsums[head, at, :]), 0.0)
            share_grads = contract_last(out_grad, values[head, :stop, :])
            centre = jnp.sum(shares * share_grads, 1, keepdims=True)
            score_grads = (shares * (share_grads - centre)).astype(bf16)
            value_grads[head, :stop, :] += contract_rows(shares.astype(bf16), out_grad)
            key_grads[head, :stop, :] += contract_rows(score_grads, query)
            query_grad = matmul(score_grads, key) * scale
            plain.append(query_grad[:, :NOPE])
            ropes.append(query_grad[:, NOPE:])
        rope = jnp.where(left_half, ropes[0], ropes[1])
        rope = rope * cosine[at, :] - swap_halves(rope) * sine[at, :]
        moved = pltpu.roll(plain[1], ROPE, 1)
        turned[at, :NOPE] = plain[0].astype(bf16)
        turned[at, NOPE : 2 * NOPE] = jnp.where(left_half, rope, moved).astype(bf16)
        turned[at, 2 * NOPE :] = jnp.where(left_half, moved, rope).astype(bf16)

    for slot in range(8):
        own, at = slot_rows(slot), slice(slot * rows, (slot + 1) * rows)
        query_grads[at, :] = turned[own, :]
        for head in range(heads):
            start = head * (NOPE + VDIM)
            kv_grads[at, start : start + NOPE] = (key_grads[head, own, :NOPE] * scale).astype(bf16)
            kv_grads[at, start + NOPE : start + NOPE + VDIM] = value_grads[head, own, :].astype(bf16)
        rope = sum(key_grads[head, own, NOPE:] for head in range(heads)) * scale
        rope = rope + pltpu.roll(rope, ROPE, 1)
        rope = rope * cosine[own, :] - swap_halves(rope) * sine[own, :]
        lane = lax.broadcasted_iota(jnp.int32, rope.shape, 1)
        rope_grads[at, :] = jnp.where(lane < ROPE, rope, 0.0).astype(bf16)
    stored.wait()


def attention_grad(place, blocks, out_w, cosine, sine, queries, keys, values, logsums):
    seq_len, width = queries.shape[1], blocks[0].shape[1]
    heads = queries.shape[0]
    f32, bf16 = jnp.float32, jnp.bfloat16
    shape = jax.ShapeDtypeStruct
    vmem, far = pl.BlockSpec(memory_space=pltpu.VMEM), pl.BlockSpec(memory_space=pl.ANY)
    return pl.pallas_call(
        functools.partial(attention_grad_kernel, heads),
        in_specs=[pl.BlockSpec(memory_space=pltpu.SMEM)] + [vmem] * 12 + [far] * 3,
        out_specs=[far] + [vmem] * 3,
        out_shape=[
            shape((seq_len, width), bf16),
            shape((seq_len, heads * (NOPE + ROPE)), bf16),
            shape((seq_len, heads * (NOPE + VDIM)), bf16),
            shape((seq_len, NOPE), bf16),
        ],
        scratch_shapes=[pltpu.VMEM(a.shape, a.dtype) for a in (queries, keys, values)]
        + [
            pltpu.VMEM((seq_len, width), bf16),
            pltpu.VMEM((seq_len, heads * VDIM), bf16),
            pltpu.VMEM((heads, seq_len, 2 * NOPE), f32),
            pltpu.VMEM((heads, seq_len, VDIM), f32),
            pltpu.VMEM((seq_len, heads * (NOPE + ROPE)), bf16),
            pltpu.SemaphoreType.DMA((3,)),
            pltpu.SemaphoreType.DMA((1,)),
        ],
        compiler_params=grant(56),
        cost_estimate=pl.CostEstimate(
            flops=8 * seq_len * width * width // 4, bytes_accessed=20 * 2**20, transcendentals=0
        ),
        name="attention_grad",
    )(place, *blocks, out_w, cosine, sine, logsums, queries, keys, values)


def input_kernel(rank, spare, order, *refs):
    query_grads, kv_grads, rope_grads, gain, latent_gain, up_w, factors, router, mixer_gain = refs[:9]
    query_far, down_far, normed_far, scaled_far = refs[9:13]
    mine, other = refs[13:15]
    parts_far = refs[15:23]
    query_w, down_t, normed, scaled, pair, parts, lhs, wide, input_gain, load_sems, store_sems = refs[23:]
    f32, bf16 = jnp.float32, jnp.bfloat16
    seq_len, width = normed.shape
    rows = seq_len // 8
    arrays = loads(
        [(scaled_far, scaled), (query_far, query_w), (down_far, down_t), (normed_far, normed)], load_sems
    )
    lhs[:, rank:] = rope_grads[...]
    latent_total = jnp.zeros((1, rank), f32)
    arrays[0].wait()
    half = seq_len // 2
    for step in range(2):
        at = slice(step * half, (step + 1) * half)
        back = contract_last(kv_grads[at, :], up_w[...])
        value = scaled[at, :]
        latent_total = latent_total + jnp.sum(back * value, 0, keepdims=True)
        weighted = back * latent_gain[...]
        centre = jnp.mean(weighted * value, 1, keepdims=True)
        lhs[at, :rank] = (factors[at, :] * (weighted - value * centre)).astype(bf16)

    input_gain[...] = jnp.zeros_like(input_gain)
    stores = []
    for turn in (1, 0):
        start = turn * half
        at = slice(start, start + half)
        if turn:
            arrays[1].wait()
            arrays[2].wait()
        pair[...] = contract_last(query_grads[at, :], query_w[...]) + matmul(lhs[at, : rank + ROPE], down_t[...])
        if turn:
            arrays[3].wait()
        for step in range(4):
            spot = slice(step * rows, (step + 1) * rows)
            block = pair[spot, :]
            slot = 4 * turn + step
            parts[slot] = block.astype(bf16)
            copy = pltpu.make_async_copy(parts.at[slot], parts_far[slot], store_sems.at[slot])
            copy.start()
            stores.append(copy)
            input_gain[...] += jnp.sum(
                block * normed[start + step * rows : start + (step + 1) * rows, :].astype(f32),
                0,
                keepdims=True,
            )

    wide[...] = contract_rows(lhs[...], normed[...])
    lanes = mine.shape[2]
    at = spare + router.shape[0]
    wide[spare:at, :] = router[...]
    wide[at : at + 1, :] = input_gain[...] / gain[...]
    wide[at + 1 : at + 2, :] = mixer_gain[...]
    share = rank // 16
    entry = lax.broadcasted_iota(jnp.int32, (rank, width), 0)
    lane = lax.broadcasted_iota(jnp.int32, (rank, width), 1)
    each = share // 8
    spot = entry // share * lanes + entry % share // each * (lanes // 8) + entry % each
    wide[at + 2 : at + 3, :] = matmul(latent_total, (spot == lane).astype(f32))
    for slot in range(16):
        at = pl.multiple_of(order[slot] * lanes, lanes)
        block = wide[:, pl.ds(at, lanes)].astype(bf16)
        if slot < 8:
            mine[slot] = block
        else:
            other[slot - 8] = block
    for copy in stores:
        copy.wait()


def input_grads(order, spare, query_grads, kv_grads, rope_grads, gain, query_w, down_t, latent_gain, up_w, normed, scaled, factors, router, mixer_gain):
    seq_len, width = normed.shape
    rank = up_w.shape[0]
    columns = rank + NOPE
    f32, bf16 = jnp.float32, jnp.bfloat16
    shape = jax.ShapeDtypeStruct
    vmem, far = pl.BlockSpec(memory_space=pltpu.VMEM), pl.BlockSpec(memory_space=pl.ANY)
    arrays = [query_w, down_t, normed, scaled]
    return pl.pallas_call(
        functools.partial(input_kernel, rank, spare),
        in_specs=[pl.BlockSpec(memory_space=pltpu.SMEM)] + [vmem] * 9 + [far] * 4,
        out_specs=[vmem] * 2 + [far] * 8,
        out_shape=[shape((8, columns, width // 16), bf16)] * 2 + [shape((seq_len // 8, width), bf16)] * 8,
        scratch_shapes=[pltpu.VMEM(a.shape, a.dtype) for a in arrays]
        + [
            pltpu.VMEM((seq_len // 2, width), f32),
            pltpu.VMEM((8, seq_len // 8, width), bf16),
            pltpu.VMEM((seq_len, columns), bf16),
            pltpu.VMEM((columns, width), f32),
            pltpu.VMEM((1, width), f32),
            pltpu.SemaphoreType.DMA((4,)),
            pltpu.SemaphoreType.DMA((8,)),
        ],
        compiler_params=grant(56),
        cost_estimate=pl.CostEstimate(
            flops=8 * seq_len * width * width // 4, bytes_accessed=20 * 2**20, transcendentals=0
        ),
        name="input_grads",
    )(order, query_grads, kv_grads, rope_grads, gain, latent_gain, up_w, factors, router, mixer_gain, *arrays)


def forward_kernel(blocks, steps, expert_units, fused, *refs):
    hid_far, cot_far, refs = refs[:blocks], refs[blocks : blocks + 4], refs[blocks + 4 :]
    own, router, gate_w, up_w, down_w = refs[:5]
    refs = refs[5:]
    if fused:
        (gate_rows, up_rows, router_rows), refs = refs[:3], refs[3:]
    scaled, gate_g, up_g, logit_g, hid_out, cot_out = refs[:6]
    refs = refs[6:]
    if fused:
        parts, refs = refs[:4], refs[4:]
    hid, cot, probs, gate, total, chosen, load_sems, store_sems = refs[:8]
    j = pl.program_id(0)
    width, experts = hid.shape[1], own.shape[1]

    def stores():
        return [
            pltpu.make_async_copy(hid, hid_out, store_sems.at[0]),
            pltpu.make_async_copy(cot.at[:, :width], cot_out, store_sems.at[1]),
        ]

    @pl.when(j == 0)
    def _():
        pairs = []
        for sources, target in ((hid_far, hid), (cot_far, cot)):
            at = 0
            for source in sources:
                pairs.append((source, target.at[at : at + source.shape[0], :]))
                at += source.shape[0]
        for copy in loads(pairs, load_sems):
            copy.wait()
        for copy in stores():
            copy.start()
        mask = cot[:, width : width + experts].astype(jnp.float32)
        chosen[...] = jnp.sum(mask * own[...], 1, keepdims=True)
        logits = matmul(hid[...], router[...])
        powers = jnp.exp(logits - jnp.max(logits, 1, keepdims=True))
        probs[...] = powers / jnp.sum(powers, 1, keepdims=True)
        gate[...] = jnp.sum(probs[...] * own[...], 1, keepdims=True) * chosen[...]
        total[...] = jnp.zeros_like(total)

    def chunk():
        lanes = gate_w.shape[1]
        column = j * lanes + lax.broadcasted_iota(jnp.int32, (1, lanes), 1)
        is_expert = column < expert_units
        pre_gate = matmul(hid[...], gate_w[...])
        pre_up = matmul(hid[...], up_w[...])
        back = matmul(cot[:, :width], down_w[...])
        sigmoid = 1.0 / (1.0 + jnp.exp(-pre_gate))
        act = pre_gate * sigmoid
        slope = sigmoid * (1.0 + pre_gate * (1.0 - sigmoid))
        hidden = act * pre_up
        scale = jnp.where(is_expert, gate[...], 1.0)
        scaled[...] = (hidden * scale).astype(scaled.dtype)
        total[...] += jnp.sum(jnp.where(is_expert, hidden * back, 0.0), 1, keepdims=True)
        back = back * scale
        gate_grad = (back * pre_up * slope).astype(gate_g.dtype)
        up_grad = (back * act).astype(up_g.dtype)
        gate_g[...] = gate_grad
        up_g[...] = up_grad
        if fused:
            at = pl.ds(pl.multiple_of(j * lanes, lanes), lanes)
            gate_all, up_all = refs[8:]
            gate_all[:, at] = gate_grad
            up_all[:, at] = up_grad

    if fused:
        pl.when(j < steps)(chunk)
    else:
        chunk()

    @pl.when(j == steps - 1)
    def _():
        own_prob = jnp.sum(probs[...] * own[...], 1, keepdims=True)
        logit_g[...] = (total[...] * chosen[...] * probs[...] * (own[...] - own_prob)).astype(logit_g.dtype)
        for copy in stores():
            copy.wait()

    if fused:

        @pl.when(j >= steps)
        def _():
            gate_all, up_all = refs[8:]
            grad = contract_last(gate_all[...], gate_rows[...]) + contract_last(up_all[...], up_rows[...])
            split_refs(grad + contract_last(logit_g[...], router_rows[...]), parts, 0)


def feed_forward(hid, cot, own, router, gate_w, up_w, weight_out, expert_units, fused):
    rows, width = sum(block.shape[0] for block in hid), hid[0].shape[1]
    units = gate_w.shape[1]
    steps = units // CHUNK
    experts = own.shape[1]
    bf16, f32 = jnp.bfloat16, jnp.float32
    shape = jax.ShapeDtypeStruct
    part = pl.BlockSpec((rows, CHUNK), lambda j: (0, jnp.minimum(j, steps - 1)))
    weight = pl.BlockSpec((width, CHUNK), lambda j: (0, jnp.minimum(j, steps - 1)))
    whole, far = pl.BlockSpec(memory_space=pltpu.VMEM), pl.BlockSpec(memory_space=pl.ANY)
    column = pltpu.VMEM((rows, 1), f32)
    operands = [*hid, *cot, own, router, gate_w, up_w, weight_out]
    in_specs = [far] * (len(hid) + 4) + [whole] * 2 + [weight] * 3
    out_specs = [part, part, part, whole, far, far]
    out_shape = [shape((rows, units), bf16)] * 3 + [shape((rows, experts), bf16)]
    out_shape += [shape((rows, width), bf16)] * 2
    scratch = [
        pltpu.VMEM((rows, width), bf16),
        pltpu.VMEM((rows, cot[0].shape[1]), bf16),
        pltpu.VMEM((rows, experts), f32),
        column,
        column,
        column,
        pltpu.SemaphoreType.DMA((len(hid) + 4,)),
        pltpu.SemaphoreType.DMA((2,)),
    ]
    grid = steps
    if fused:
        deep = min(512, width)
        grid += width // deep
        operands += [gate_w, up_w, router]
        in_specs += [pl.BlockSpec((deep, units), lambda j: (jnp.maximum(j - steps, 0), 0))] * 2
        in_specs += [pl.BlockSpec((deep, experts), lambda j: (jnp.maximum(j - steps, 0), 0))]
        out_specs += [pl.BlockSpec((rows // 4, deep), lambda j: (0, jnp.maximum(j - steps, 0)))] * 4
        out_shape += [shape((rows // 4, width), bf16)] * 4
        scratch += [pltpu.VMEM((rows, units), bf16)] * 2
    return pl.pallas_call(
        functools.partial(forward_kernel, len(hid), steps, expert_units, fused),
        grid=(grid,),
        in_specs=in_specs,
        out_specs=out_specs,
        out_shape=out_shape,
        scratch_shapes=scratch,
        compiler_params=grant(56),
        cost_estimate=pl.CostEstimate(
            flops=(10 if fused else 6) * rows * width * units,
            bytes_accessed=6 * width * units,
            transcendentals=rows * units,
        ),
        name="feed_forward",
    )(*operands)


def input_grad_kernel(gate_g, up_g, logit_g, gate_w, up_w, router, *outs):
    total = contract_last(gate_g[...], gate_w[...]) + contract_last(up_g[...], up_w[...])
    split_refs(total + contract_last(logit_g[...], router[...]), outs, 0)


def input_grad(gate_g, up_g, logit_g, gate_w, up_w, router):
    rows, units = gate_g.shape
    sizes = [rows // 4] * 4
    width, experts = router.shape
    part = min(512, width)
    whole = pl.BlockSpec(memory_space=pltpu.VMEM)
    return pl.pallas_call(
        input_grad_kernel,
        grid=(width // part,),
        in_specs=[
            whole,
            whole,
            whole,
            pl.BlockSpec((part, units), lambda j: (j, 0)),
            pl.BlockSpec((part, units), lambda j: (j, 0)),
            pl.BlockSpec((part, experts), lambda j: (j, 0)),
        ],
        out_specs=[pl.BlockSpec((size, part), lambda j: (0, j)) for size in sizes],
        out_shape=[jax.ShapeDtypeStruct((size, width), jnp.bfloat16) for size in sizes],
        compiler_params=grant(56),
        cost_estimate=pl.CostEstimate(
            flops=4 * rows * width * units, bytes_accessed=4 * width * units, transcendentals=0
        ),
        name="input_grad",
    )(gate_g, up_g, logit_g, gate_w, up_w, router)


def output_kernel(first, second, down_w, *outs):
    scaled = jnp.concatenate([first[...], second[...]], 0)
    split_refs(contract_last(scaled, down_w[...]), outs, 0)


def mixer_output(scaled, weight_out):
    rows, units = scaled[0].shape
    sizes = [rows // 4] * 8
    width = weight_out.shape[0]
    part = min(512, width)
    return pl.pallas_call(
        output_kernel,
        grid=(width // part,),
        in_specs=[
            pl.BlockSpec(memory_space=pltpu.VMEM),
            pl.BlockSpec(memory_space=pltpu.VMEM),
            pl.BlockSpec((part, units), lambda j: (j, 0)),
        ],
        out_specs=[pl.BlockSpec((size, part), lambda j: (0, j)) for size in sizes],
        out_shape=[jax.ShapeDtypeStruct((size, width), jnp.bfloat16) for size in sizes],
        compiler_params=grant(56),
        cost_estimate=pl.CostEstimate(
            flops=4 * rows * width * units, bytes_accessed=2 * width * units, transcendentals=0
        ),
        name="mixer_output",
    )(*scaled, weight_out)


def store_blocks(out, product, at=0):
    rows = product.shape[0]
    lanes = out.shape[2]
    for slot, block in enumerate(BLOCKS):
        out[slot, at : at + rows, :] = product[:, block * lanes : (block + 1) * lanes].astype(out.dtype)


def mixer_weight_kernel(la, lb, ra, rb, *refs):
    store_blocks(refs[-1], contract_rows(la[...], ra[...]) + contract_rows(lb[...], rb[...]))


def mixer_weights(order, parts, lhs, rhs, kept=None):
    rows, units = lhs[0].shape
    width = rhs[0].shape[1]
    steps = units // CHUNK
    part = pl.BlockSpec((rows, CHUNK), lambda j: (0, j))
    whole = pl.BlockSpec(memory_space=pltpu.VMEM)
    kept = [] if kept is None else [kept]
    return pl.pallas_call(
        mixer_weight_kernel,
        grid=(steps,),
        in_specs=[part, part, whole, whole] + [pl.BlockSpec(memory_space=pl.ANY)] * len(kept),
        out_specs=pl.BlockSpec((16, CHUNK, width // 16), lambda j: (0, j + order * steps, 0)),
        out_shape=jax.ShapeDtypeStruct((16, parts * units, width // 16), jnp.bfloat16),
        input_output_aliases={4: 0} if kept else {},
        compiler_params=grant(56),
        cost_estimate=pl.CostEstimate(
            flops=4 * rows * width * units, bytes_accessed=2 * width * units, transcendentals=0
        ),
        name="mixer_weights",
    )(*lhs, *rhs, *kept)


def head_weight_kernel(query_grads, normed, attended, branch_grads, compressed, kv_grads, out):
    store_blocks(out, contract_rows(query_grads[...], normed[...]))
    at = query_grads.shape[1]
    store_blocks(out, contract_rows(attended[...], branch_grads[...]), at)
    at += attended.shape[1]
    lanes = out.shape[2]
    product = contract_rows(compressed[...], kv_grads[...]).astype(out.dtype)
    share = product.shape[0] // 16
    for slot, block in enumerate(BLOCKS):
        for step in range(product.shape[1] // lanes):
            start = at + step * share
            out[slot, start : start + share, :] = product[
                block * share : (block + 1) * share, step * lanes : (step + 1) * lanes
            ]


def head_weights(query_grads, normed, attended, branch_grads, compressed, kv_grads):
    rows, width = normed.shape
    lanes = width // 16
    total = query_grads.shape[1] + attended.shape[1]
    total += compressed.shape[1] // 16 * kv_grads.shape[1] // lanes
    vmem = pl.BlockSpec(memory_space=pltpu.VMEM)
    return pl.pallas_call(
        head_weight_kernel,
        in_specs=[vmem] * 6,
        out_specs=vmem,
        out_shape=jax.ShapeDtypeStruct((16, total, lanes), jnp.bfloat16),
        compiler_params=grant(56),
        cost_estimate=pl.CostEstimate(
            flops=2 * rows * width * total, bytes_accessed=4 * width * rows, transcendentals=0
        ),
        name="head_weights",
    )(query_grads, normed, attended, branch_grads, compressed, kv_grads)


def latent_finish_kernel(late, rest):
    rest[...] = late[...].astype(jnp.float32).T.astype(rest.dtype)


def latent_finish(late):
    return pl.pallas_call(
        latent_finish_kernel,
        out_shape=jax.ShapeDtypeStruct(late.shape[::-1], late.dtype),
        compiler_params=grant(8),
        name="latent_finish",
    )(late)


def head_finish_kernel(query_wide, late, query, output, up):
    query[...] = late[:query_wide, :].astype(jnp.float32).T
    at = query_wide + output.shape[1]
    output[...] = late[query_wide:at, :].astype(jnp.float32).T
    lanes, share = late.shape[1], up.shape[0]
    for step in range(up.shape[1] // lanes):
        start = at + step * share
        up[:, step * lanes : (step + 1) * lanes] = late[start : start + share, :].astype(jnp.float32)


def head_finish(late, query_wide, value_wide, up_shape):
    lanes = late.shape[1]
    f32 = jnp.float32
    return pl.pallas_call(
        functools.partial(head_finish_kernel, query_wide),
        out_shape=[
            jax.ShapeDtypeStruct((lanes, query_wide), f32),
            jax.ShapeDtypeStruct((lanes, value_wide), f32),
            jax.ShapeDtypeStruct(up_shape, f32),
        ],
        compiler_params=grant(8),
        name="head_finish",
    )(late)


def mixer_finish_kernel(expert_units, shared_units, gate, other, *outs):
    units = gate.shape[0]
    for order, (totals, start) in enumerate(((gate, 0), (other, 0), (other, units))):
        expert = totals[start : start + expert_units, :].astype(jnp.float32)
        outs[order][:, 0, :] = expert.T
        start += expert_units
        outs[3 + order][...] = totals[start : start + shared_units, :].astype(jnp.float32)


def mixer_finish(gate, other, expert_units, shared_units):
    lanes = gate.shape[1]
    f32 = jnp.float32
    return pl.pallas_call(
        functools.partial(mixer_finish_kernel, expert_units, shared_units),
        out_shape=[jax.ShapeDtypeStruct((lanes, 1, expert_units), f32)] * 3
        + [jax.ShapeDtypeStruct((shared_units, lanes), f32)] * 3,
        compiler_params=grant(16),
        name="mixer_finish",
    )(gate, other)


def on_device(
    tokens,
    expert_index,
    cotangent,
    input_gain,
    query_weight,
    latent_down,
    latent_gain,
    latent_up,
    output_weight,
    mixer_gain,
    router_weight,
    shared_gate,
    shared_up,
    shared_down,
    expert_gate,
    expert_up,
    expert_down,
):
    tok_rows, width = tokens.shape
    group = lax.axis_index("tensor")
    z, x = group // 4, group % 4
    rank = latent_up.shape[0]
    heads_local = query_weight.shape[1] // (NOPE + ROPE)
    experts_all = router_weight.shape[1]
    scale = (NOPE + ROPE) ** (-0.5)
    expert_units = expert_gate.shape[2]
    shared_units = shared_gate.shape[1]
    shared_wide = -(-shared_units // 128) * 128
    units = expert_units + shared_wide
    bf16, f32 = jnp.bfloat16, jnp.float32

    first_order, second_order = ORDER[:4], ORDER[4:]
    seq_len = tok_rows * 8

    cosine, sine = rope_tables(jnp.arange(seq_len, dtype=jnp.int32))
    cosine = jnp.concatenate([cosine] * (2 * NOPE // ROPE), 1)
    sine = jnp.concatenate([-sine, sine] * (NOPE // ROPE), 1)
    chosen = (expert_index[:, :, None] == jnp.arange(experts_all, dtype=jnp.int32)).any(1)
    sent = jnp.concatenate([cotangent, widen(chosen.astype(bf16), 128)], 1)
    shared_gate, shared_up, shared_down = (
        widen(part, shared_wide) for part in (shared_gate, shared_up, shared_down)
    )
    got = pair_gather_first(tokens)
    got, cosine, sine, sent, shared_gate, shared_up, shared_down = fence(
        got, cosine, sine, sent, shared_gate, shared_up, shared_down
    )
    got = pair_gather_second(got)
    weight_out = jnp.concatenate([expert_down.reshape(width, expert_units), shared_down], 1)
    got, weight_out, sent = fence(got, weight_out, sent)

    upstream = pair_gather_first(sent)

    place = jnp.stack([(z ^ dz) * 4 + (x + dx) % 4 for dz, dx in ORDER]).astype(jnp.int32)
    outs = attention(
        place,
        [got[rel] for rel in ORDER],
        input_gain[None],
        query_weight,
        latent_down.T,
        latent_gain[None],
        latent_up,
        output_weight,
        cosine,
        sine,
    )
    logsums, latent_factor, normed_all, queries, keys, values, latent_scaled = outs[:7]
    compressed, attended = outs[7:9]
    part = dict(zip(ORDER, outs[9:]))
    part, upstream = fence(part, upstream)
    sums = pair_scatter_first(part)
    gate_w = jnp.concatenate([expert_gate.reshape(width, expert_units), shared_gate], 1)
    sums, part, gate_w, expert_up, shared_up = fence(sums, part, gate_w, expert_up, shared_up)
    ends = pair_scatter_second(sums, part), left(part[0, -1]), right(part[0, 1])
    up_w = jnp.concatenate([expert_up.reshape(width, expert_units), shared_up], 1)
    ends, up_w = fence(ends, up_w)
    branch = scatter_total(part, ends)

    middle = tokens.astype(f32) + branch
    second_normed, second_scaled, second_factor = normalize(middle, mixer_gain)
    own_expert = (jnp.arange(experts_all) == group).astype(f32)[None, :]

    def feed(got, order, fused):
        return feed_forward(
            listed(got, order),
            [upstream[rel] for rel in order],
            own_expert,
            router_weight,
            gate_w,
            up_w,
            weight_out,
            expert_units,
            fused,
        )

    got = gather_second(gather_first(second_normed.astype(bf16)))
    fed_first = feed(got, first_order, False)
    got, fed_first, upstream = fence(got, fed_first, upstream)
    got, upstream = gather_third(got), pair_gather_second(upstream)
    first_part = input_grad(*fed_first[1:4], gate_w, up_w, router_weight)
    got, upstream, first_part = fence(got, upstream, first_part)
    fed_second = feed(got, second_order, True)
    hidden_scaled, gate_grads, up_grads, logit_grads, hidden, upstream = zip(
        fed_first, fed_second[:6]
    )
    part = dict(zip(second_order, fed_second[6:]))
    sums = pair_scatter_first(part)
    gate_parts = mixer_weights(0, 1, gate_grads, hidden)
    sums, gate_parts = fence(sums, gate_parts)
    gate_totals = level_scatter_sum(gate_parts)
    part.update(zip(first_order, first_part))
    ends = pair_scatter_second(sums, part), left(part[0, -1]), right(part[0, 1])
    other_parts = mixer_weights(0, 2, up_grads, hidden)
    ends, other_parts = fence(ends, other_parts)
    mixer_back = scatter_total(part, ends)
    middle_from, grad_mixer_gain = norm_backward(
        mixer_back, second_scaled, second_factor, mixer_gain
    )
    middle_grads = cotangent.astype(f32) + middle_from
    got = pair_gather_first(middle_grads.astype(bf16))
    other_parts = mixer_weights(1, 2, hidden_scaled, upstream, other_parts)
    grad_router = sum(contract_rows(g, hid) for g, hid in zip(logit_grads, hidden))
    got, other_parts, grad_router = fence(got, other_parts, grad_router)
    other_totals = level_scatter_sum(other_parts)
    got = pair_gather_second(got)
    out_blocks = mixer_output(hidden_scaled, weight_out)
    got, out_blocks, gate_totals = fence(got, out_blocks, gate_totals)

    out = dict(zip(ORDER, out_blocks))
    out_sums, out_left = pair_scatter_first(out), left(out[0, -1])
    gate_total = high_sum(gate_totals)
    grads = attention_grad(
        place, [got[rel] for rel in ORDER], output_weight, cosine, sine, queries, keys, values, logsums
    )
    out_sums, grads, gate_total = fence(out_sums, grads, gate_total)
    branch_all, query_grads, kv_grads, rope_grads = grads
    out_ends, out_right = pair_scatter_second(out_sums, out), right(out[0, 1])
    wide = latent_down.shape[1]
    lanes = width // 16
    share = rank // 16
    grads = input_grads(
        dp_order(),
        wide,
        query_grads,
        kv_grads,
        rope_grads,
        input_gain[None],
        query_weight,
        latent_down.T,
        latent_gain[None],
        latent_up,
        normed_all,
        latent_scaled,
        latent_factor,
        grad_router,
        grad_mixer_gain[None],
    )
    head_parts = head_weights(query_grads, normed_all, attended, branch_all, compressed, kv_grads)
    out_ends, out_left, out_right, grads, head_parts = fence(
        out_ends, out_left, out_right, grads, head_parts
    )
    mine, other = grads[:2]
    part = dict(zip(ORDER, grads[2:]))

    sums = pair_scatter_first(part)
    other = lax.ppermute(other, "dp", CORE)
    sums, other, head_parts, other_totals = fence(
        sums, plus(mine, other), head_parts, other_totals
    )
    terms = column_exchange(other)
    head_totals = level_scatter_sum(head_parts)
    other_total = high_sum(other_totals)
    sums, terms = fence(sums, terms)
    late = dp_third(terms)
    ends = *pair_scatter_second(sums, part), left(part[0, -1]), right(part[0, 1])
    late, other_total = fence(late, other_total)
    normed_grads = scatter_total(part, ends)
    _, first_scaled, first_factor = normalize(tokens.astype(f32), input_gain)
    input_from, _ = norm_backward(normed_grads, first_scaled, first_factor, input_gain)
    grad_tokens = middle_grads + input_from
    rest = latent_finish(late).reshape(8, lanes // 8, -1)
    rest = lax.all_to_all(rest, "tensor", 0, 0, tiled=True)
    head_total = high_sum(head_totals)
    layer_out = (middle + scatter_total(out, (out_ends, out_left, out_right))).astype(bf16)
    rest, head_total, layer_out, grad_tokens = fence(rest, head_total, layer_out, grad_tokens)
    rest = jnp.sum(rest.astype(f32), 0)
    at = wide + experts_all
    expert_outs = mixer_finish(gate_total, other_total, expert_units, shared_units)
    total_query, total_output, total_up = head_finish(
        head_total, query_weight.shape[1], attended.shape[1], (share, latent_up.shape[1])
    )
    return (
        layer_out,
        grad_tokens,
        rest[:, at],
        total_query,
        rest[:, :wide],
        rest[: share // 8, at + 2],
        total_up,
        total_output,
        rest[:, at + 1],
        rest[:, wide:at],
        *[shared.T for shared in expert_outs[3:]],
        *expert_outs[:3],
    )


def solution(mesh):
    rows = P(("dp", "tensor"), None)
    columns = P(None, "tensor")
    middle = P(None, "tensor", None)
    return jax.shard_map(
        on_device,
        mesh=mesh,
        in_specs=(rows, rows, rows, P(), columns, P(), P(), columns, columns, P(), P())
        + (columns,) * 3
        + (middle,) * 3,
        out_specs=(
            rows,
            rows,
            P(("dp", "tensor")),
            P("dp", "tensor"),
            rows,
            P(("dp", "tensor")),
            P("dp", "tensor"),
            P("dp", "tensor"),
            P(("dp", "tensor")),
            rows,
        )
        + (P("dp", "tensor"),) * 3
        + (P("dp", "tensor", None),) * 3,
        check_vma=False,
    )
```
